32 devices in a mesh: dp: 8 (over y, x, core), tensor: 4 (over z).
Axes of the slice: x: 2, y: 2, z: 4, core: 2. Of those that a mesh axis runs over, the one named last changes fastest.
Arguments:
- tokens: bfloat16 [2, 2048, 1024], P(None, 'dp', 'tensor'), may hold values from -6 to 6
- lengths: int32 [2, 8], P(None, 'dp'), may hold values from 16 to 256, as said below
- norm_gain: float32 [1024], replicated, may hold values from 0.5 to 1.5
- in_weight: bfloat16 [1024, 2, 2048], P('dp', None, 'tensor'), may hold values from -0.1875 to 0.1875
- x_weight: bfloat16 [2048, 96], P('tensor'), may hold values from -0.125 to 0.125
- dt_weight: bfloat16 [64, 2048], P(None, 'tensor'), may hold values from -0.75 to 0.75
- dt_bias: float32 [2048], P('tensor'), may hold values from -6 to -2
- conv_weight: float32 [4, 2048], P(None, 'tensor'), may hold values from -3 to 3
- conv_bias: float32 [2048], P('tensor'), may hold values from -3 to 3
- a_log: float32 [16, 2048], P(None, 'tensor'), may hold values from 0 to 2.77
- skip: float32 [2048], P('tensor'), may hold values from 0.5 to 1.5
- out_weight: bfloat16 [2048, 1024], P('tensor', 'dp'), may hold values from -0.125 to 0.125
- cotangent: bfloat16 [2, 2048, 1024], P(None, 'dp', 'tensor'), may hold values from -6 to 6
Outputs:
- mixed: bfloat16 [2, 2048, 1024], P(None, 'dp', 'tensor')
- input_grad: float32 [2, 2048, 1024], P(None, 'dp', 'tensor')
- grad_norm_gain: float32 [1024], replicated
- grad_in_weight: float32 [1024, 2, 2048], P('dp', None, 'tensor')
- grad_x_weight: float32 [2048, 96], P('tensor')
- grad_dt_weight: float32 [64, 2048], P(None, 'tensor')
- grad_dt_bias: float32 [2048], P('tensor')
- grad_conv_weight: float32 [4, 2048], P(None, 'tensor')
- grad_conv_bias: float32 [2048], P('tensor')
- grad_a_log: float32 [16, 2048], P(None, 'tensor')
- grad_skip: float32 [2048], P('tensor')
- grad_out_weight: float32 [2048, 1024], P('tensor', 'dp')
The draws below stay inside these ranges and needn't reach their ends.
Inputs may be any that keep to these rules, and one draw needn't show every extreme that they name: lengths[m, c] is the number of valid tokens at the head of context c of micro-batch m; the rest is padding. Some context is full and some has exactly 16 valid tokens.
All inputs are finite; a program needn't handle non-finite values.
Results may differ from the reference program's by a relative error of at most 0.011.
Values may be sent and summed in bfloat16 or wider, within the bound.
No kernel may reach another device: no remote copies, remote signals or barrier semaphores. Data moves between devices by JAX's collectives and lax.ppermute only.
A program may use at most 192 MiB of HBM per device.

```python
from functools import partial
import jax
import jax.numpy as jnp
from jax import lax

D = 1024
E = 2048
N = 16
CONV = 4
R = 64
PROJ = 96
SEQ_LEN = 256
MICRO = 2
TOKENS = 2048


def draw_lengths(key, part):
    key = jax.random.fold_in(key, 7)
    key_lens, key_first, key_second = jax.random.split(key, 3)
    count = MICRO * (TOKENS // SEQ_LEN)
    lens_flat = jax.random.randint(key_lens, (count,), SEQ_LEN // 16, SEQ_LEN + 1)
    first_pos = jax.random.randint(key_first, (), 0, count)
    second_pos = (first_pos + jax.random.randint(key_second, (), 1, count)) % count
    places = jnp.arange(count)
    lens_flat = jnp.where(places == first_pos, SEQ_LEN, lens_flat)
    lens_flat = jnp.where(places == second_pos, SEQ_LEN // 16, lens_flat)
    return lens_flat.reshape(MICRO, count // MICRO).astype(jnp.int32)


def spiked(result, stream_key, source, target, parts, factor):
    def block_of(position):
        return (jnp.arange(result.shape[position]) // (result.shape[position] // parts)).reshape((-1,) + (1,) * (result.ndim - 1 - position))

    near = jax.random.permutation(stream_key, parts)[block_of(target)]
    far = (block_of(target) + parts // 2) % parts
    return jnp.where((block_of(source) == near) | (block_of(source) == far), factor * result, result)


def levels(key, shape, cuts, least, high):
    factor_of, own = 1.0, jax.random.fold_in(key, 6)
    for dim, blocks in cuts:
        heights = jnp.exp(jax.random.uniform(jax.random.fold_in(own, dim), (blocks,), jnp.float32, least / len(cuts), high / len(cuts)))
        factor_of = factor_of * jnp.repeat(heights, shape[dim] // blocks).reshape([-1 if axis == dim else 1 for axis in range(len(shape))])
    return factor_of


def noise(rng, extent, scale, bound, cuts=(), kind=jnp.bfloat16):
    result = jax.random.normal(rng, extent, jnp.float32) * scale
    if len(cuts) > 0:
        result = levels(rng, extent, cuts, -0.22, 0.18) * result
    return jnp.clip(result, min=-bound, max=bound).astype(kind)


def noise_with(stream_key, dims, width, most, cuts, heavy, kind=jnp.bfloat16):
    result = width * jax.random.normal(stream_key, dims, jnp.float32)
    if cuts:
        result = result * levels(stream_key, dims, cuts, -0.22, 0.18)
    return jnp.clip(spiked(result, jax.random.fold_in(stream_key, 3), *heavy), -most, most).astype(kind)


def setup_inputs(seed: int = 0) -> dict:
    seeds = jax.random.split(jax.random.key(seed), 14)
    return {
        "tokens": noise(seeds[0], (MICRO, TOKENS, D), 1.0, 6.0, ((1, 8), (2, 4))),
        "lengths": draw_lengths(jax.random.fold_in(seeds[13], 71), 0),
        "norm_gain": jnp.clip(1.0 + 0.1 * jax.random.normal(seeds[2], (D,), jnp.float32), 0.5, 1.5),
        "in_weight": noise(seeds[3], (D, 2, E), D ** -0.5, 0.1875, ((0, 8), (2, 4))),
        "x_weight": noise(seeds[4], (E, PROJ), E ** -0.5, 0.125, ((0, 4),)),
        "dt_weight": noise(seeds[5], (R, E), R ** -0.5, 0.75, ((1, 4),)),
        "dt_bias": jnp.clip(-6.0 + 4.0 * jax.random.uniform(seeds[6], (E,), jnp.float32) ** levels(seeds[6], (E,), ((0, 4),), -0.2, 0.2), -6.0, -2.0),
        "conv_weight": noise(seeds[7], (CONV, E), CONV ** -0.5, 3.0, ((1, 4),), jnp.float32),
        "conv_bias": noise(seeds[8], (E,), 0.5, 3.0, ((0, 4),), jnp.float32),
        "a_log": jnp.clip(2.77 * jax.random.uniform(seeds[9], (N, E), jnp.float32) ** levels(seeds[9], (N, E), ((1, 4),), -0.2, 0.2), 0.0, 2.77),
        "skip": jnp.clip(0.5 + 1.0 * jax.random.uniform(seeds[10], (E,), jnp.float32) ** levels(seeds[10], (E,), ((0, 4),), -0.2, 0.2), 0.5, 1.5),
        "out_weight": noise(seeds[11], (E, D), E ** -0.5, 0.125, ((0, 4), (1, 8))),
        "cotangent": noise_with(seeds[12], (MICRO, TOKENS, D), 1.0, 6.0, ((1, 8), (2, 4)), (1, 2, 8, 2.0)),
    }


@jax.custom_vjp
def low(v):
    return lax.optimization_barrier(v.astype(jnp.bfloat16)).astype(jnp.float32)

@jax.custom_vjp
def low_back(v):
    return v

def low_keep(v):
    return (low(v), None)

def low_pass(kept, grad):
    return (grad,)

def back_keep(v):
    return (v, None)

def back_low(kept, grad):
    return (low(grad),)
low.defvjp(low_keep, low_pass)
low_back.defvjp(back_keep, back_low)
EPS = 1e-05
HIGH = lax.Precision.HIGHEST

def combine_pair(earlier, latter):
    return (earlier[0] * latter[0], latter[0] * earlier[1] + latter[1])

def scan_block(carry_state, block_in, neg_rate):
    step_dt, b_in, c_in, u_in = block_in
    decays = jnp.exp(step_dt[:, None, :] * neg_rate[None, :, :])
    drives = (step_dt * u_in)[:, None, :] * b_in[:, :, None]
    dec_run, drv_run = lax.associative_scan(combine_pair, (decays, drives), axis=0)
    states = dec_run * carry_state[None] + drv_run
    y_out = lax.optimization_barrier(jnp.sum(c_in[:, :, None] * states, axis=1))
    return (states[-1], y_out)

def run_scan(step_dt, b_in, c_in, u_in, neg_rate):
    length = step_dt.shape[0]
    block_len = min(128, length)
    blocks = length // block_len

    def shape_blocks(values):
        return values.reshape((blocks, block_len) + values.shape[1:])
    inputs = (shape_blocks(step_dt), shape_blocks(b_in), shape_blocks(c_in), shape_blocks(u_in))
    start_state = jnp.zeros((b_in.shape[1], step_dt.shape[1]), jnp.float32)
    stepper = jax.checkpoint(partial(scan_block, neg_rate=neg_rate))
    carry_out, y_blocks = lax.scan(stepper, start_state, inputs)
    return y_blocks.reshape(step_dt.shape)

def conv_silu(inner_in, conv_weight, conv_bias):
    kernel_len = conv_weight.shape[0]
    padded = jnp.pad(inner_in, ((kernel_len - 1, 0), (0, 0)))
    summed = jnp.zeros_like(inner_in) + conv_bias[None, :]
    for offset in range(kernel_len):
        summed = summed + conv_weight[offset][None, :] * padded[offset:offset + inner_in.shape[0]]
    return jax.nn.silu(summed)

def context_forward(x_rows, live_rows, params):
    norm_gain, in_weight, x_weight, dt_weight, dt_bias, conv_weight, conv_bias, a_log, skip, out_weight = params
    mean_sq = lax.optimization_barrier(jnp.mean(x_rows * x_rows, axis=1, keepdims=True))
    normed = low(x_rows * lax.rsqrt(mean_sq + EPS) * norm_gain[None, :])
    both_parts = low_back(jnp.einsum('td,dke->tke', normed, in_weight, precision=HIGH))
    inner_in = both_parts[:, 0]
    gate_in = both_parts[:, 1]
    u_act = conv_silu(inner_in, conv_weight, conv_bias)
    u_low = low(u_act)
    projected = low_back(jnp.dot(u_low, x_weight, precision=HIGH))
    dt_rank = dt_weight.shape[0]
    nstate = a_log.shape[0]
    dt_low = low(projected[:, :dt_rank])
    b_in = projected[:, dt_rank:dt_rank + nstate]
    c_in = projected[:, dt_rank + nstate:]
    dt_lin = low_back(jnp.dot(dt_low, dt_weight, precision=HIGH))
    step_dt = jax.nn.softplus(dt_lin + dt_bias[None, :])
    scanned = run_scan(step_dt, b_in, c_in, u_act, -jnp.exp(a_log))
    y_rows = scanned + skip[None, :] * u_act
    gated = low(y_rows * jax.nn.silu(gate_in) * live_rows[:, None])
    return x_rows + jnp.dot(gated, out_weight, precision=HIGH)

def reference(tokens, lengths, norm_gain, in_weight, x_weight, dt_weight, dt_bias, conv_weight, conv_bias, a_log, skip, out_weight, cotangent):
    contexts = tokens.astype(jnp.float32).reshape(MICRO * (TOKENS // SEQ_LEN), SEQ_LEN, D)
    positions = jnp.arange(SEQ_LEN, dtype=jnp.int32)
    live_all = (positions[None, :] < lengths.reshape(-1, 1).astype(jnp.int32)).astype(jnp.float32)
    params = tuple((weight.astype(jnp.float32) for weight in (norm_gain, in_weight, x_weight, dt_weight, dt_bias, conv_weight, conv_bias, a_log, skip, out_weight)))

    def forward(ctx_all, weights):

        def one_context(paired):
            return context_forward(paired[0], paired[1], weights)
        return lax.map(jax.checkpoint(one_context), (ctx_all, live_all))
    outputs, pull_back = jax.vjp(forward, contexts, params)
    d_ctx, d_params = pull_back(cotangent.astype(jnp.float32).reshape(contexts.shape))
    mixed = outputs.reshape(MICRO, TOKENS, D).astype(jnp.bfloat16)
    input_grad = d_ctx.reshape(MICRO, TOKENS, D)
    return (mixed, input_grad, d_params[0], d_params[1], d_params[2], d_params[3], d_params[4], d_params[5], d_params[6], d_params[7], d_params[8], d_params[9])
```

```python
import math
from functools import partial

import jax
import jax.numpy as jnp
from jax import lax
from jax.experimental import pallas as pl
from jax.experimental.pallas import tpu as pltpu
from jax.sharding import PartitionSpec as P

EPS = 1e-05
LOG2E = math.log2(math.e)
F32 = jnp.float32
BF16 = jnp.bfloat16
GROUP = 8
LANES = 128


def contract(left, right, left_dim, right_dim):
    return lax.dot_general(
        left, right, (((left_dim,), (right_dim,)), ((), ())), preferred_element_type=F32
    )


def sigmoid(v):
    return 1.0 / (1.0 + jnp.exp(-v))


def softplus(v):
    return jnp.maximum(v, 0.0) + jnp.log1p(jnp.exp(-jnp.abs(v)))


def swap(value, axis, mask):
    count = lax.axis_size(axis)
    return lax.ppermute(value, axis, [(i, i ^ mask) for i in range(count)])


def pre_kernel(parts, blocks, ids, *refs):
    xs, refs = refs[:parts], refs[parts:]
    ws, refs = refs[:blocks], refs[blocks:]
    gain, conv_w, conv_b, xw_t = refs[:4]
    normed, w_full, inner, summed, u_act, gate, inv, proj, proj_low, padded = refs[4:]
    quarter = xs[0].shape[2]
    chans = inner.shape[2]

    @pl.when(pl.program_id(0) == 0)
    def _():
        gather_rows(ids, ws, w_full)
        padded[:GROUP, :] = jnp.zeros((GROUP, chans), F32)

    square = 0.0
    for x in xs:
        rows = x[0].astype(F32)
        square = square + jnp.sum(rows * rows, axis=1, keepdims=True)
    scale = lax.rsqrt(square / (parts * quarter) + EPS)
    inv[0] = jnp.broadcast_to(scale, inv.shape[1:])
    for k, x in enumerate(xs):
        cols = pl.ds(pl.multiple_of((ids[0] ^ k) * quarter, LANES), quarter)
        normed[0, :, cols] = (x[0].astype(F32) * scale * gain[:, cols]).astype(BF16)
    both = jnp.dot(normed[0], w_full[...], preferred_element_type=F32)
    gate[0] = both[:, chans:]
    inner_in = both[:, :chans]
    inner[0] = inner_in
    tokens = inner_in.shape[0]
    padded[GROUP:, :] = inner_in
    taps = conv_w.shape[0]
    total = jnp.broadcast_to(conv_b[...], inner_in.shape)
    for j in range(taps):
        total = total + conv_w[j : j + 1, :] * padded[pl.ds(GROUP - taps + 1 + j, tokens), :]
    summed[0] = total
    act = total * sigmoid(total)
    u_act[0] = act
    partial_sum = contract(xw_t[...], act.astype(BF16), 1, 1)
    proj[0] = partial_sum
    proj_low[0] = partial_sum.astype(BF16)


def gather_rows(ids, blocks, full):
    if len(blocks) == 1:
        full[...] = blocks[0][...]
        return
    chips = len(blocks) // 2
    for side in range(2):
        for j in range(chips):
            block = blocks[side * chips + j]
            index = (ids[1] ^ (2 * j)) ^ side
            rows = block.shape[0]
            full[pl.ds(pl.multiple_of(index * rows, 16), rows), :] = block[...]


def gather_cols(ids, blocks, full):
    if len(blocks) == 1:
        full[...] = blocks[0][...]
        return
    chips = len(blocks) // 2
    for side in range(2):
        for j in range(chips):
            block = blocks[side * chips + j]
            index = (ids[1] ^ (2 * j)) ^ side
            cols = block.shape[1]
            full[:, pl.ds(pl.multiple_of(index * cols, LANES), cols)] = block[...]


def fold(pend, out, start):
    for g in range(pend.shape[0]):
        total = pend[g, pl.ds(0, GROUP, stride=GROUP), :]
        for s in range(1, GROUP):
            total = total + pend[g, pl.ds(s, GROUP, stride=GROUP), :]
        out[pl.ds(start, GROUP), g * LANES : (g + 1) * LANES] = total


def fwd_kernel(parts, blocks, ids, lens, *refs):
    projs, refs = refs[:parts], refs[parts:]
    ws, refs = refs[:blocks], refs[blocks:]
    u_act, gate, dt_w, dt_b, a_log, skip = refs[:6]
    refs = refs[6:]
    dt_lin, y_rows, gated, states, w_full, own = refs[:6]
    sends, refs = refs[6 : 5 + parts], refs[5 + parts :]
    dt, dtu, y, pend, carry = refs
    span, chans = dt.shape
    nstate = a_log.shape[0]
    rank = dt_w.shape[0]
    block = pl.program_id(1)
    groups = chans // LANES

    @pl.when((pl.program_id(0) == 0) & (block == 0))
    def _():
        gather_cols(ids, ws, w_full)

    @pl.when(block == 0)
    def _():
        carry[...] = jnp.zeros(carry.shape, F32)

    proj = projs[0][0]
    for other in projs[1:]:
        proj = proj + other[0].astype(F32)
    lin = contract(proj[:rank].astype(BF16), dt_w[...], 0, 0) + dt_b[...]
    dt_lin[0] = lin
    step = softplus(lin)
    dt[...] = step
    dtu[...] = step * u_act[0]
    b_in = proj[rank : rank + nstate]
    c_in = proj[rank + nstate :]
    rate = -LOG2E * jnp.exp(a_log[...])
    lane = [slice(g * LANES, (g + 1) * LANES) for g in range(groups)]

    def steps(i, state):
        state = list(state)
        start = pl.multiple_of(i * GROUP, GROUP)
        shift = lax.rem(span - start, span)
        b_roll = pltpu.roll(b_in, shift, 1)
        c_roll = pltpu.roll(c_in, shift, 1)
        dt_rows = dt[pl.ds(start, GROUP), :]
        dtu_rows = dtu[pl.ds(start, GROUP), :]
        for k in range(GROUP):
            b_t = jnp.broadcast_to(b_roll[:, k : k + 1], (nstate, LANES))
            c_t = jnp.broadcast_to(c_roll[:, k : k + 1], (nstate, LANES))
            for g in range(groups):
                dt_t = dt_rows[k : k + 1, lane[g]]
                dtu_t = dtu_rows[k : k + 1, lane[g]]
                new = jnp.exp2(dt_t * rate[:, lane[g]]) * state[g] + dtu_t * b_t
                state[g] = new
                states[0, pl.ds(pl.multiple_of((start + k) * nstate, nstate), nstate), lane[g]] = new
                term = c_t * new
                pend[g, k * GROUP : (k + 1) * GROUP, :] = sum(
                    term[s : s + GROUP] for s in range(0, nstate, GROUP)
                )
        fold(pend, y, start)
        return tuple(state)

    last = lax.fori_loop(0, span // GROUP, steps, tuple(carry[:, l] for l in lane))
    for g in range(groups):
        carry[:, lane[g]] = last[g]
    rows = y[...] + skip[...] * u_act[0]
    y_rows[0] = rows
    gate_in = gate[0]
    position = block * span + lax.broadcasted_iota(jnp.int32, (span, 1), 0)
    live = (position < lens[pl.program_id(0)]).astype(F32)
    low = (rows * (gate_in * sigmoid(gate_in)) * live).astype(BF16)
    gated[0] = low
    quarter = own.shape[2]
    for k in range(parts):
        cols = pl.ds(pl.multiple_of((ids[0] ^ k) * quarter, LANES), quarter)
        term = jnp.dot(low, w_full[:, cols], preferred_element_type=F32)
        if k == 0:
            own[0] = term
        else:
            sends[k - 1][0] = term.astype(BF16)


def bwd_kernel(parts, ids, lens, *refs):
    projs, refs = refs[:parts], refs[parts:]
    cots, refs = refs[:parts], refs[parts:]
    w_full, u_act, gate, dt_lin, y_rows, states, dt_w, a_log, skip = refs[:9]
    refs = refs[9:]
    cot_full, d_proj, d_proj_low, d_scan, d_gate, small = refs[:6]
    dt, dtu, d_y, d_dtu, d_dta, pend_q, pend_r, carry, g_rate = refs[6:]
    span, chans = dt.shape
    nstate = a_log.shape[0]
    rank = dt_w.shape[0]
    first = (pl.program_id(0) == 0) & (pl.program_id(1) == 0)
    last = (pl.program_id(0) == pl.num_programs(0) - 1) & (pl.program_id(1) == pl.num_programs(1) - 1)
    block = pl.num_programs(1) - 1 - pl.program_id(1)
    groups = chans // LANES
    quarter = cots[0].shape[2]
    lane = [slice(g * LANES, (g + 1) * LANES) for g in range(groups)]

    @pl.when(first)
    def _():
        small[...] = jnp.zeros(small.shape, F32)
        g_rate[...] = jnp.zeros(g_rate.shape, F32)

    @pl.when(pl.program_id(1) == 0)
    def _():
        carry[...] = jnp.zeros(carry.shape, F32)

    for k, cot in enumerate(cots):
        cols = pl.ds(pl.multiple_of((ids[0] ^ k) * quarter, LANES), quarter)
        cot_full[0, :, cols] = cot[0]
    d_gated = contract(cot_full[0], w_full[...], 1, 1)

    proj = projs[0][0]
    for other in projs[1:]:
        proj = proj + other[0].astype(F32)
    dt_low = proj[:rank].astype(BF16)
    b_in = proj[rank : rank + nstate]
    c_in = proj[rank + nstate :]
    lin = dt_lin[0]
    u = u_act[0]
    step = softplus(lin)
    dt[...] = step
    dtu[...] = step * u
    gate_in = gate[0]
    gate_sig = sigmoid(gate_in)
    position = block * span + lax.broadcasted_iota(jnp.int32, (span, 1), 0)
    live = (position < lens[pl.program_id(0)]).astype(F32)
    d_live = d_gated * live
    d_rows = d_live * (gate_in * gate_sig)
    d_y[...] = d_rows
    d_gate[0] = (d_live * y_rows[0] * (gate_sig * (1.0 + gate_in * (1.0 - gate_sig)))).astype(BF16)
    rate = -jnp.exp(a_log[...])
    rate2 = LOG2E * rate
    lanes = lax.broadcasted_iota(jnp.int32, (nstate, span), 1)
    count = span // GROUP

    def steps(i, loop):
        run, acc, d_b, d_c = list(loop[0]), list(loop[1]), loop[2], loop[3]
        start = pl.multiple_of((count - 1 - i) * GROUP, GROUP)
        shift = lax.rem(span - start, span)
        b_roll = pltpu.roll(b_in, shift, 1)
        c_roll = pltpu.roll(c_in, shift, 1)
        dt_rows = dt[pl.ds(start, GROUP), :]
        dtu_rows = dtu[pl.ds(start, GROUP), :]
        dy_rows = d_y[pl.ds(start, GROUP), :]
        for k in reversed(range(GROUP)):
            b_t = jnp.broadcast_to(b_roll[:, k : k + 1], (nstate, LANES))
            c_t = jnp.broadcast_to(c_roll[:, k : k + 1], (nstate, LANES))
            sum_b = 0.0
            sum_c = 0.0
            for g in range(groups):
                dt_t = dt_rows[k : k + 1, lane[g]]
                dtu_t = dtu_rows[k : k + 1, lane[g]]
                dy_t = dy_rows[k : k + 1, lane[g]]
                state = states[0, pl.ds(pl.multiple_of((start + k) * nstate, nstate), nstate), lane[g]]
                d_state = run[g] + c_t * dy_t
                kept = state - dtu_t * b_t
                d_exp = d_state * kept
                acc[g] = acc[g] + d_exp * dt_t
                run[g] = jnp.exp2(dt_t * rate2[:, lane[g]]) * d_state
                term_q = d_exp * rate[:, lane[g]]
                term_r = d_state * b_t
                rows = slice(k * GROUP, (k + 1) * GROUP)
                pend_q[g, rows, :] = sum(term_q[s : s + GROUP] for s in range(0, nstate, GROUP))
                pend_r[g, rows, :] = sum(term_r[s : s + GROUP] for s in range(0, nstate, GROUP))
                sum_b = sum_b + d_state * dtu_t
                sum_c = sum_c + state * dy_t
            here = lanes == start + k
            d_b = jnp.where(here, jnp.sum(sum_b, axis=1, keepdims=True), d_b)
            d_c = jnp.where(here, jnp.sum(sum_c, axis=1, keepdims=True), d_c)
        fold(pend_q, d_dta, start)
        fold(pend_r, d_dtu, start)
        return tuple(run), tuple(acc), d_b, d_c

    empty = jnp.zeros((nstate, span), F32)
    run, acc, d_b, d_c = lax.fori_loop(
        0,
        count,
        steps,
        (tuple(carry[:, l] for l in lane), tuple(g_rate[:, l] for l in lane), empty, empty),
    )
    for g in range(groups):
        carry[:, lane[g]] = run[g]
        g_rate[:, lane[g]] = acc[g]
    d_lin = (d_dtu[...] * u + d_dta[...]) * sigmoid(lin)
    d_scan[0] = d_dtu[...] * step + d_rows * skip[...]
    d_low = d_lin.astype(BF16)
    full = jnp.concatenate([contract(dt_w[...], d_low, 1, 1), d_b, d_c], axis=0)
    d_proj[0] = full
    d_proj_low[0] = full.astype(BF16)
    small[:rank, :] += jnp.dot(dt_low, d_low, preferred_element_type=F32)
    row = rank + nstate
    small[row : row + 1, :] += jnp.sum(d_lin, axis=0, keepdims=True)
    small[row + 1 : row + 2, :] += jnp.sum(d_rows * u, axis=0, keepdims=True)

    @pl.when(last)
    def _():
        small[rank : rank + nstate, :] = g_rate[...] * rate


def post_kernel(parts, ids, *refs):
    projs, refs = refs[:parts], refs[parts:]
    xs, refs = refs[:parts], refs[parts:]
    d_scan, d_gate, u_act, summed, inner, inv, w_full, gain, xw_t, conv_w = refs[:10]
    refs = refs[10:]
    d_both, small, tiny, own = refs[:4]
    sends, refs = refs[4 : 3 + parts], refs[3 + parts :]
    padded, front = refs
    tokens, chans = d_scan.shape[1:]
    quarter = own.shape[2]
    taps = conv_w.shape[0]
    m = pl.program_id(0)

    @pl.when(m == 0)
    def _():
        padded[tokens:, :] = jnp.zeros((GROUP, chans), F32)
        front[:GROUP, :] = jnp.zeros((GROUP, chans), F32)
        small[...] = jnp.zeros(small.shape, F32)
        tiny[...] = jnp.zeros(tiny.shape, F32)

    proj = projs[0][0]
    for other in projs[1:]:
        proj = proj + other[0].astype(F32)
    d_proj = proj.astype(BF16)
    count = d_proj.shape[0]
    d_u = d_scan[0] + contract(d_proj, xw_t[...], 0, 0)
    small[:count, :] += jnp.dot(d_proj, u_act[0].astype(BF16), preferred_element_type=F32)
    conv = summed[0]
    sig = sigmoid(conv)
    d_conv = d_u * (sig * (1.0 + conv * (1.0 - sig)))
    padded[:tokens, :] = d_conv
    front[GROUP:, :] = inner[0]
    d_inner = 0.0
    for j in range(taps):
        d_inner = d_inner + conv_w[j : j + 1, :] * padded[pl.ds(taps - 1 - j, tokens), :]
        small[count + j : count + j + 1, :] += jnp.sum(
            d_conv * front[pl.ds(GROUP - taps + 1 + j, tokens), :], axis=0, keepdims=True
        )
    small[count + taps : count + taps + 1, :] += jnp.sum(d_conv, axis=0, keepdims=True)
    d_both[0, :, :chans] = d_inner.astype(BF16)
    d_both[0, :, chans:] = d_gate[0]
    scale = inv[0][:, :1]
    ones = jnp.ones((GROUP, quarter), F32)
    dots = 0.0
    for k in range(parts):
        cols = pl.ds(pl.multiple_of((ids[0] ^ k) * quarter, LANES), quarter)
        d_norm = contract(d_both[0], w_full[cols, :], 1, 1)
        if k == 0:
            own[0] = d_norm
        else:
            sends[k - 1][0] = d_norm.astype(BF16)
        along = d_norm * xs[k][0].astype(F32)
        tiny[0:1, cols] += jnp.sum(along * scale, axis=0, keepdims=True)
        dots = dots + lax.dot_general(
            ones,
            along * gain[:, cols],
            (((1,), (1,)), ((), ())),
            precision=lax.Precision.HIGHEST,
            preferred_element_type=F32,
        )
    tiny[1:2, pl.ds(pl.multiple_of(m * tokens, LANES), tokens)] = dots[:1]


def grad_in_kernel(chips, ids, normed, d_both, mine, theirs):
    if chips == 0:
        mine[...] = contract(normed[...], d_both[...], 0, 0)
        return
    rows = mine.shape[1]
    for side, out in enumerate((theirs, mine)):
        for j in range(chips):
            index = (ids[1] ^ (2 * j)) ^ (1 - side)
            cols = pl.ds(pl.multiple_of(index * rows, LANES), rows)
            out[j] = contract(normed[:, cols], d_both[...], 0, 0).astype(out.dtype)


def grad_out_kernel(chips, ids, gated, cot, mine, theirs):
    if chips == 0:
        mine[...] = contract(gated[...], cot[...], 0, 0)
        return
    width = mine.shape[2]
    for side, out in enumerate((theirs, mine)):
        for j in range(chips):
            index = (ids[1] ^ (2 * j)) ^ (1 - side)
            cols = pl.ds(pl.multiple_of(index * width, LANES), width)
            out[j] = contract(gated[...], cot[:, cols], 0, 0).astype(out.dtype)


def whole(shape):
    return pl.BlockSpec(shape, lambda *_: (0,) * len(shape))


SMEM = pl.BlockSpec(memory_space=pltpu.SMEM)


def params(grid, mib=56):
    return pltpu.CompilerParams(
        dimension_semantics=("arbitrary",) * grid, vmem_limit_bytes=mib * 1024 * 1024
    )


def struct(shape, dtype):
    return jax.ShapeDtypeStruct(shape, dtype)


def run_pre(ids, xs, ws, gain, conv_w, conv_b, xw_t):
    micro, tokens, quarter = xs[0].shape
    width = gain.shape[1]
    chans = conv_w.shape[1]
    count = xw_t.shape[0]
    per = lambda *tail: pl.BlockSpec((1,) + tail, lambda m: (m,) + (0,) * len(tail))
    return pl.pallas_call(
        partial(pre_kernel, len(xs), len(ws)),
        grid=(micro,),
        in_specs=[SMEM]
        + [per(tokens, quarter)] * len(xs)
        + [whole(w.shape) for w in ws]
        + [whole(gain.shape), whole(conv_w.shape), whole(conv_b.shape), whole(xw_t.shape)],
        out_specs=[
            per(tokens, width),
            whole((width, 2 * chans)),
            per(tokens, chans),
            per(tokens, chans),
            per(tokens, chans),
            per(tokens, chans),
            per(tokens, LANES),
            per(count, tokens),
            per(count, tokens),
        ],
        out_shape=[
            struct((micro, tokens, width), BF16),
            struct((width, 2 * chans), BF16),
            struct((micro, tokens, chans), F32),
            struct((micro, tokens, chans), F32),
            struct((micro, tokens, chans), F32),
            struct((micro, tokens, chans), F32),
            struct((micro, tokens, LANES), F32),
            struct((micro, count, tokens), F32),
            struct((micro, count, tokens), BF16),
        ],
        scratch_shapes=[pltpu.VMEM((tokens + GROUP, chans), F32)],
        compiler_params=params(1),
        name="pre",
    )(ids, *xs, *ws, gain, conv_w, conv_b, xw_t)


def run_fwd(ids, lens, projs, ws, u_act, gate, dt_w, dt_b, a_log, skip, width):
    micro, tokens, chans = u_act.shape
    parts = len(projs)
    quarter = width // parts
    count = projs[0].shape[1]
    nstate = a_log.shape[0]
    span = min(LANES, tokens)
    rows = lambda *tail: pl.BlockSpec((1, span) + tail, lambda m, b: (m, b) + (0,) * len(tail))
    return pl.pallas_call(
        partial(fwd_kernel, parts, len(ws)),
        grid=(micro, tokens // span),
        in_specs=[SMEM, SMEM]
        + [pl.BlockSpec((1, count, span), lambda m, b: (m, 0, b))] * parts
        + [whole(w.shape) for w in ws]
        + [rows(chans), rows(chans)]
        + [whole(v.shape) for v in (dt_w, dt_b, a_log, skip)],
        out_specs=[
            rows(chans),
            rows(chans),
            rows(chans),
            pl.BlockSpec((1, span * nstate, chans), lambda m, b: (m, b, 0)),
            whole((chans, width)),
        ]
        + [rows(quarter)] * parts,
        out_shape=[
            struct((micro, tokens, chans), F32),
            struct((micro, tokens, chans), F32),
            struct((micro, tokens, chans), BF16),
            struct((micro, tokens * nstate, chans), F32),
            struct((chans, width), BF16),
            struct((micro, tokens, quarter), F32),
        ]
        + [struct((micro, tokens, quarter), BF16)] * (parts - 1),
        scratch_shapes=[pltpu.VMEM((span, chans), F32)] * 3
        + [pltpu.VMEM((chans // LANES, GROUP * GROUP, LANES), F32), pltpu.VMEM((nstate, chans), F32)],
        compiler_params=params(2),
        name="scan_forward",
    )(ids, lens, *projs, *ws, u_act, gate, dt_w, dt_b, a_log, skip)


def run_bwd(ids, lens, projs, cots, w_full, u_act, gate, dt_lin, y_rows, states, dt_w, a_log, skip):
    micro, tokens, chans = u_act.shape
    parts = len(projs)
    width = w_full.shape[1]
    quarter = cots[0].shape[2]
    count = projs[0].shape[1]
    nstate = a_log.shape[0]
    rank = dt_w.shape[0]
    span = min(LANES, tokens)
    blocks = tokens // span
    small = rank + nstate + GROUP
    rows = lambda *tail: pl.BlockSpec(
        (1, span) + tail, lambda m, b: (m, blocks - 1 - b) + (0,) * len(tail)
    )
    proj = pl.BlockSpec((1, count, span), lambda m, b: (m, 0, blocks - 1 - b))
    return pl.pallas_call(
        partial(bwd_kernel, parts),
        grid=(micro, blocks),
        in_specs=[SMEM, SMEM]
        + [proj] * parts
        + [rows(quarter)] * parts
        + [whole(w_full.shape), rows(chans), rows(chans), rows(chans), rows(chans)]
        + [pl.BlockSpec((1, span * nstate, chans), lambda m, b: (m, blocks - 1 - b, 0))]
        + [whole(v.shape) for v in (dt_w, a_log, skip)],
        out_specs=[rows(width), proj, proj, rows(chans), rows(chans), whole((small, chans))],
        out_shape=[
            struct((micro, tokens, width), BF16),
            struct((micro, count, tokens), F32),
            struct((micro, count, tokens), BF16),
            struct((micro, tokens, chans), F32),
            struct((micro, tokens, chans), BF16),
            struct((small, chans), F32),
        ],
        scratch_shapes=[pltpu.VMEM((span, chans), F32)] * 5
        + [pltpu.VMEM((chans // LANES, GROUP * GROUP, LANES), F32)] * 2
        + [pltpu.VMEM((nstate, chans), F32)] * 2,
        compiler_params=params(2),
        name="scan_backward",
    )(ids, lens, *projs, *cots, w_full, u_act, gate, dt_lin, y_rows, states, dt_w, a_log, skip)


def run_post(ids, projs, xs, d_scan, d_gate, u_act, summed, inner, inv, w_full, gain, xw_t, conv_w):
    micro, tokens, chans = u_act.shape
    parts = len(projs)
    width = w_full.shape[0]
    quarter = width // parts
    count = projs[0].shape[1]
    taps = conv_w.shape[0]
    small = count + GROUP * -(-(taps + 1) // GROUP)
    lanes = max(width, LANES * -(-micro * tokens // LANES))
    per = lambda *tail: pl.BlockSpec((1,) + tail, lambda m: (m,) + (0,) * len(tail))
    return pl.pallas_call(
        partial(post_kernel, parts),
        grid=(micro,),
        in_specs=[SMEM]
        + [per(count, tokens)] * parts
        + [per(tokens, quarter)] * parts
        + [per(tokens, chans)] * 5
        + [per(tokens, LANES)]
        + [whole(v.shape) for v in (w_full, gain, xw_t, conv_w)],
        out_specs=[per(tokens, 2 * chans), whole((small, chans)), whole((GROUP, lanes))]
        + [per(tokens, quarter)] * parts,
        out_shape=[
            struct((micro, tokens, 2 * chans), BF16),
            struct((small, chans), F32),
            struct((GROUP, lanes), F32),
            struct((micro, tokens, quarter), F32),
        ]
        + [struct((micro, tokens, quarter), BF16)] * (parts - 1),
        scratch_shapes=[pltpu.VMEM((tokens + GROUP, chans), F32)] * 2,
        compiler_params=params(1),
        name="post",
    )(ids, *projs, *xs, d_scan, d_gate, u_act, summed, inner, inv, w_full, gain, xw_t, conv_w)


def run_grad(kernel, name, ids, left, right, shape, chips):
    if chips == 0:
        outs = [struct(shape, F32), struct((GROUP, LANES), BF16)]
    else:
        outs = [struct((chips,) + shape, F32), struct((chips,) + shape, BF16)]
    return pl.pallas_call(
        partial(kernel, chips),
        in_specs=[SMEM, pl.BlockSpec(memory_space=pltpu.VMEM), pl.BlockSpec(memory_space=pltpu.VMEM)],
        out_specs=[pl.BlockSpec(memory_space=pltpu.VMEM)] * 2,
        out_shape=outs,
        compiler_params=pltpu.CompilerParams(vmem_limit_bytes=56 * 1024 * 1024),
        name=name,
    )(ids, left, right)


def others(value, axis, step=1):
    count = lax.axis_size(axis)
    return [swap(value, axis, mask) for mask in range(step, count, step)]


def gather_blocks(shard):
    mine = [shard] + others(shard, "dp", 2)
    return mine + [swap(block, "dp", 1) for block in mine]


def sum_scattered(mine, theirs):
    got = swap(theirs, "dp", 1)
    total = mine + got.astype(F32)
    result = total[0]
    for j in range(1, mine.shape[0]):
        result = result + swap(total[j].astype(BF16), "dp", 2 * j).astype(F32)
    return result


def sum_all(value):
    core = lax.rem(lax.axis_index("dp"), 2)
    half = value.shape[0] // 2
    halves = value.reshape((2, half) + value.shape[1:])
    mine = lax.dynamic_index_in_dim(halves, core, 0, keepdims=False)
    theirs = lax.dynamic_index_in_dim(halves, 1 - core, 0, keepdims=False)
    total = mine + swap(theirs, "dp", 1)
    for got in others(total, "dp", 2):
        total = total + got
    other = swap(total, "dp", 1)
    first = jnp.where(core == 0, total, other)
    second = jnp.where(core == 0, other, total)
    return jnp.concatenate([first, second], axis=0)


def body(
    tokens,
    lengths,
    norm_gain,
    in_weight,
    x_weight,
    dt_weight,
    dt_bias,
    conv_weight,
    conv_bias,
    a_log,
    skip,
    out_weight,
    cotangent,
):
    micro, seq, quarter = tokens.shape
    chans = in_weight.shape[2]
    width = norm_gain.shape[0]
    dps = lax.axis_size("dp")
    rank = dt_weight.shape[0]
    nstate = a_log.shape[0]
    taps = conv_weight.shape[0]
    count = x_weight.shape[1]
    ids = jnp.stack([lax.axis_index("tensor"), lax.axis_index("dp")]).astype(jnp.int32)
    lens = lengths[:, 0]
    gain = norm_gain[None]
    xw_t = x_weight.T
    in_rows = in_weight.reshape(in_weight.shape[0], 2 * chans)
    by_block = in_rows.shape[0] % LANES == 0 and out_weight.shape[1] % LANES == 0
    chips = dps // 2 if by_block else 0

    xs = [tokens] + others(tokens, "tensor")
    if by_block:
        in_blocks = gather_blocks(in_rows)
        out_blocks = gather_blocks(out_weight)
    else:
        in_blocks = [lax.all_gather(in_rows, "dp", axis=0, tiled=True)]
        out_blocks = [lax.all_gather(out_weight, "dp", axis=1, tiled=True)]
    cots = [cotangent] + others(cotangent, "tensor")

    normed, in_full, inner, summed, u_act, gate, inv, proj, proj_low = run_pre(
        ids, xs, in_blocks, gain, conv_weight, conv_bias[None], xw_t
    )
    projs = [proj] + others(proj_low, "tensor")
    dt_lin, y_rows, gated, states, out_full, own_out, *out_terms = run_fwd(
        ids, lens, projs, out_blocks, u_act, gate, dt_weight, dt_bias[None], a_log, skip[None], width
    )
    branch = own_out
    for k, term in enumerate(out_terms):
        branch = branch + swap(term, "tensor", k + 1).astype(F32)
    mixed = (tokens.astype(F32) + branch).astype(BF16)
    cot_full, d_proj, d_proj_low, d_scan, d_gate, small = run_bwd(
        ids, lens, projs, cots, out_full, u_act, gate, dt_lin, y_rows, states, dt_weight, a_log, skip[None]
    )
    d_projs = [d_proj] + others(d_proj_low, "tensor")
    out_mine, out_theirs = run_grad(
        grad_out_kernel,
        "grad_out",
        ids,
        gated.reshape(micro * seq, chans),
        cot_full.reshape(micro * seq, width),
        (chans, out_weight.shape[1]) if chips else (chans, width),
        chips,
    )
    d_both, small_in, tiny, own_norm, *norm_terms = run_post(
        ids, d_projs, xs, d_scan, d_gate, u_act, summed, inner, inv, in_full, gain, xw_t, conv_weight
    )
    in_mine, in_theirs = run_grad(
        grad_in_kernel,
        "grad_in",
        ids,
        normed.reshape(micro * seq, width),
        d_both.reshape(micro * seq, 2 * chans),
        (in_rows.shape[0], 2 * chans) if chips else (width, 2 * chans),
        chips,
    )
    for got in others(tiny, "tensor"):
        tiny = tiny + got
    d_norm = own_norm
    for k, term in enumerate(norm_terms):
        d_norm = d_norm + swap(term, "tensor", k + 1).astype(F32)
    if chips:
        grad_out = sum_scattered(out_mine, out_theirs)
        grad_in = sum_scattered(in_mine, in_theirs)
    else:
        grad_out = lax.psum_scatter(out_mine, "dp", scatter_dimension=1, tiled=True)
        grad_in = lax.psum_scatter(in_mine, "dp", scatter_dimension=0, tiled=True)
    small = sum_all(small)
    gain_rows = tiny[0, :width].reshape(-1, chans)
    small_in = lax.dynamic_update_slice_in_dim(small_in, gain_rows, count + taps + 1, 0)
    small_in = sum_all(small_in)
    scale = inv[:, :, :1]
    dots = tiny[1, : micro * seq].reshape(micro, seq, 1)
    own_gain = lax.dynamic_slice_in_dim(norm_gain, ids[0] * quarter, quarter, 0)
    d_x = scale * (d_norm * own_gain) - tokens.astype(F32) * (scale * scale * scale * dots / width)
    input_grad = cotangent.astype(F32) + d_x
    row = count + taps + 1
    return (
        mixed,
        input_grad,
        small_in[row : row + width // chans].reshape(width),
        grad_in.reshape(in_weight.shape),
        small_in[:count].T,
        small[:rank],
        small[rank + nstate],
        small_in[count : count + taps],
        small_in[count + taps],
        small[rank : rank + nstate],
        small[rank + nstate + 1],
        grad_out,
    )


def solution(mesh):
    rows = P(None, "dp", "tensor")
    chans = P(None, "tensor")
    return jax.shard_map(
        body,
        mesh=mesh,
        in_specs=(
            rows,
            P(None, "dp"),
            P(),
            P("dp", None, "tensor"),
            P("tensor", None),
            chans,
            P("tensor"),
            chans,
            P("tensor"),
            chans,
            P("tensor"),
            P("tensor", "dp"),
            rows,
        ),
        out_specs=(
            rows,
            rows,
            P(),
            P("dp", None, "tensor"),
            P("tensor", None),
            chans,
            P("tensor"),
            chans,
            P("tensor"),
            chans,
            P("tensor"),
            P("tensor", "dp"),
        ),
        check_vma=False,
    )
```

```python
from functools import partial

import jax
import jax.numpy as jnp
from jax import lax
from jax.experimental import pallas as pl
from jax.experimental.pallas import tpu as pltpu
from jax.sharding import PartitionSpec as P

EPS = 1e-05
F32 = jnp.float32
BF16 = jnp.bfloat16
GROUP = 8
LANES = 128
STEP = 48


def contract(left, right, left_dim, right_dim):
    return lax.dot_general(
        left, right, (((left_dim,), (right_dim,)), ((), ())), preferred_element_type=F32
    )


def sigmoid(v):
    return 1.0 / (1.0 + jnp.exp(-v))


def softplus(v):
    return jnp.maximum(v, 0.0) + jnp.log1p(jnp.exp(-jnp.abs(v)))


def swap(value, axis, mask):
    count = lax.axis_size(axis)
    return lax.ppermute(value, axis, [(i, i ^ mask) for i in range(count)])


def pre_kernel(parts, blocks, ids, *refs):
    xs, refs = refs[:parts], refs[parts:]
    ws, refs = refs[:blocks], refs[blocks:]
    gain, conv_w, conv_b, xw_t = refs[:4]
    normed, w_full, inner, summed, u_act, gate, inv, proj, proj_low, padded = refs[4:]
    quarter = xs[0].shape[2]
    chans = inner.shape[2]

    @pl.when(pl.program_id(0) == 0)
    def _():
        gather_rows(ids, ws, w_full)
        padded[:GROUP, :] = jnp.zeros((GROUP, chans), F32)

    square = 0.0
    for x in xs:
        rows = x[0].astype(F32)
        square = square + jnp.sum(rows * rows, axis=1, keepdims=True)
    scale = lax.rsqrt(square / (parts * quarter) + EPS)
    inv[0] = jnp.broadcast_to(scale, inv.shape[1:])
    for k, x in enumerate(xs):
        cols = pl.ds(pl.multiple_of((ids[0] ^ k) * quarter, LANES), quarter)
        normed[0, :, cols] = (x[0].astype(F32) * scale * gain[:, cols]).astype(BF16)
    both = jnp.dot(normed[0], w_full[:, : 2 * chans], preferred_element_type=F32)
    gate[0] = both[:, chans:]
    inner_in = both[:, :chans]
    inner[0] = inner_in
    tokens = inner_in.shape[0]
    padded[GROUP:, :] = inner_in
    taps = conv_w.shape[0]
    total = jnp.broadcast_to(conv_b[...], inner_in.shape)
    for j in range(taps):
        total = total + conv_w[j : j + 1, :] * padded[pl.ds(GROUP - taps + 1 + j, tokens), :]
    summed[0] = total
    act = total * sigmoid(total)
    u_act[0] = act
    partial_sum = contract(xw_t[...], act.astype(BF16), 1, 1)
    proj[0] = partial_sum
    proj_low[0] = partial_sum.astype(BF16)


def core_half(ids, chans, flip=0):
    half = chans // 2
    return pl.ds(pl.multiple_of(((ids[1] & 1) ^ flip) * half, LANES), half)


def gather_rows(ids, blocks, full):
    if len(blocks) == 1:
        full[...] = blocks[0][...]
        return
    chips = len(blocks) // 2
    for side in range(2):
        for j in range(chips):
            block = blocks[side * chips + j]
            index = (ids[1] ^ (2 * j)) ^ side
            rows = block.shape[0]
            full[pl.ds(pl.multiple_of(index * rows, 16), rows), :] = block[...]


def split(v):
    high = v.astype(BF16)
    return high, (v - high.astype(F32)).astype(BF16)


def spread(left, right, out):
    count, span = left.shape
    lanes = lax.broadcasted_iota(jnp.int32, left.shape, 1)
    shape = (2 * span, 2 * LANES)
    from_left = lax.broadcasted_iota(jnp.int32, shape, 0) < span
    to_left = lax.broadcasted_iota(jnp.int32, shape, 1) < LANES
    ones = jnp.where(from_left == to_left, 1.0, 0.0).astype(BF16)
    rows = []
    for t in range(span):
        pair = [jnp.where(lanes == t, part, 0.0).astype(BF16) for part in (left, right)]
        rows.append(jnp.concatenate(pair, axis=1))
    out[...] = jnp.dot(jnp.concatenate(rows, axis=0), ones, preferred_element_type=F32)


def gather(left, right, count):
    span = right.shape[0]
    lanes = lax.broadcasted_iota(jnp.int32, (count, span), 1)
    wide = contract(left[...], right, 1, 1)
    totals = [jnp.zeros((count, span), F32)] * 4
    for t in range(span):
        totals[t % 4] = jnp.where(lanes == t, wide[t * count : (t + 1) * count, :], totals[t % 4])
    return (totals[0] + totals[1]) + (totals[2] + totals[3])


def sigmoid_of_softplus(step):
    series = step * (1.0 - step * (0.5 - step * (1.0 / 6.0 - step * (1.0 / 24.0))))
    return jnp.where(step < 0.05, series, 1.0 - jnp.exp(-step))


def fold(pend, out, start, half):
    for g in range(pend.shape[0]):
        total = pend[g, pl.ds(half * GROUP * GROUP, GROUP, stride=GROUP), :]
        for s in range(1, GROUP):
            total = total + pend[g, pl.ds(half * GROUP * GROUP + s, GROUP, stride=GROUP), :]
        out[pl.ds(start, GROUP), g * LANES : (g + 1) * LANES] = total


def fwd_kernel(parts, ids, lens, *refs):
    projs, refs = refs[:parts], refs[parts:]
    w_out, u_act, gate, dt_w, dt_b, a_log, skip = refs[:7]
    refs = refs[7:]
    dt, y_rows, gated, edge, low_state, vectors, own = refs[:7]
    sends, refs = refs[7 : 6 + parts], refs[6 + parts :]
    dtu, y, pend, carry = refs
    span, chans = dtu.shape
    nstate = a_log.shape[0]
    rank = dt_w.shape[0]
    block = pl.program_id(1)
    groups = chans // LANES

    @pl.when(block == 0)
    def _():
        carry[...] = jnp.zeros(carry.shape, F32)

    proj = projs[0][0]
    for other in projs[1:]:
        proj = proj + other[0].astype(F32)
    lin = contract(proj[:rank].astype(BF16), dt_w[...], 0, 0) + dt_b[...]
    step = softplus(lin)
    dt[0] = step
    dtu[...] = step * u_act[0]
    spread(proj[rank : rank + nstate], proj[rank + nstate :], vectors.at[0])
    rate = -jnp.exp(a_log[...])
    lane = [slice(g * LANES, (g + 1) * LANES) for g in range(groups)]

    edge[0, 0] = carry[...]

    def steps(i, state):
        state = list(state)
        for half in range(2):
            start = pl.multiple_of((2 * i + half) * GROUP, GROUP)
            dt_rows = dt[0, pl.ds(start, GROUP), :]
            dtu_rows = dtu[pl.ds(start, GROUP), :]
            for k in range(GROUP):
                at = pl.ds(pl.multiple_of((start + k) * nstate, nstate), nstate)
                b_t = vectors[0, at, :LANES]
                c_t = vectors[0, at, LANES:]
                rows = pl.ds((half * GROUP + k) * GROUP, GROUP)
                for g in range(groups):
                    dt_t = dt_rows[k : k + 1, lane[g]]
                    dtu_t = dtu_rows[k : k + 1, lane[g]]
                    new = jnp.exp(dt_t * rate[:, lane[g]]) * state[g] + dtu_t * b_t
                    state[g] = new
                    low_state[0, at, lane[g]] = new.astype(BF16)
                    term = c_t * new
                    pend[g, rows, :] = sum(term[s : s + GROUP] for s in range(0, nstate, GROUP))
            fold(pend, y, start, half)
        return tuple(state)

    last = lax.fori_loop(0, span // (2 * GROUP), steps, tuple(carry[:, l] for l in lane))
    for g in range(groups):
        carry[:, lane[g]] = last[g]
    rows = y[...] + skip[...] * u_act[0]
    y_rows[0] = rows
    gate_in = gate[0]
    position = block * span + lax.broadcasted_iota(jnp.int32, (span, 1), 0)
    live = (position < lens[pl.program_id(0)]).astype(F32)
    low = (rows * (gate_in * sigmoid(gate_in)) * live).astype(BF16)
    gated[0] = low
    quarter = own.shape[2]
    for k in range(parts):
        rows = pl.ds(pl.multiple_of((ids[0] ^ k) * quarter, LANES), quarter)
        term = contract(low, w_out[rows, :], 1, 1)
        if k == 0:
            own[0] = term
        else:
            sends[k - 1][0] = term.astype(BF16)


def bwd_kernel(parts, ids, lens, *refs):
    projs, refs = refs[:parts], refs[parts:]
    cots, refs = refs[:parts], refs[parts:]
    w_full, u_act, gate, dt, y_rows, edge, low_state, vectors, dt_w, a_log, skip = refs[:11]
    refs = refs[11:]
    cot_full, d_proj, d_proj_low, d_scan, d_gate, small = refs[:6]
    dtu, d_y, d_dtu, d_dta, pend_q, pend_r, carry, g_rate, low_grad = refs[6:]
    span, chans = dtu.shape
    nstate = a_log.shape[0]
    rank = dt_w.shape[0]
    first = (pl.program_id(0) == 0) & (pl.program_id(1) == 0)
    last = (pl.program_id(0) == pl.num_programs(0) - 1) & (pl.program_id(1) == pl.num_programs(1) - 1)
    block = pl.num_programs(1) - 1 - pl.program_id(1)
    groups = chans // LANES
    quarter = cots[0].shape[2]
    lane = [slice(g * LANES, (g + 1) * LANES) for g in range(groups)]

    @pl.when(first)
    def _():
        small[...] = jnp.zeros(small.shape, F32)
        g_rate[...] = jnp.zeros(g_rate.shape, F32)

    @pl.when(pl.program_id(1) == 0)
    def _():
        carry[...] = jnp.zeros(carry.shape, F32)

    for k, cot in enumerate(cots):
        cols = pl.ds(pl.multiple_of((ids[0] ^ k) * quarter, LANES), quarter)
        cot_full[0, :, cols] = cot[0]
    d_gated = jnp.dot(cot_full[0], w_full[...], preferred_element_type=F32)

    proj = projs[0][0]
    for other in projs[1:]:
        proj = proj + other[0].astype(F32)
    dt_low = proj[:rank].astype(BF16)
    u = u_act[0]
    step = dt[0]
    dtu[...] = step * u
    gate_in = gate[0]
    gate_sig = sigmoid(gate_in)
    position = block * span + lax.broadcasted_iota(jnp.int32, (span, 1), 0)
    live = (position < lens[pl.program_id(0)]).astype(F32)
    d_live = d_gated * live
    d_rows = d_live * (gate_in * gate_sig)
    d_y[...] = d_rows
    d_gate[0] = (d_live * y_rows[0] * (gate_sig * (1.0 + gate_in * (1.0 - gate_sig)))).astype(BF16)
    rate = -jnp.exp(a_log[...])
    count = span // (2 * GROUP)

    def steps(i, loop):
        run, acc = list(loop[0]), list(loop[1])
        for half in reversed(range(2)):
            start = pl.multiple_of((2 * (count - 1 - i) + half) * GROUP, GROUP)
            dt_rows = dt[0, pl.ds(start, GROUP), :]
            dy_rows = d_y[pl.ds(start, GROUP), :]
            for k in reversed(range(GROUP)):
                at = pl.ds(pl.multiple_of((start + k) * nstate, nstate), nstate)
                b_t = vectors[0, at, :LANES]
                c_t = vectors[0, at, LANES:]
                rows = pl.ds((half * GROUP + k) * GROUP, GROUP)
                before = start + k - 1
                if half == 0 and k == 0:
                    before = jnp.maximum(before, 0)
                before = pl.ds(pl.multiple_of(before * nstate, nstate), nstate)
                for g in range(groups):
                    old = low_state[0, before, lane[g]].astype(F32)
                    if half == 0 and k == 0:
                        old = jnp.where(start == 0, edge[0, 0, :, lane[g]], old)
                    dt_t = dt_rows[k : k + 1, lane[g]]
                    dy_t = dy_rows[k : k + 1, lane[g]]
                    d_state = run[g] + c_t * dy_t
                    low_grad[at, lane[g]] = d_state.astype(BF16)
                    decayed = jnp.exp(dt_t * rate[:, lane[g]]) * d_state
                    run[g] = decayed
                    d_exp = decayed * old
                    acc[g] = acc[g] + d_exp * dt_t
                    term_q = d_exp * rate[:, lane[g]]
                    term_r = d_state * b_t
                    pend_q[g, rows, :] = sum(term_q[s : s + GROUP] for s in range(0, nstate, GROUP))
                    pend_r[g, rows, :] = sum(term_r[s : s + GROUP] for s in range(0, nstate, GROUP))
            fold(pend_q, d_dta, start, half)
            fold(pend_r, d_dtu, start, half)
        return tuple(run), tuple(acc)

    run, acc = lax.fori_loop(
        0,
        count,
        steps,
        (tuple(carry[:, l] for l in lane), tuple(g_rate[:, l] for l in lane)),
    )
    d_b = gather(low_grad, dtu[...].astype(BF16), nstate)
    d_c = gather(low_state.at[0], d_rows.astype(BF16), nstate)
    for g in range(groups):
        carry[:, lane[g]] = run[g]
        g_rate[:, lane[g]] = acc[g]
    d_lin = (d_dtu[...] * u + d_dta[...]) * sigmoid_of_softplus(step)
    d_scan[0] = d_dtu[...] * step + d_rows * skip[...]
    d_low = d_lin.astype(BF16)
    full = jnp.concatenate([contract(dt_w[...], d_low, 1, 1), d_b, d_c], axis=0)
    d_proj[0] = full
    d_proj_low[0] = full.astype(BF16)
    small[:rank, :] += jnp.dot(dt_low, d_low, preferred_element_type=F32)
    row = rank + nstate
    small[row : row + 1, :] += jnp.sum(d_lin, axis=0, keepdims=True)
    small[row + 1 : row + 2, :] += jnp.sum(d_rows * u, axis=0, keepdims=True)

    @pl.when(last)
    def _():
        small[rank : rank + nstate, :] = g_rate[...] * rate


def post_kernel(parts, ids, *refs):
    projs, refs = refs[:parts], refs[parts:]
    xs, refs = refs[:parts], refs[parts:]
    d_scan, d_gate, u_act, summed, inner, inv, w_full, gain, xw_t, conv_w, scan_small = refs[:11]
    refs = refs[11:]
    d_both, small, small_theirs, tiny, own = refs[:5]
    sends, refs = refs[5 : 4 + parts], refs[4 + parts :]
    padded, front = refs
    tokens, chans = d_scan.shape[1:]
    quarter = own.shape[2]
    taps = conv_w.shape[0]
    m = pl.program_id(0)
    base = scan_small.shape[0]

    @pl.when(m == 0)
    def _():
        padded[tokens:, :] = jnp.zeros((GROUP, chans), F32)
        front[:GROUP, :] = jnp.zeros((GROUP, chans), F32)
        small[...] = jnp.zeros(small.shape, F32)
        small[:base, :] = scan_small[...]
        tiny[...] = jnp.zeros(tiny.shape, F32)

    proj = projs[0][0]
    for other in projs[1:]:
        proj = proj + other[0].astype(F32)
    d_proj = proj.astype(BF16)
    count = d_proj.shape[0]
    d_u = d_scan[0] + contract(d_proj, xw_t[...], 0, 0)
    small[base : base + count, :] += jnp.dot(d_proj, u_act[0].astype(BF16), preferred_element_type=F32)
    conv = summed[0]
    sig = sigmoid(conv)
    d_conv = d_u * (sig * (1.0 + conv * (1.0 - sig)))
    padded[:tokens, :] = d_conv
    front[GROUP:, :] = inner[0]
    d_inner = 0.0
    for j in range(taps):
        d_inner = d_inner + conv_w[j : j + 1, :] * padded[pl.ds(taps - 1 - j, tokens), :]
        small[base + count + j : base + count + j + 1, :] += jnp.sum(
            d_conv * front[pl.ds(GROUP - taps + 1 + j, tokens), :], axis=0, keepdims=True
        )
    small[base + count + taps : base + count + taps + 1, :] += jnp.sum(d_conv, axis=0, keepdims=True)

    @pl.when(m == pl.num_programs(0) - 1)
    def _():
        small_theirs[...] = small[:, core_half(ids, chans, 1)]

    d_both[0, :, :chans] = d_inner.astype(BF16)
    d_both[0, :, chans:] = d_gate[0]
    scale = inv[0][:, :1]
    dots = 0.0
    for k in range(parts):
        cols = pl.ds(pl.multiple_of((ids[0] ^ k) * quarter, LANES), quarter)
        d_norm = contract(d_both[0], w_full[cols, :], 1, 1)
        if k == 0:
            own[0] = d_norm
        else:
            sends[k - 1][0] = d_norm.astype(BF16)
        along = d_norm * xs[k][0].astype(F32)
        tiny[0:1, cols] += jnp.sum(along * scale, axis=0, keepdims=True)
        weighted = along * gain[:, cols]
        for c in range(0, quarter, LANES):
            dots = dots + weighted[:, c : c + LANES]
    dots = jnp.sum(jnp.transpose(dots), axis=0, keepdims=True)
    tiny[1:2, pl.ds(pl.multiple_of(m * tokens, LANES), tokens)] = dots


def grad_kernel(chips, ids, rows_of, columns_of, mine, theirs):
    if chips == 0:
        mine[...] = contract(rows_of[...], columns_of[...], 0, 0)
        return
    rows = mine.shape[1]
    for side, out in enumerate((theirs, mine)):
        for j in range(chips):
            index = (ids[1] ^ (2 * j)) ^ (1 - side)
            cols = pl.ds(pl.multiple_of(index * rows, LANES), rows)
            out[j] = contract(rows_of[:, cols], columns_of[...], 0, 0).astype(out.dtype)


def merge_kernel(
    row, ids, mine_in, got_in, mine_out, got_out, small, small_got, tiny, tiny_got, own, part, *sends
):
    rows, wide = mine_in.shape[1:]
    chans = small.shape[1]
    half = chans // 2
    width = tiny.shape[1]
    part[...] = small[:, core_half(ids, chans)] + small_got[...]
    for i in range(width // chans):
        cols = pl.ds(pl.multiple_of((ids[1] & 1) * half, LANES) + i * chans, half)
        part[row + i : row + i + 1, :] = tiny[0:1, cols] + tiny_got[0:1, cols]
    own[:, :wide] = mine_in[0] + got_in[0].astype(F32)
    own[:, wide:] = mine_out[0] + got_out[0].astype(F32)
    pieces = part.shape[0] // STEP
    for j, send in enumerate(sends):
        send[:rows, :wide] = (mine_in[j + 1] + got_in[j + 1].astype(F32)).astype(BF16)
        send[:rows, wide:] = (mine_out[j + 1] + got_out[j + 1].astype(F32)).astype(BF16)
        for c in range(pieces):
            send[rows:, c * half : (c + 1) * half] = part[c * STEP : (c + 1) * STEP, :].astype(BF16)
        send[rows:, pieces * half :] = jnp.zeros((STEP, send.shape[1] - pieces * half), BF16)


def final_kernel(own, part, *refs):
    gots, (grad_in, grad_out, half) = refs[:-3], refs[-3:]
    rows, kinds, chans = grad_in.shape
    wide = kinds * chans
    total = own[...]
    for got in gots:
        total = total + got[:rows, :].astype(F32)
    for k in range(kinds):
        grad_in[:, k, :] = total[:, k * chans : (k + 1) * chans]
    grad_out[...] = jnp.transpose(total[:, wide:])
    lanes = part.shape[1]
    for c in range(part.shape[0] // STEP):
        total = part[c * STEP : (c + 1) * STEP, :]
        for got in gots:
            total = total + got[rows:, c * lanes : (c + 1) * lanes].astype(F32)
        half[c * STEP : (c + 1) * STEP, :] = total


def outputs_kernel(base, ids, half, half_got, gain, x_w, dt_w, dt_b, conv_w, conv_b, a_log, skip, full):
    chans = full.shape[1]
    full[:, core_half(ids, chans)] = half[...]
    full[:, core_half(ids, chans, 1)] = half_got[...]
    rank = dt_w.shape[0]
    nstate = a_log.shape[0]
    count = x_w.shape[0]
    taps = conv_w.shape[0]
    dt_w[...] = full[:rank, :]
    a_log[...] = full[rank : rank + nstate, :]
    dt_b[...] = full[rank + nstate : rank + nstate + 1, :]
    skip[...] = full[rank + nstate + 1 : rank + nstate + 2, :]
    x_w[...] = full[base : base + count, :]
    conv_w[...] = full[base + count : base + count + taps, :]
    conv_b[...] = full[base + count + taps : base + count + taps + 1, :]
    for i in range(gain.shape[1] // chans):
        row = base + count + taps + 1 + i
        gain[:, i * chans : (i + 1) * chans] = full[row : row + 1, :]


def whole(shape):
    return pl.BlockSpec(shape, lambda *_: (0,) * len(shape))


SMEM = pl.BlockSpec(memory_space=pltpu.SMEM)


def params(grid, mib=56):
    return pltpu.CompilerParams(
        dimension_semantics=("arbitrary",) * grid, vmem_limit_bytes=mib * 1024 * 1024
    )


def struct(shape, dtype):
    return jax.ShapeDtypeStruct(shape, dtype)


def run_pre(ids, xs, ws, gain, conv_w, conv_b, xw_t):
    micro, tokens, quarter = xs[0].shape
    width = gain.shape[1]
    chans = conv_w.shape[1]
    count = xw_t.shape[0]
    per = lambda *tail: pl.BlockSpec((1,) + tail, lambda m: (m,) + (0,) * len(tail))
    return pl.pallas_call(
        partial(pre_kernel, len(xs), len(ws)),
        grid=(micro,),
        in_specs=[SMEM]
        + [per(tokens, quarter)] * len(xs)
        + [whole(w.shape) for w in ws]
        + [whole(gain.shape), whole(conv_w.shape), whole(conv_b.shape), whole(xw_t.shape)],
        out_specs=[
            per(tokens, width),
            whole((width, ws[0].shape[1])),
            per(tokens, chans),
            per(tokens, chans),
            per(tokens, chans),
            per(tokens, chans),
            per(tokens, LANES),
            per(count, tokens),
            per(count, tokens),
        ],
        out_shape=[
            struct((micro, tokens, width), BF16),
            struct((width, ws[0].shape[1]), BF16),
            struct((micro, tokens, chans), F32),
            struct((micro, tokens, chans), F32),
            struct((micro, tokens, chans), F32),
            struct((micro, tokens, chans), F32),
            struct((micro, tokens, LANES), F32),
            struct((micro, count, tokens), F32),
            struct((micro, count, tokens), BF16),
        ],
        scratch_shapes=[pltpu.VMEM((tokens + GROUP, chans), F32)],
        compiler_params=params(1),
        name="pre",
    )(ids, *xs, *ws, gain, conv_w, conv_b, xw_t)


def run_fwd(ids, lens, projs, w_full, u_act, gate, dt_w, dt_b, a_log, skip):
    micro, tokens, chans = u_act.shape
    parts = len(projs)
    width = w_full.shape[0]
    quarter = width // parts
    count = projs[0].shape[1]
    nstate = a_log.shape[0]
    span = min(LANES, tokens)
    rows = lambda *tail: pl.BlockSpec((1, span) + tail, lambda m, b: (m, b) + (0,) * len(tail))
    return pl.pallas_call(
        partial(fwd_kernel, parts),
        grid=(micro, tokens // span),
        in_specs=[SMEM, SMEM]
        + [pl.BlockSpec((1, count, span), lambda m, b: (m, 0, b))] * parts
        + [pl.BlockSpec((width, chans), lambda m, b: (0, 2)), rows(chans), rows(chans)]
        + [whole(v.shape) for v in (dt_w, dt_b, a_log, skip)],
        out_specs=[
            rows(chans),
            rows(chans),
            rows(chans),
            pl.BlockSpec((1, 1, nstate, chans), lambda m, b: (m, b, 0, 0)),
            pl.BlockSpec((1, span * nstate, chans), lambda m, b: (m, b, 0)),
            pl.BlockSpec((1, span * nstate, 2 * LANES), lambda m, b: (m, b, 0)),
        ]
        + [rows(quarter)] * parts,
        out_shape=[
            struct((micro, tokens, chans), F32),
            struct((micro, tokens, chans), F32),
            struct((micro, tokens, chans), BF16),
            struct((micro, tokens // span, nstate, chans), F32),
            struct((micro, tokens * nstate, chans), BF16),
            struct((micro, tokens * nstate, 2 * LANES), F32),
            struct((micro, tokens, quarter), F32),
        ]
        + [struct((micro, tokens, quarter), BF16)] * (parts - 1),
        scratch_shapes=[pltpu.VMEM((span, chans), F32)] * 2
        + [pltpu.VMEM((chans // LANES, 2 * GROUP * GROUP, LANES), F32), pltpu.VMEM((nstate, chans), F32)],
        compiler_params=params(2),
        name="scan_forward",
    )(ids, lens, *projs, w_full, u_act, gate, dt_w, dt_b, a_log, skip)


def run_bwd(ids, lens, projs, cots, w_full, u_act, gate, dt, y_rows, edge, low_state, vectors, dt_w, a_log, skip):
    micro, tokens, chans = u_act.shape
    parts = len(projs)
    width = w_full.shape[0]
    quarter = cots[0].shape[2]
    count = projs[0].shape[1]
    nstate = a_log.shape[0]
    rank = dt_w.shape[0]
    span = min(LANES, tokens)
    blocks = tokens // span
    small = STEP * -(-(rank + nstate + 2) // STEP)
    rows = lambda *tail: pl.BlockSpec(
        (1, span) + tail, lambda m, b: (m, blocks - 1 - b) + (0,) * len(tail)
    )
    proj = pl.BlockSpec((1, count, span), lambda m, b: (m, 0, blocks - 1 - b))
    return pl.pallas_call(
        partial(bwd_kernel, parts),
        grid=(micro, blocks),
        in_specs=[SMEM, SMEM]
        + [proj] * parts
        + [rows(quarter)] * parts
        + [pl.BlockSpec((width, chans), lambda m, b: (0, 2)), rows(chans), rows(chans), rows(chans), rows(chans)]
        + [pl.BlockSpec((1, 1, nstate, chans), lambda m, b: (m, blocks - 1 - b, 0, 0))]
        + [pl.BlockSpec((1, span * nstate, chans), lambda m, b: (m, blocks - 1 - b, 0))]
        + [pl.BlockSpec((1, span * nstate, 2 * LANES), lambda m, b: (m, blocks - 1 - b, 0))]
        + [whole(v.shape) for v in (dt_w, a_log, skip)],
        out_specs=[rows(width), proj, proj, rows(chans), rows(chans), whole((small, chans))],
        out_shape=[
            struct((micro, tokens, width), BF16),
            struct((micro, count, tokens), F32),
            struct((micro, count, tokens), BF16),
            struct((micro, tokens, chans), F32),
            struct((micro, tokens, chans), BF16),
            struct((small, chans), F32),
        ],
        scratch_shapes=[pltpu.VMEM((span, chans), F32)] * 4
        + [pltpu.VMEM((chans // LANES, 2 * GROUP * GROUP, LANES), F32)] * 2
        + [pltpu.VMEM((nstate, chans), F32)] * 2
        + [pltpu.VMEM((span * nstate, chans), BF16)],
        compiler_params=params(2),
        name="scan_backward",
    )(ids, lens, *projs, *cots, w_full, u_act, gate, dt, y_rows, edge, low_state, vectors, dt_w, a_log, skip)


def run_post(ids, projs, xs, d_scan, d_gate, u_act, summed, inner, inv, w_full, gain, xw_t, conv_w, scan_small):
    micro, tokens, chans = u_act.shape
    parts = len(projs)
    width = w_full.shape[0]
    quarter = width // parts
    count = projs[0].shape[1]
    taps = conv_w.shape[0]
    small = scan_small.shape[0] + STEP * -(-(count + taps + 1 + width // chans) // STEP)
    lanes = max(width, LANES * -(-micro * tokens // LANES))
    per = lambda *tail: pl.BlockSpec((1,) + tail, lambda m: (m,) + (0,) * len(tail))
    return pl.pallas_call(
        partial(post_kernel, parts),
        grid=(micro,),
        in_specs=[SMEM]
        + [per(count, tokens)] * parts
        + [per(tokens, quarter)] * parts
        + [per(tokens, chans)] * 5
        + [per(tokens, LANES)]
        + [whole((width, 2 * chans))]
        + [whole(v.shape) for v in (gain, xw_t, conv_w, scan_small)],
        out_specs=[
            per(tokens, 2 * chans),
            whole((small, chans)),
            whole((small, chans // 2)),
            whole((GROUP, lanes)),
        ]
        + [per(tokens, quarter)] * parts,
        out_shape=[
            struct((micro, tokens, 2 * chans), BF16),
            struct((small, chans), F32),
            struct((small, chans // 2), F32),
            struct((GROUP, lanes), F32),
            struct((micro, tokens, quarter), F32),
        ]
        + [struct((micro, tokens, quarter), BF16)] * (parts - 1),
        scratch_shapes=[pltpu.VMEM((tokens + GROUP, chans), F32)] * 2,
        compiler_params=params(1),
        name="post",
    )(ids, *projs, *xs, d_scan, d_gate, u_act, summed, inner, inv, w_full, gain, xw_t, conv_w, scan_small)


def run_grad(name, ids, left, right, shape, chips):
    if chips == 0:
        outs = [struct(shape, F32), struct((GROUP, LANES), BF16)]
    else:
        outs = [struct((chips,) + shape, F32), struct((chips,) + shape, BF16)]
    return pl.pallas_call(
        partial(grad_kernel, chips),
        in_specs=[SMEM, pl.BlockSpec(memory_space=pltpu.VMEM), pl.BlockSpec(memory_space=pltpu.VMEM)],
        out_specs=[pl.BlockSpec(memory_space=pltpu.VMEM)] * 2,
        out_shape=outs,
        compiler_params=pltpu.CompilerParams(vmem_limit_bytes=56 * 1024 * 1024),
        name=name,
    )(ids, left, right)


VMEM = pl.BlockSpec(memory_space=pltpu.VMEM)


def run_local(kernel, name, outs, ids, *operands, scratch=()):
    return pl.pallas_call(
        kernel,
        in_specs=([SMEM] if ids is not None else []) + [VMEM] * len(operands),
        out_specs=[VMEM] * len(outs),
        out_shape=outs,
        scratch_shapes=list(scratch),
        compiler_params=pltpu.CompilerParams(vmem_limit_bytes=56 * 1024 * 1024),
        name=name,
    )(*(() if ids is None else (ids,)), *operands)


def after(value, *earlier):
    return lax.optimization_barrier((value, earlier))[0]


def others(value, axis, step=1):
    count = lax.axis_size(axis)
    return [swap(value, axis, mask) for mask in range(step, count, step)]


def with_sibling(blocks):
    return blocks + [swap(block, "dp", 1) for block in blocks]


def sum_all(value):
    core = lax.rem(lax.axis_index("dp"), 2)
    half = value.shape[0] // 2
    halves = value.reshape((2, half) + value.shape[1:])
    mine = lax.dynamic_index_in_dim(halves, core, 0, keepdims=False)
    theirs = lax.dynamic_index_in_dim(halves, 1 - core, 0, keepdims=False)
    total = mine + swap(theirs, "dp", 1)
    for got in others(total, "dp", 2):
        total = total + got
    other = swap(total, "dp", 1)
    first = jnp.where(core == 0, total, other)
    second = jnp.where(core == 0, other, total)
    return jnp.concatenate([first, second], axis=0)


def body(
    tokens,
    lengths,
    norm_gain,
    in_weight,
    x_weight,
    dt_weight,
    dt_bias,
    conv_weight,
    conv_bias,
    a_log,
    skip,
    out_weight,
    cotangent,
):
    micro, seq, quarter = tokens.shape
    chans = in_weight.shape[2]
    width = norm_gain.shape[0]
    dps = lax.axis_size("dp")
    rank = dt_weight.shape[0]
    nstate = a_log.shape[0]
    taps = conv_weight.shape[0]
    count = x_weight.shape[1]
    ids = jnp.stack([lax.axis_index("tensor"), lax.axis_index("dp")]).astype(jnp.int32)
    lens = lengths[:, 0]
    gain = norm_gain[None]
    xw_t = x_weight.T
    in_rows = in_weight.reshape(in_weight.shape[0], 2 * chans)
    by_block = in_rows.shape[0] % LANES == 0
    chips = dps // 2 if by_block else 0
    parts = lax.axis_size("tensor")
    weight = jnp.concatenate([in_rows, out_weight.T], axis=1)

    xs = [tokens] + others(tokens, "tensor")
    if by_block:
        mine = [weight] + [
            swap(after(weight, xs[1]) if mask > 4 else weight, "dp", mask) for mask in range(2, dps, 2)
        ]
        blocks = with_sibling(after(mine, *xs))
    else:
        blocks = [lax.all_gather(weight, "dp", axis=0, tiled=True)]
    normed, w_full, inner, summed, u_act, gate, inv, proj, proj_low = run_pre(
        ids, xs, blocks, gain, conv_weight, conv_bias[None], xw_t
    )
    early = swap(after(cotangent, *xs), "tensor", 2)
    projs = [proj] + others(proj_low, "tensor")
    late = after(cotangent, *projs)
    cots = [cotangent] + [early if mask == 2 else swap(late, "tensor", mask) for mask in range(1, parts)]
    dt, y_rows, gated, edge, low_state, vectors, own_out, *out_terms = run_fwd(
        ids, lens, projs, w_full, u_act, gate, dt_weight, dt_bias[None], a_log, skip[None]
    )
    out_got = [swap(term, "tensor", k + 1) for k, term in enumerate(out_terms)]
    cot_full, d_proj, d_proj_low, d_scan, d_gate, small = run_bwd(
        ids, lens, projs, cots, w_full, u_act, gate, dt, y_rows, edge, low_state, vectors, dt_weight, a_log, skip[None]
    )
    d_projs = [d_proj] + others(after(d_proj_low, *out_got), "tensor")
    branch = own_out
    for term in out_got:
        branch = branch + term.astype(F32)
    mixed = (tokens.astype(F32) + branch).astype(BF16)
    out_mine, out_theirs = run_grad(
        "grad_out",
        ids,
        after(cot_full, d_projs[1]).reshape(micro * seq, width),
        gated.reshape(micro * seq, chans),
        (weight.shape[0] if chips else width, chans),
        chips,
    )
    d_both, small, small_theirs, tiny, own_norm, *norm_terms = run_post(
        ids,
        d_projs,
        xs,
        after(d_scan, out_mine),
        d_gate,
        u_act,
        summed,
        inner,
        inv,
        w_full,
        gain,
        xw_t,
        conv_weight,
        small,
    )
    tiny_got = others(tiny, "tensor")
    norm_got = [swap(term, "tensor", k + 1) for k, term in enumerate(norm_terms[:1] + list(after(norm_terms[1:], *tiny_got)))]
    in_mine, in_theirs = run_grad(
        "grad_in",
        ids,
        after(normed, tiny_got[0]).reshape(micro * seq, width),
        d_both.reshape(micro * seq, 2 * chans),
        (weight.shape[0] if chips else width, 2 * chans),
        chips,
    )
    for got in tiny_got:
        tiny = tiny + got
    base = STEP * -(-(rank + nstate + 2) // STEP)
    row = base + count + taps + 1
    if chips:
        part_shape = struct((small.shape[0], chans // 2), F32)
        own_grad, part, *sends = run_local(
            partial(merge_kernel, row),
            "merge",
            [struct(weight.shape, F32), part_shape]
            + [struct((weight.shape[0] + STEP, weight.shape[1]), BF16)] * (chips - 1),
            ids,
            after(in_mine, norm_got[0]),
            swap(in_theirs, "dp", 1),
            out_mine,
            swap(out_theirs, "dp", 1),
            small,
            swap(small_theirs, "dp", 1),
            tiny,
            swap(tiny, "dp", 1),
        )
        gots = [swap(send, "dp", 2 * (j + 1)) for j, send in enumerate(sends)]
        own_grad = after(own_grad, *norm_got)
        grad_in, grad_out, half = run_local(
            final_kernel,
            "final",
            [struct(in_weight.shape, F32), struct(out_weight.shape, F32), part_shape],
            None,
            own_grad,
            part,
            *gots,
        )
        g_gain, g_x, g_dt, g_dtb, g_conv, g_convb, g_alog, g_skip = run_local(
            partial(outputs_kernel, base),
            "outputs",
            [
                struct((1, width), F32),
                struct((count, chans), F32),
                struct((rank, chans), F32),
                struct((1, chans), F32),
                struct((taps, chans), F32),
                struct((1, chans), F32),
                struct((nstate, chans), F32),
                struct((1, chans), F32),
            ],
            ids,
            half,
            swap(half, "dp", 1),
            scratch=[pltpu.VMEM((small.shape[0], chans), F32)],
        )
        smalls = (g_gain[0], g_x.T, g_dt, g_dtb[0], g_conv, g_convb[0], g_alog, g_skip[0])
    else:
        grad_in = lax.psum_scatter(in_mine, "dp", scatter_dimension=0, tiled=True)
        grad_out = lax.psum_scatter(out_mine, "dp", scatter_dimension=0, tiled=True).T
        small = sum_all(lax.dynamic_update_slice_in_dim(small, tiny[0, :width].reshape(-1, chans), row, 0))
        smalls = (
            small[row : row + width // chans].reshape(width),
            small[base : base + count].T,
            small[:rank],
            small[rank + nstate],
            small[base + count : base + count + taps],
            small[base + count + taps],
            small[rank : rank + nstate],
            small[rank + nstate + 1],
        )
    d_norm = own_norm
    for term in norm_got:
        d_norm = d_norm + term.astype(F32)
    scale = inv[:, :, :1]
    dots = tiny[1, : micro * seq].reshape(micro, seq, 1)
    own_gain = lax.dynamic_slice_in_dim(norm_gain, ids[0] * quarter, quarter, 0)
    d_x = scale * (d_norm * own_gain) - tokens.astype(F32) * (scale * scale * scale * dots / width)
    input_grad = cotangent.astype(F32) + d_x
    return (mixed, input_grad, smalls[0], grad_in.reshape(in_weight.shape)) + smalls[1:] + (grad_out,)


def solution(mesh):
    rows = P(None, "dp", "tensor")
    chans = P(None, "tensor")
    return jax.shard_map(
        body,
        mesh=mesh,
        in_specs=(
            rows,
            P(None, "dp"),
            P(),
            P("dp", None, "tensor"),
            P("tensor", None),
            chans,
            P("tensor"),
            chans,
            P("tensor"),
            chans,
            P("tensor"),
            P("tensor", "dp"),
            rows,
        ),
        out_specs=(
            rows,
            rows,
            P(),
            P("dp", None, "tensor"),
            P("tensor", None),
            chans,
            P("tensor"),
            chans,
            P("tensor"),
            chans,
            P("tensor"),
            P("tensor", "dp"),
        ),
        check_vma=False,
    )
```

```python
from functools import partial

import jax
import jax.numpy as jnp
from jax import lax
from jax.experimental import pallas as pl
from jax.experimental.pallas import tpu as pltpu
from jax.sharding import PartitionSpec as P

EPS = 1e-05
F32 = jnp.float32
BF16 = jnp.bfloat16
GROUP = 8
LANES = 128
SCAN_STEP = 32
POST_STEP = 64


def contract(left, right, left_dim, right_dim):
    return lax.dot_general(
        left, right, (((left_dim,), (right_dim,)), ((), ())), preferred_element_type=F32
    )


def sigmoid(v):
    return 1.0 / (1.0 + jnp.exp(-v))


def softplus(v):
    return jnp.maximum(v, 0.0) + jnp.log1p(jnp.exp(-jnp.abs(v)))


def swap(value, axis, mask):
    count = lax.axis_size(axis)
    return lax.ppermute(value, axis, [(i, i ^ mask) for i in range(count)])


def pre_kernel(parts, blocks, ids, *refs):
    xs, refs = refs[:parts], refs[parts:]
    ws, refs = refs[:blocks], refs[blocks:]
    gain, conv_w, conv_b, xw_t = refs[:4]
    normed, w_full, inner, summed, u_act, gate, inv, proj, proj_low, padded = refs[4:]
    quarter = xs[0].shape[2]
    chans = inner.shape[2]

    @pl.when(pl.program_id(0) == 0)
    def _():
        gather_rows(ids, ws, w_full)
        padded[:GROUP, :] = jnp.zeros((GROUP, chans), F32)

    square = 0.0
    for x in xs:
        rows = x[0].astype(F32)
        square = square + jnp.sum(rows * rows, axis=1, keepdims=True)
    scale = lax.rsqrt(square / (parts * quarter) + EPS)
    inv[0] = jnp.broadcast_to(scale, inv.shape[1:])
    for k, x in enumerate(xs):
        cols = pl.ds(pl.multiple_of((ids[0] ^ k) * quarter, LANES), quarter)
        normed[0, :, cols] = (x[0].astype(F32) * scale * gain[:, cols]).astype(BF16)
    both = jnp.dot(normed[0], w_full[:, : 2 * chans], preferred_element_type=F32)
    gate[0] = both[:, chans:]
    inner_in = both[:, :chans]
    inner[0] = inner_in
    tokens = inner_in.shape[0]
    padded[GROUP:, :] = inner_in
    taps = conv_w.shape[0]
    total = jnp.broadcast_to(conv_b[...], inner_in.shape)
    for j in range(taps):
        total = total + conv_w[j : j + 1, :] * padded[pl.ds(GROUP - taps + 1 + j, tokens), :]
    summed[0] = total
    act = total * sigmoid(total)
    u_act[0] = act
    partial_sum = contract(xw_t[...], act.astype(BF16), 1, 1)
    proj[0] = partial_sum
    proj_low[0] = partial_sum.astype(BF16)


def core_half(ids, chans, flip=0):
    half = chans // 2
    return pl.ds(pl.multiple_of(((ids[1] & 1) ^ flip) * half, LANES), half)


def gather_rows(ids, blocks, full):
    if len(blocks) == 1:
        full[...] = blocks[0][...]
        return
    chips = len(blocks) // 2
    for side in range(2):
        for j in range(chips):
            block = blocks[side * chips + j]
            index = (ids[1] ^ (2 * j)) ^ side
            rows = block.shape[0]
            full[pl.ds(pl.multiple_of(index * rows, 16), rows), :] = block[...]


def split(v):
    high = v.astype(BF16)
    return high, (v - high.astype(F32)).astype(BF16)


def spread(left, right, out):
    count, span = left.shape
    lanes = lax.broadcasted_iota(jnp.int32, left.shape, 1)
    shape = (2 * span, 2 * LANES)
    from_left = lax.broadcasted_iota(jnp.int32, shape, 0) < span
    to_left = lax.broadcasted_iota(jnp.int32, shape, 1) < LANES
    ones = jnp.where(from_left == to_left, 1.0, 0.0).astype(BF16)
    rows = []
    for t in range(span):
        pair = [jnp.where(lanes == t, part, 0.0).astype(BF16) for part in (left, right)]
        rows.append(jnp.concatenate(pair, axis=1))
    out[...] = jnp.dot(jnp.concatenate(rows, axis=0), ones, preferred_element_type=F32)


def gather(left, right, count):
    span = right.shape[0]
    lanes = lax.broadcasted_iota(jnp.int32, (count, span), 1)
    wide = contract(left[...], right, 1, 1)
    totals = [jnp.zeros((count, span), F32)] * 4
    for t in range(span):
        totals[t % 4] = jnp.where(lanes == t, wide[t * count : (t + 1) * count, :], totals[t % 4])
    return (totals[0] + totals[1]) + (totals[2] + totals[3])


def sigmoid_of_softplus(step):
    series = step * (1.0 - step * (0.5 - step * (1.0 / 6.0 - step * (1.0 / 24.0))))
    return jnp.where(step < 0.05, series, 1.0 - jnp.exp(-step))


def fold(pend, out, start, half):
    for g in range(pend.shape[0]):
        total = pend[g, pl.ds(half * GROUP * GROUP, GROUP, stride=GROUP), :]
        for s in range(1, GROUP):
            total = total + pend[g, pl.ds(half * GROUP * GROUP + s, GROUP, stride=GROUP), :]
        out[pl.ds(start, GROUP), g * LANES : (g + 1) * LANES] = total


def fwd_kernel(parts, ids, lens, *refs):
    projs, refs = refs[:parts], refs[parts:]
    w_out, u_act, gate, dt_w, dt_b, a_log, skip = refs[:7]
    refs = refs[7:]
    dt, y_rows, gated, edge, low_state, vectors, own = refs[:7]
    sends, refs = refs[7 : 6 + parts], refs[6 + parts :]
    dtu, y, pend, carry = refs
    span, chans = dtu.shape
    nstate = a_log.shape[0]
    rank = dt_w.shape[0]
    block = pl.program_id(1)
    groups = chans // LANES

    @pl.when(block == 0)
    def _():
        carry[...] = jnp.zeros(carry.shape, F32)

    proj = projs[0][0]
    for other in projs[1:]:
        proj = proj + other[0].astype(F32)
    lin = contract(proj[:rank].astype(BF16), dt_w[...], 0, 0) + dt_b[...]
    step = softplus(lin)
    dt[0] = step
    dtu[...] = step * u_act[0]
    spread(proj[rank : rank + nstate], proj[rank + nstate :], vectors.at[0])
    rate = -jnp.exp(a_log[...])
    lane = [slice(g * LANES, (g + 1) * LANES) for g in range(groups)]

    edge[0, 0] = carry[...]

    def steps(i, state):
        state = list(state)
        for half in range(2):
            start = pl.multiple_of((2 * i + half) * GROUP, GROUP)
            dt_rows = dt[0, pl.ds(start, GROUP), :]
            dtu_rows = dtu[pl.ds(start, GROUP), :]
            for k in range(GROUP):
                at = pl.ds(pl.multiple_of((start + k) * nstate, nstate), nstate)
                b_t = vectors[0, at, :LANES]
                c_t = vectors[0, at, LANES:]
                rows = pl.ds((half * GROUP + k) * GROUP, GROUP)
                for g in range(groups):
                    dt_t = dt_rows[k : k + 1, lane[g]]
                    dtu_t = dtu_rows[k : k + 1, lane[g]]
                    new = jnp.exp(dt_t * rate[:, lane[g]]) * state[g] + dtu_t * b_t
                    state[g] = new
                    low_state[0, at, lane[g]] = new.astype(BF16)
                    term = c_t * new
                    pend[g, rows, :] = sum(term[s : s + GROUP] for s in range(0, nstate, GROUP))
            fold(pend, y, start, half)
        return tuple(state)

    last = lax.fori_loop(0, span // (2 * GROUP), steps, tuple(carry[:, l] for l in lane))
    for g in range(groups):
        carry[:, lane[g]] = last[g]
    rows = y[...] + skip[...] * u_act[0]
    y_rows[0] = rows
    gate_in = gate[0]
    position = block * span + lax.broadcasted_iota(jnp.int32, (span, 1), 0)
    live = (position < lens[pl.program_id(0)]).astype(F32)
    low = (rows * (gate_in * sigmoid(gate_in)) * live).astype(BF16)
    gated[0] = low
    quarter = own.shape[2]
    for k in range(parts):
        rows = pl.ds(pl.multiple_of((ids[0] ^ k) * quarter, LANES), quarter)
        term = contract(low, w_out[rows, :], 1, 1)
        if k == 0:
            own[0] = term
        else:
            sends[k - 1][0] = term.astype(BF16)


def bwd_kernel(parts, ids, lens, *refs):
    projs, refs = refs[:parts], refs[parts:]
    cots, refs = refs[:parts], refs[parts:]
    w_full, u_act, gate, dt, y_rows, edge, low_state, vectors, dt_w, a_log, skip = refs[:11]
    refs = refs[11:]
    cot_full, d_proj, d_proj_low, d_scan, d_gate, small, small_theirs = refs[:7]
    dtu, d_y, d_dtu, d_dta, pend_q, pend_r, carry, g_rate, low_grad = refs[7:]
    span, chans = dtu.shape
    nstate = a_log.shape[0]
    rank = dt_w.shape[0]
    first = (pl.program_id(0) == 0) & (pl.program_id(1) == 0)
    last = (pl.program_id(0) == pl.num_programs(0) - 1) & (pl.program_id(1) == pl.num_programs(1) - 1)
    block = pl.num_programs(1) - 1 - pl.program_id(1)
    groups = chans // LANES
    quarter = cots[0].shape[2]
    lane = [slice(g * LANES, (g + 1) * LANES) for g in range(groups)]

    @pl.when(first)
    def _():
        small[...] = jnp.zeros(small.shape, F32)
        g_rate[...] = jnp.zeros(g_rate.shape, F32)

    @pl.when(pl.program_id(1) == 0)
    def _():
        carry[...] = jnp.zeros(carry.shape, F32)

    for k, cot in enumerate(cots):
        cols = pl.ds(pl.multiple_of((ids[0] ^ k) * quarter, LANES), quarter)
        cot_full[0, :, cols] = cot[0]
    d_gated = jnp.dot(cot_full[0], w_full[...], preferred_element_type=F32)

    proj = projs[0][0]
    for other in projs[1:]:
        proj = proj + other[0].astype(F32)
    dt_low = proj[:rank].astype(BF16)
    u = u_act[0]
    step = dt[0]
    dtu[...] = step * u
    gate_in = gate[0]
    gate_sig = sigmoid(gate_in)
    position = block * span + lax.broadcasted_iota(jnp.int32, (span, 1), 0)
    live = (position < lens[pl.program_id(0)]).astype(F32)
    d_live = d_gated * live
    d_rows = d_live * (gate_in * gate_sig)
    d_y[...] = d_rows
    d_gate[0] = (d_live * y_rows[0] * (gate_sig * (1.0 + gate_in * (1.0 - gate_sig)))).astype(BF16)
    rate = -jnp.exp(a_log[...])
    count = span // (2 * GROUP)

    def steps(i, loop):
        run, acc = list(loop[0]), list(loop[1])
        for half in reversed(range(2)):
            start = pl.multiple_of((2 * (count - 1 - i) + half) * GROUP, GROUP)
            dt_rows = dt[0, pl.ds(start, GROUP), :]
            dy_rows = d_y[pl.ds(start, GROUP), :]
            for k in reversed(range(GROUP)):
                at = pl.ds(pl.multiple_of((start + k) * nstate, nstate), nstate)
                b_t = vectors[0, at, :LANES]
                c_t = vectors[0, at, LANES:]
                rows = pl.ds((half * GROUP + k) * GROUP, GROUP)
                before = start + k - 1
                if half == 0 and k == 0:
                    before = jnp.maximum(before, 0)
                before = pl.ds(pl.multiple_of(before * nstate, nstate), nstate)
                for g in range(groups):
                    old = low_state[0, before, lane[g]].astype(F32)
                    if half == 0 and k == 0:
                        old = jnp.where(start == 0, edge[0, 0, :, lane[g]], old)
                    dt_t = dt_rows[k : k + 1, lane[g]]
                    dy_t = dy_rows[k : k + 1, lane[g]]
                    d_state = run[g] + c_t * dy_t
                    low_grad[at, lane[g]] = d_state.astype(BF16)
                    decayed = jnp.exp(dt_t * rate[:, lane[g]]) * d_state
                    run[g] = decayed
                    d_exp = decayed * old
                    acc[g] = acc[g] + d_exp * dt_t
                    term_q = d_exp * rate[:, lane[g]]
                    term_r = d_state * b_t
                    pend_q[g, rows, :] = sum(term_q[s : s + GROUP] for s in range(0, nstate, GROUP))
                    pend_r[g, rows, :] = sum(term_r[s : s + GROUP] for s in range(0, nstate, GROUP))
            fold(pend_q, d_dta, start, half)
            fold(pend_r, d_dtu, start, half)
        return tuple(run), tuple(acc)

    run, acc = lax.fori_loop(
        0,
        count,
        steps,
        (tuple(carry[:, l] for l in lane), tuple(g_rate[:, l] for l in lane)),
    )
    d_b = gather(low_grad, dtu[...].astype(BF16), nstate)
    d_c = gather(low_state.at[0], d_rows.astype(BF16), nstate)
    for g in range(groups):
        carry[:, lane[g]] = run[g]
        g_rate[:, lane[g]] = acc[g]
    d_lin = (d_dtu[...] * u + d_dta[...]) * sigmoid_of_softplus(step)
    d_scan[0] = d_dtu[...] * step + d_rows * skip[...]
    d_low = d_lin.astype(BF16)
    full = jnp.concatenate([contract(dt_w[...], d_low, 1, 1), d_b, d_c], axis=0)
    d_proj[0] = full
    d_proj_low[0] = full.astype(BF16)
    small[:rank, :] += jnp.dot(dt_low, d_low, preferred_element_type=F32)
    row = rank + nstate
    small[row : row + 1, :] += jnp.sum(d_lin, axis=0, keepdims=True)
    small[row + 1 : row + 2, :] += jnp.sum(d_rows * u, axis=0, keepdims=True)

    @pl.when(last)
    def _():
        small[rank : rank + nstate, :] = g_rate[...] * rate
        small_theirs[...] = small[:, core_half(ids, chans, 1)]


def post_kernel(parts, ids, *refs):
    projs, refs = refs[:parts], refs[parts:]
    xs, refs = refs[:parts], refs[parts:]
    d_scan, d_gate, u_act, summed, inner, inv, w_full, gain, xw_t, conv_w = refs[:10]
    refs = refs[10:]
    d_inner_low, small, small_theirs, tiny, own = refs[:5]
    sends, refs = refs[5 : 4 + parts], refs[4 + parts :]
    padded, front, d_both = refs
    tokens, chans = d_scan.shape[1:]
    quarter = own.shape[2]
    taps = conv_w.shape[0]
    m = pl.program_id(0)

    @pl.when(m == 0)
    def _():
        padded[tokens:, :] = jnp.zeros((GROUP, chans), F32)
        front[:GROUP, :] = jnp.zeros((GROUP, chans), F32)
        small[...] = jnp.zeros(small.shape, F32)
        tiny[...] = jnp.zeros(tiny.shape, F32)

    proj = projs[0][0]
    for other in projs[1:]:
        proj = proj + other[0].astype(F32)
    d_proj = proj.astype(BF16)
    count = d_proj.shape[0]
    d_u = d_scan[0] + contract(d_proj, xw_t[...], 0, 0)
    small[:count, :] += jnp.dot(d_proj, u_act[0].astype(BF16), preferred_element_type=F32)
    conv = summed[0]
    sig = sigmoid(conv)
    d_conv = d_u * (sig * (1.0 + conv * (1.0 - sig)))
    padded[:tokens, :] = d_conv
    front[GROUP:, :] = inner[0]
    d_inner = 0.0
    for j in range(taps):
        d_inner = d_inner + conv_w[j : j + 1, :] * padded[pl.ds(taps - 1 - j, tokens), :]
        small[count + j : count + j + 1, :] += jnp.sum(
            d_conv * front[pl.ds(GROUP - taps + 1 + j, tokens), :], axis=0, keepdims=True
        )
    small[count + taps : count + taps + 1, :] += jnp.sum(d_conv, axis=0, keepdims=True)

    @pl.when(m == pl.num_programs(0) - 1)
    def _():
        small_theirs[...] = small[:, core_half(ids, chans, 1)]

    d_inner_low[0] = d_inner.astype(BF16)
    d_both[:, :chans] = d_inner.astype(BF16)
    d_both[:, chans:] = d_gate[0]
    scale = inv[0][:, :1]
    dots = 0.0
    for k in range(parts):
        cols = pl.ds(pl.multiple_of((ids[0] ^ k) * quarter, LANES), quarter)
        d_norm = contract(d_both[...], w_full[cols, :], 1, 1)
        if k == 0:
            own[0] = d_norm
        else:
            sends[k - 1][0] = d_norm.astype(BF16)
        along = d_norm * xs[k][0].astype(F32)
        tiny[0:1, cols] += jnp.sum(along * scale, axis=0, keepdims=True)
        weighted = along * gain[:, cols]
        for c in range(0, quarter, LANES):
            dots = dots + weighted[:, c : c + LANES]
    dots = jnp.sum(jnp.transpose(dots), axis=0, keepdims=True)
    tiny[1:2, pl.ds(pl.multiple_of(m * tokens, LANES), tokens)] = dots


def grad_kernel(chips, pairs, ids, *refs):
    lefts, rights, (mine, theirs) = refs[:pairs], refs[pairs : 2 * pairs], refs[2 * pairs :]
    wide = rights[0].shape[1]
    for p, (left, right) in enumerate(zip(lefts, rights)):
        at = slice(p * wide, (p + 1) * wide)
        if chips == 0:
            mine[:, at] = contract(left[...], right[...], 0, 0)
            continue
        rows = mine.shape[1]
        for side, out in enumerate((theirs, mine)):
            for j in range(chips):
                index = (ids[1] ^ (2 * j)) ^ (1 - side)
                cols = pl.ds(pl.multiple_of(index * rows, LANES), rows)
                out[j, :, at] = contract(left[:, cols], right[...], 0, 0).astype(out.dtype)


def merge_kernel(step, row, ids, mine, got, small, small_got, *refs):
    tinies, (own, part, *sends) = (refs[:2], refs[2:]) if row else ((), refs)
    rows = mine.shape[1]
    chans = small.shape[1]
    half = chans // 2
    part[...] = small[:, core_half(ids, chans)] + small_got[...]
    if row:
        for i in range(tinies[0].shape[1] // chans):
            cols = pl.ds(pl.multiple_of((ids[1] & 1) * half, LANES) + i * chans, half)
            part[row + i : row + i + 1, :] = tinies[0][0:1, cols] + tinies[1][0:1, cols]
    own[...] = mine[0] + got[0].astype(F32)
    pieces = part.shape[0] // step
    for j, send in enumerate(sends):
        send[:rows, :] = (mine[j + 1] + got[j + 1].astype(F32)).astype(BF16)
        for c in range(pieces):
            send[rows:, c * half : (c + 1) * half] = part[c * step : (c + 1) * step, :].astype(BF16)
        if pieces * half < send.shape[1]:
            send[rows:, pieces * half :] = jnp.zeros((step, send.shape[1] - pieces * half), BF16)


def add_received(step, own, part, gots, half):
    rows = own.shape[0]
    total = own[...]
    for got in gots:
        total = total + got[:rows, :].astype(F32)
    lanes = part.shape[1]
    for c in range(part.shape[0] // step):
        piece = part[c * step : (c + 1) * step, :]
        for got in gots:
            piece = piece + got[rows:, c * lanes : (c + 1) * lanes].astype(F32)
        half[c * step : (c + 1) * step, :] = piece
    return total


def final_early_kernel(step, own, part, *refs):
    gots, (grad_gate, grad_out, half) = refs[:-3], refs[-3:]
    total = add_received(step, own, part, gots, half)
    wide = grad_gate.shape[1]
    grad_gate[...] = total[:, :wide]
    grad_out[...] = jnp.transpose(total[:, wide:])


def final_late_kernel(step, own, part, grad_gate, *refs):
    gots, (grad_in, half) = refs[:-2], refs[-2:]
    grad_in[:, 0, :] = add_received(step, own, part, gots, half)
    grad_in[:, 1, :] = grad_gate[...]


def outputs_kernel(
    ids, scan_half, scan_got, post_half, post_got, gain, x_w, dt_w, dt_b, conv_w, conv_b, a_log, skip, scan, post
):
    chans = scan.shape[1]
    for full, half, got in ((scan, scan_half, scan_got), (post, post_half, post_got)):
        full[:, core_half(ids, chans)] = half[...]
        full[:, core_half(ids, chans, 1)] = got[...]
    rank = dt_w.shape[0]
    nstate = a_log.shape[0]
    count = x_w.shape[0]
    taps = conv_w.shape[0]
    dt_w[...] = scan[:rank, :]
    a_log[...] = scan[rank : rank + nstate, :]
    dt_b[...] = scan[rank + nstate : rank + nstate + 1, :]
    skip[...] = scan[rank + nstate + 1 : rank + nstate + 2, :]
    x_w[...] = post[:count, :]
    conv_w[...] = post[count : count + taps, :]
    conv_b[...] = post[count + taps : count + taps + 1, :]
    for i in range(gain.shape[1] // chans):
        row = count + taps + 1 + i
        gain[:, i * chans : (i + 1) * chans] = post[row : row + 1, :]


def whole(shape):
    return pl.BlockSpec(shape, lambda *_: (0,) * len(shape))


SMEM = pl.BlockSpec(memory_space=pltpu.SMEM)


def params(grid, mib=56):
    return pltpu.CompilerParams(
        dimension_semantics=("arbitrary",) * grid, vmem_limit_bytes=mib * 1024 * 1024
    )


def cost(micros):
    return pl.CostEstimate(flops=int(micros * 1.15e9), bytes_accessed=0, transcendentals=0)


def struct(shape, dtype):
    return jax.ShapeDtypeStruct(shape, dtype)


def run_pre(ids, xs, ws, gain, conv_w, conv_b, xw_t):
    micro, tokens, quarter = xs[0].shape
    width = gain.shape[1]
    chans = conv_w.shape[1]
    count = xw_t.shape[0]
    per = lambda *tail: pl.BlockSpec((1,) + tail, lambda m: (m,) + (0,) * len(tail))
    return pl.pallas_call(
        partial(pre_kernel, len(xs), len(ws)),
        grid=(micro,),
        in_specs=[SMEM]
        + [per(tokens, quarter)] * len(xs)
        + [whole(w.shape) for w in ws]
        + [whole(gain.shape), whole(conv_w.shape), whole(conv_b.shape), whole(xw_t.shape)],
        out_specs=[
            per(tokens, width),
            whole((width, ws[0].shape[1])),
            per(tokens, chans),
            per(tokens, chans),
            per(tokens, chans),
            per(tokens, chans),
            per(tokens, LANES),
            per(count, tokens),
            per(count, tokens),
        ],
        out_shape=[
            struct((micro, tokens, width), BF16),
            struct((width, ws[0].shape[1]), BF16),
            struct((micro, tokens, chans), F32),
            struct((micro, tokens, chans), F32),
            struct((micro, tokens, chans), F32),
            struct((micro, tokens, chans), F32),
            struct((micro, tokens, LANES), F32),
            struct((micro, count, tokens), F32),
            struct((micro, count, tokens), BF16),
        ],
        scratch_shapes=[pltpu.VMEM((tokens + GROUP, chans), F32)],
        compiler_params=params(1),
        cost_estimate=cost(7),
        name="pre",
    )(ids, *xs, *ws, gain, conv_w, conv_b, xw_t)


def run_fwd(ids, lens, projs, w_full, u_act, gate, dt_w, dt_b, a_log, skip):
    micro, tokens, chans = u_act.shape
    parts = len(projs)
    width = w_full.shape[0]
    quarter = width // parts
    count = projs[0].shape[1]
    nstate = a_log.shape[0]
    span = min(LANES, tokens)
    rows = lambda *tail: pl.BlockSpec((1, span) + tail, lambda m, b: (m, b) + (0,) * len(tail))
    return pl.pallas_call(
        partial(fwd_kernel, parts),
        grid=(micro, tokens // span),
        in_specs=[SMEM, SMEM]
        + [pl.BlockSpec((1, count, span), lambda m, b: (m, 0, b))] * parts
        + [pl.BlockSpec((width, chans), lambda m, b: (0, 2)), rows(chans), rows(chans)]
        + [whole(v.shape) for v in (dt_w, dt_b, a_log, skip)],
        out_specs=[
            rows(chans),
            rows(chans),
            rows(chans),
            pl.BlockSpec((1, 1, nstate, chans), lambda m, b: (m, b, 0, 0)),
            pl.BlockSpec((1, span * nstate, chans), lambda m, b: (m, b, 0)),
            pl.BlockSpec((1, span * nstate, 2 * LANES), lambda m, b: (m, b, 0)),
        ]
        + [rows(quarter)] * parts,
        out_shape=[
            struct((micro, tokens, chans), F32),
            struct((micro, tokens, chans), F32),
            struct((micro, tokens, chans), BF16),
            struct((micro, tokens // span, nstate, chans), F32),
            struct((micro, tokens * nstate, chans), BF16),
            struct((micro, tokens * nstate, 2 * LANES), F32),
            struct((micro, tokens, quarter), F32),
        ]
        + [struct((micro, tokens, quarter), BF16)] * (parts - 1),
        scratch_shapes=[pltpu.VMEM((span, chans), F32)] * 2
        + [pltpu.VMEM((chans // LANES, 2 * GROUP * GROUP, LANES), F32), pltpu.VMEM((nstate, chans), F32)],
        compiler_params=params(2),
        cost_estimate=cost(16),
        name="scan_forward",
    )(ids, lens, *projs, w_full, u_act, gate, dt_w, dt_b, a_log, skip)


def run_bwd(ids, lens, projs, cots, w_full, u_act, gate, dt, y_rows, edge, low_state, vectors, dt_w, a_log, skip):
    micro, tokens, chans = u_act.shape
    parts = len(projs)
    width = w_full.shape[0]
    quarter = cots[0].shape[2]
    count = projs[0].shape[1]
    nstate = a_log.shape[0]
    rank = dt_w.shape[0]
    span = min(LANES, tokens)
    blocks = tokens // span
    small = SCAN_STEP * -(-(rank + nstate + 2) // SCAN_STEP)
    rows = lambda *tail: pl.BlockSpec(
        (1, span) + tail, lambda m, b: (m, blocks - 1 - b) + (0,) * len(tail)
    )
    proj = pl.BlockSpec((1, count, span), lambda m, b: (m, 0, blocks - 1 - b))
    return pl.pallas_call(
        partial(bwd_kernel, parts),
        grid=(micro, blocks),
        in_specs=[SMEM, SMEM]
        + [proj] * parts
        + [rows(quarter)] * parts
        + [pl.BlockSpec((width, chans), lambda m, b: (0, 2)), rows(chans), rows(chans), rows(chans), rows(chans)]
        + [pl.BlockSpec((1, 1, nstate, chans), lambda m, b: (m, blocks - 1 - b, 0, 0))]
        + [pl.BlockSpec((1, span * nstate, chans), lambda m, b: (m, blocks - 1 - b, 0))]
        + [pl.BlockSpec((1, span * nstate, 2 * LANES), lambda m, b: (m, blocks - 1 - b, 0))]
        + [whole(v.shape) for v in (dt_w, a_log, skip)],
        out_specs=[rows(width), proj, proj, rows(chans), rows(chans), whole((small, chans)), whole((small, chans // 2))],
        out_shape=[
            struct((micro, tokens, width), BF16),
            struct((micro, count, tokens), F32),
            struct((micro, count, tokens), BF16),
            struct((micro, tokens, chans), F32),
            struct((micro, tokens, chans), BF16),
            struct((small, chans), F32),
            struct((small, chans // 2), F32),
        ],
        scratch_shapes=[pltpu.VMEM((span, chans), F32)] * 4
        + [pltpu.VMEM((chans // LANES, 2 * GROUP * GROUP, LANES), F32)] * 2
        + [pltpu.VMEM((nstate, chans), F32)] * 2
        + [pltpu.VMEM((span * nstate, chans), BF16)],
        compiler_params=params(2),
        cost_estimate=cost(21),
        name="scan_backward",
    )(ids, lens, *projs, *cots, w_full, u_act, gate, dt, y_rows, edge, low_state, vectors, dt_w, a_log, skip)


def run_post(ids, projs, xs, d_scan, d_gate, u_act, summed, inner, inv, w_full, gain, xw_t, conv_w):
    micro, tokens, chans = u_act.shape
    parts = len(projs)
    width = w_full.shape[0]
    quarter = width // parts
    count = projs[0].shape[1]
    taps = conv_w.shape[0]
    small = POST_STEP * -(-(count + taps + 1 + width // chans) // POST_STEP)
    lanes = max(width, LANES * -(-micro * tokens // LANES))
    per = lambda *tail: pl.BlockSpec((1,) + tail, lambda m: (m,) + (0,) * len(tail))
    return pl.pallas_call(
        partial(post_kernel, parts),
        grid=(micro,),
        in_specs=[SMEM]
        + [per(count, tokens)] * parts
        + [per(tokens, quarter)] * parts
        + [per(tokens, chans)] * 5
        + [per(tokens, LANES)]
        + [whole((width, 2 * chans))]
        + [whole(v.shape) for v in (gain, xw_t, conv_w)],
        out_specs=[
            per(tokens, chans),
            whole((small, chans)),
            whole((small, chans // 2)),
            whole((GROUP, lanes)),
        ]
        + [per(tokens, quarter)] * parts,
        out_shape=[
            struct((micro, tokens, chans), BF16),
            struct((small, chans), F32),
            struct((small, chans // 2), F32),
            struct((GROUP, lanes), F32),
            struct((micro, tokens, quarter), F32),
        ]
        + [struct((micro, tokens, quarter), BF16)] * (parts - 1),
        scratch_shapes=[pltpu.VMEM((tokens + GROUP, chans), F32)] * 2
        + [pltpu.VMEM((tokens, 2 * chans), BF16)],
        compiler_params=params(1),
        cost_estimate=cost(8),
        name="post",
    )(ids, *projs, *xs, d_scan, d_gate, u_act, summed, inner, inv, w_full, gain, xw_t, conv_w)


def run_grad(name, ids, lefts, rights, shape, chips):
    if chips == 0:
        outs = [struct(shape, F32), struct((GROUP, LANES), BF16)]
    else:
        outs = [struct((chips,) + shape, F32), struct((chips,) + shape, BF16)]
    flat = lambda v: v.reshape(-1, v.shape[-1])
    return run_local(
        partial(grad_kernel, chips, len(lefts)), name, outs, ids, *map(flat, lefts), *map(flat, rights)
    )


VMEM = pl.BlockSpec(memory_space=pltpu.VMEM)


def run_local(kernel, name, outs, ids, *operands, scratch=()):
    return pl.pallas_call(
        kernel,
        in_specs=([SMEM] if ids is not None else []) + [VMEM] * len(operands),
        out_specs=[VMEM] * len(outs),
        out_shape=outs,
        scratch_shapes=list(scratch),
        compiler_params=pltpu.CompilerParams(vmem_limit_bytes=56 * 1024 * 1024),
        cost_estimate=cost(3),
        name=name,
    )(*(() if ids is None else (ids,)), *operands)


def after(value, *earlier):
    return lax.optimization_barrier((value, earlier))[0]


def others(value, axis, step=1):
    count = lax.axis_size(axis)
    return [swap(value, axis, mask) for mask in range(step, count, step)]


def gather_line(value, axis, early=()):
    count = lax.axis_size(axis)
    got = {0: value}
    mask = count // 2
    while mask:
        for known in sorted(got):
            fresh = swap(got[known], axis, mask) if known or mask not in early else early[mask]
            got[known | mask] = fresh
        mask //= 2
    return [got[k] for k in range(count)]


def with_sibling(blocks):
    return blocks + [swap(block, "dp", 1) for block in blocks]


def sum_all(value):
    core = lax.rem(lax.axis_index("dp"), 2)
    half = value.shape[0] // 2
    halves = value.reshape((2, half) + value.shape[1:])
    mine = lax.dynamic_index_in_dim(halves, core, 0, keepdims=False)
    theirs = lax.dynamic_index_in_dim(halves, 1 - core, 0, keepdims=False)
    total = mine + swap(theirs, "dp", 1)
    for got in others(total, "dp", 2):
        total = total + got
    other = swap(total, "dp", 1)
    first = jnp.where(core == 0, total, other)
    second = jnp.where(core == 0, other, total)
    return jnp.concatenate([first, second], axis=0)


def body(
    tokens,
    lengths,
    norm_gain,
    in_weight,
    x_weight,
    dt_weight,
    dt_bias,
    conv_weight,
    conv_bias,
    a_log,
    skip,
    out_weight,
    cotangent,
):
    micro, seq, quarter = tokens.shape
    chans = in_weight.shape[2]
    width = norm_gain.shape[0]
    dps = lax.axis_size("dp")
    rank = dt_weight.shape[0]
    nstate = a_log.shape[0]
    taps = conv_weight.shape[0]
    count = x_weight.shape[1]
    ids = jnp.stack([lax.axis_index("tensor"), lax.axis_index("dp")]).astype(jnp.int32)
    lens = lengths[:, 0]
    gain = norm_gain[None]
    xw_t = x_weight.T
    in_rows = in_weight.reshape(in_weight.shape[0], 2 * chans)
    by_block = in_rows.shape[0] % LANES == 0
    chips = dps // 2 if by_block else 0
    parts = lax.axis_size("tensor")
    weight = jnp.concatenate([in_rows, out_weight.T], axis=1)

    xs = gather_line(tokens, "tensor")
    if by_block:
        mine = [weight] + [
            swap(weight, "dp", mask) for mask in range(2, dps, 2)
        ]
        blocks = with_sibling(after(mine, *xs))
    else:
        blocks = [lax.all_gather(weight, "dp", axis=0, tiled=True)]
    normed, w_full, inner, summed, u_act, gate, inv, proj, proj_low = run_pre(
        ids, xs, blocks, gain, conv_weight, conv_bias[None], xw_t
    )
    cot_early = after(cotangent, *xs)
    early = {mask: swap(cot_early, "tensor", mask) for mask in (parts // 2, 1)}
    projs = [proj] + others(proj_low, "tensor")
    far = after(early[parts // 2], *projs)
    early[parts // 2] = far
    cots = gather_line(cotangent, "tensor", early)
    dt, y_rows, gated, edge, low_state, vectors, own_out, *out_terms = run_fwd(
        ids, lens, projs, w_full, u_act, gate, dt_weight, dt_bias[None], a_log, skip[None]
    )
    out_got = [swap(term, "tensor", k + 1) for k, term in enumerate(out_terms)]
    cot_full, d_proj, d_proj_low, d_scan, d_gate, scan_small, scan_theirs = run_bwd(
        ids, lens, projs, cots, w_full, u_act, gate, dt, y_rows, edge, low_state, vectors, dt_weight, a_log, skip[None]
    )
    d_projs = [d_proj] + others(after(d_proj_low, *out_got), "tensor")
    branch = own_out
    for term in out_got:
        branch = branch + term.astype(F32)
    mixed = (tokens.astype(F32) + branch).astype(BF16)
    rows = weight.shape[0] if chips else width
    early_mine, early_theirs = run_grad(
        "grad_early",
        ids,
        [after(normed, d_projs), cot_full],
        [d_gate, gated],
        (rows, 2 * chans),
        chips,
    )

    def merged(name, step, row, mine, theirs, small, small_theirs, tinies, wide):
        part = struct((small.shape[0], chans // 2), F32)
        own, part, *sends = run_local(
            partial(merge_kernel, step, row),
            name,
            [struct((rows, wide), F32), part] + [struct((rows + step, wide), BF16)] * (chips - 1),
            ids,
            mine,
            swap(theirs, "dp", 1),
            small,
            swap(small_theirs, "dp", 1),
            *tinies,
        )
        return own, part, sends

    if chips:
        early_own, early_part, sends = merged(
            "merge_early", SCAN_STEP, 0, early_mine, early_theirs, scan_small, scan_theirs, (), 2 * chans
        )
        early_gots = [swap(send, "dp", 2 * (j + 1)) for j, send in enumerate(sends)]
    d_inner, small, small_theirs, tiny, own_norm, *norm_terms = run_post(
        ids, d_projs, xs, d_scan, d_gate, u_act, summed, inner, inv, w_full, gain, xw_t, conv_weight
    )
    tiny_got = others(tiny, "tensor")
    near = parts // 2
    halves = [own_norm] + norm_terms
    passed = [swap(halves[k], "tensor", k) for k in range(1, near)]
    relayed = [swap(halves[near + k], "tensor", k) for k in range(1, near)]
    far = halves[near].astype(F32)
    for got in relayed:
        far = far + got.astype(F32)
    far = far.astype(BF16)
    norm_got = passed + [swap(far, "tensor", near)]
    late_mine, late_theirs = run_grad("grad_late", ids, [normed], [d_inner], (rows, chans), chips)
    for got in tiny_got:
        tiny = tiny + got
    row = count + taps + 1
    if chips:
        late_own, late_part, sends = merged(
            "merge_late",
            POST_STEP,
            row,
            after(late_mine, far),
            late_theirs,
            small,
            small_theirs,
            (tiny, swap(tiny, "dp", 1)),
            chans,
        )
        late_gots = [swap(send, "dp", 2 * (j + 1)) for j, send in enumerate(sends)]
        grad_gate, grad_out, scan_half = run_local(
            partial(final_early_kernel, SCAN_STEP),
            "final_early",
            [struct((rows, chans), F32), struct(out_weight.shape, F32), struct(early_part.shape, F32)],
            None,
            early_own,
            early_part,
            *early_gots,
        )
        grad_in, post_half = run_local(
            partial(final_late_kernel, POST_STEP),
            "final_late",
            [struct(in_weight.shape, F32), struct(late_part.shape, F32)],
            None,
            late_own,
            late_part,
            grad_gate,
            *late_gots,
        )
        g_gain, g_x, g_dt, g_dtb, g_conv, g_convb, g_alog, g_skip = run_local(
            outputs_kernel,
            "outputs",
            [
                struct((1, width), F32),
                struct((count, chans), F32),
                struct((rank, chans), F32),
                struct((1, chans), F32),
                struct((taps, chans), F32),
                struct((1, chans), F32),
                struct((nstate, chans), F32),
                struct((1, chans), F32),
            ],
            ids,
            scan_half,
            swap(scan_half, "dp", 1),
            post_half,
            swap(post_half, "dp", 1),
            scratch=[pltpu.VMEM((scan_small.shape[0], chans), F32), pltpu.VMEM((small.shape[0], chans), F32)],
        )
        smalls = (g_gain[0], g_x.T, g_dt, g_dtb[0], g_conv, g_convb[0], g_alog, g_skip[0])
    else:
        grad_inner = lax.psum_scatter(late_mine, "dp", scatter_dimension=0, tiled=True)
        early = lax.psum_scatter(early_mine, "dp", scatter_dimension=0, tiled=True)
        grad_in = jnp.stack([grad_inner, early[:, :chans]], axis=1)
        grad_out = early[:, chans:].T
        scan_small = sum_all(scan_small)
        small = sum_all(lax.dynamic_update_slice_in_dim(small, tiny[0, :width].reshape(-1, chans), row, 0))
        smalls = (
            small[row : row + width // chans].reshape(width),
            small[:count].T,
            scan_small[:rank],
            scan_small[rank + nstate],
            small[count : count + taps],
            small[count + taps],
            scan_small[rank : rank + nstate],
            scan_small[rank + nstate + 1],
        )
    d_norm = own_norm
    for term in norm_got:
        d_norm = d_norm + term.astype(F32)
    scale = inv[:, :, :1]
    dots = tiny[1, : micro * seq].reshape(micro, seq, 1)
    own_gain = lax.dynamic_slice_in_dim(norm_gain, ids[0] * quarter, quarter, 0)
    d_x = scale * (d_norm * own_gain) - tokens.astype(F32) * (scale * scale * scale * dots / width)
    input_grad = cotangent.astype(F32) + d_x
    return (mixed, input_grad, smalls[0], grad_in.reshape(in_weight.shape)) + smalls[1:] + (grad_out,)


def solution(mesh):
    rows = P(None, "dp", "tensor")
    chans = P(None, "tensor")
    return jax.shard_map(
        body,
        mesh=mesh,
        in_specs=(
            rows,
            P(None, "dp"),
            P(),
            P("dp", None, "tensor"),
            P("tensor", None),
            chans,
            P("tensor"),
            chans,
            P("tensor"),
            chans,
            P("tensor"),
            P("tensor", "dp"),
            rows,
        ),
        out_specs=(
            rows,
            rows,
            P(),
            P("dp", None, "tensor"),
            P("tensor", None),
            chans,
            P("tensor"),
            chans,
            P("tensor"),
            chans,
            P("tensor"),
            P("tensor", "dp"),
        ),
        check_vma=False,
    )
```

```python
from functools import partial

import jax
import jax.numpy as jnp
from jax import lax
from jax.experimental import pallas as pl
from jax.experimental.pallas import tpu as pltpu
from jax.sharding import PartitionSpec as P

EPS = 1e-05
F32 = jnp.float32
BF16 = jnp.bfloat16
GROUP = 8
LANES = 128
SCAN_STEP = 32
POST_STEP = 64


def contract(left, right, left_dim, right_dim):
    return lax.dot_general(
        left, right, (((left_dim,), (right_dim,)), ((), ())), preferred_element_type=F32
    )


def sigmoid(v):
    return 1.0 / (1.0 + jnp.exp(-v))


def softplus(v):
    return jnp.maximum(v, 0.0) + jnp.log1p(jnp.exp(-jnp.abs(v)))


def swap(value, axis, mask):
    count = lax.axis_size(axis)
    return lax.ppermute(value, axis, [(i, i ^ mask) for i in range(count)])


def pre_kernel(parts, blocks, ids, *refs):
    xs, refs = refs[:parts], refs[parts:]
    ws, refs = refs[:blocks], refs[blocks:]
    gain, conv_w, conv_b, xw_t = refs[:4]
    normed, w_full, inner, summed, u_act, gate, inv, proj, proj_low, padded = refs[4:]
    quarter = xs[0].shape[2]
    chans = inner.shape[2]

    @pl.when(pl.program_id(0) == 0)
    def _():
        gather_rows(ids, ws, w_full)
        padded[:GROUP, :] = jnp.zeros((GROUP, chans), F32)

    square = 0.0
    for x in xs:
        rows = x[0].astype(F32)
        square = square + jnp.sum(rows * rows, axis=1, keepdims=True)
    scale = lax.rsqrt(square / (parts * quarter) + EPS)
    inv[0] = jnp.broadcast_to(scale, inv.shape[1:])
    for k, x in enumerate(xs):
        cols = pl.ds(pl.multiple_of((ids[0] ^ k) * quarter, LANES), quarter)
        normed[0, :, cols] = (x[0].astype(F32) * scale * gain[:, cols]).astype(BF16)
    both = jnp.dot(normed[0], w_full[:, : 2 * chans], preferred_element_type=F32)
    gate[0] = both[:, chans:]
    inner_in = both[:, :chans]
    inner[0] = inner_in
    tokens = inner_in.shape[0]
    padded[GROUP:, :] = inner_in
    taps = conv_w.shape[0]
    total = jnp.broadcast_to(conv_b[...], inner_in.shape)
    for j in range(taps):
        total = total + conv_w[j : j + 1, :] * padded[pl.ds(GROUP - taps + 1 + j, tokens), :]
    summed[0] = total
    act = total * sigmoid(total)
    u_act[0] = act
    partial_sum = contract(xw_t[...], act.astype(BF16), 1, 1)
    proj[0] = partial_sum
    proj_low[0] = partial_sum.astype(BF16)


def core_half(ids, chans, flip=0):
    half = chans // 2
    return pl.ds(pl.multiple_of(((ids[1] & 1) ^ flip) * half, LANES), half)


def gather_rows(ids, blocks, full):
    if len(blocks) == 1:
        full[...] = blocks[0][...]
        return
    chips = len(blocks) // 2
    for side in range(2):
        for j in range(chips):
            block = blocks[side * chips + j]
            index = (ids[1] ^ (2 * j)) ^ side
            rows = block.shape[0]
            full[pl.ds(pl.multiple_of(index * rows, 16), rows), :] = block[...]


def split(v):
    high = v.astype(BF16)
    return high, (v - high.astype(F32)).astype(BF16)


def spread(left, right, out):
    count, span = left.shape
    lanes = lax.broadcasted_iota(jnp.int32, left.shape, 1)
    shape = (2 * span, 2 * LANES)
    from_left = lax.broadcasted_iota(jnp.int32, shape, 0) < span
    to_left = lax.broadcasted_iota(jnp.int32, shape, 1) < LANES
    ones = jnp.where(from_left == to_left, 1.0, 0.0).astype(BF16)
    rows = []
    for t in range(span):
        pair = [jnp.where(lanes == t, part, 0.0).astype(BF16) for part in (left, right)]
        rows.append(jnp.concatenate(pair, axis=1))
    out[...] = jnp.dot(jnp.concatenate(rows, axis=0), ones, preferred_element_type=F32)


def gather(left, right, count):
    span = right.shape[0]
    lanes = lax.broadcasted_iota(jnp.int32, (count, span), 1)
    wide = contract(left[...], right, 1, 1)
    totals = [jnp.zeros((count, span), F32)] * 4
    for t in range(span):
        totals[t % 4] = jnp.where(lanes == t, wide[t * count : (t + 1) * count, :], totals[t % 4])
    return (totals[0] + totals[1]) + (totals[2] + totals[3])


def sigmoid_of_softplus(step):
    series = step * (1.0 - step * (0.5 - step * (1.0 / 6.0 - step * (1.0 / 24.0))))
    return jnp.where(step < 0.05, series, 1.0 - jnp.exp(-step))


def fold(pend, out, start, half):
    for g in range(pend.shape[0]):
        total = pend[g, pl.ds(half * GROUP * GROUP, GROUP, stride=GROUP), :]
        for s in range(1, GROUP):
            total = total + pend[g, pl.ds(half * GROUP * GROUP + s, GROUP, stride=GROUP), :]
        out[pl.ds(start, GROUP), g * LANES : (g + 1) * LANES] = total


def fwd_kernel(parts, ids, lens, *refs):
    projs, refs = refs[:parts], refs[parts:]
    w_out, u_act, gate, dt_w, dt_b, a_log, skip = refs[:7]
    refs = refs[7:]
    dt, y_rows, gated, edge, low_state, vectors, own = refs[:7]
    sends, refs = refs[7 : 6 + parts], refs[6 + parts :]
    dtu, y, pend, carry = refs
    span, chans = dtu.shape
    nstate = a_log.shape[0]
    rank = dt_w.shape[0]
    block = pl.program_id(1)
    groups = chans // LANES

    @pl.when(block == 0)
    def _():
        carry[...] = jnp.zeros(carry.shape, F32)

    proj = projs[0][0]
    for other in projs[1:]:
        proj = proj + other[0].astype(F32)
    lin = contract(proj[:rank].astype(BF16), dt_w[...], 0, 0) + dt_b[...]
    step = softplus(lin)
    dt[0] = step
    dtu[...] = step * u_act[0]
    spread(proj[rank : rank + nstate], proj[rank + nstate :], vectors.at[0])
    rate = -jnp.exp(a_log[...])
    lane = [slice(g * LANES, (g + 1) * LANES) for g in range(groups)]

    edge[0, 0] = carry[...]

    def steps(i, state):
        state = list(state)
        for half in range(2):
            start = pl.multiple_of((2 * i + half) * GROUP, GROUP)
            dt_rows = dt[0, pl.ds(start, GROUP), :]
            dtu_rows = dtu[pl.ds(start, GROUP), :]
            for k in range(GROUP):
                at = pl.ds(pl.multiple_of((start + k) * nstate, nstate), nstate)
                b_t = vectors[0, at, :LANES]
                c_t = vectors[0, at, LANES:]
                rows = pl.ds((half * GROUP + k) * GROUP, GROUP)
                for g in range(groups):
                    dt_t = dt_rows[k : k + 1, lane[g]]
                    dtu_t = dtu_rows[k : k + 1, lane[g]]
                    new = jnp.exp(dt_t * rate[:, lane[g]]) * state[g] + dtu_t * b_t
                    state[g] = new
                    low_state[0, at, lane[g]] = new.astype(BF16)
                    term = c_t * new
                    pend[g, rows, :] = sum(term[s : s + GROUP] for s in range(0, nstate, GROUP))
            fold(pend, y, start, half)
        return tuple(state)

    last = lax.fori_loop(0, span // (2 * GROUP), steps, tuple(carry[:, l] for l in lane))
    for g in range(groups):
        carry[:, lane[g]] = last[g]
    rows = y[...] + skip[...] * u_act[0]
    y_rows[0] = rows
    gate_in = gate[0]
    position = block * span + lax.broadcasted_iota(jnp.int32, (span, 1), 0)
    live = (position < lens[pl.program_id(0)]).astype(F32)
    low = (rows * (gate_in * sigmoid(gate_in)) * live).astype(BF16)
    gated[0] = low
    quarter = own.shape[2]
    for k in range(parts):
        rows = pl.ds(pl.multiple_of((ids[0] ^ k) * quarter, LANES), quarter)
        term = contract(low, w_out[rows, :], 1, 1)
        if k == 0:
            own[0] = term
        else:
            sends[k - 1][0] = term.astype(BF16)


def bwd_kernel(parts, ids, lens, *refs):
    projs, refs = refs[:parts], refs[parts:]
    cots, refs = refs[:parts], refs[parts:]
    w_full, u_act, gate, dt, y_rows, edge, low_state, vectors, dt_w, a_log, skip = refs[:11]
    refs = refs[11:]
    cot_full, d_proj, d_proj_low, d_scan, d_gate, small, small_theirs = refs[:7]
    dtu, d_y, d_dtu, d_dta, pend_q, pend_r, carry, g_rate, low_grad = refs[7:]
    span, chans = dtu.shape
    nstate = a_log.shape[0]
    rank = dt_w.shape[0]
    first = (pl.program_id(0) == 0) & (pl.program_id(1) == 0)
    last = (pl.program_id(0) == pl.num_programs(0) - 1) & (pl.program_id(1) == pl.num_programs(1) - 1)
    block = pl.num_programs(1) - 1 - pl.program_id(1)
    groups = chans // LANES
    quarter = cots[0].shape[2]
    lane = [slice(g * LANES, (g + 1) * LANES) for g in range(groups)]

    @pl.when(first)
    def _():
        small[...] = jnp.zeros(small.shape, F32)
        g_rate[...] = jnp.zeros(g_rate.shape, F32)

    @pl.when(pl.program_id(1) == 0)
    def _():
        carry[...] = jnp.zeros(carry.shape, F32)

    for k, cot in enumerate(cots):
        cols = pl.ds(pl.multiple_of((ids[0] ^ k) * quarter, LANES), quarter)
        cot_full[0, :, cols] = cot[0]
    d_gated = jnp.dot(cot_full[0], w_full[...], preferred_element_type=F32)

    proj = projs[0][0]
    for other in projs[1:]:
        proj = proj + other[0].astype(F32)
    dt_low = proj[:rank].astype(BF16)
    u = u_act[0]
    step = dt[0]
    dtu[...] = step * u
    gate_in = gate[0]
    gate_sig = sigmoid(gate_in)
    position = block * span + lax.broadcasted_iota(jnp.int32, (span, 1), 0)
    live = (position < lens[pl.program_id(0)]).astype(F32)
    d_live = d_gated * live
    d_rows = d_live * (gate_in * gate_sig)
    d_y[...] = d_rows
    d_gate[0] = (d_live * y_rows[0] * (gate_sig * (1.0 + gate_in * (1.0 - gate_sig)))).astype(BF16)
    rate = -jnp.exp(a_log[...])
    count = span // (2 * GROUP)

    def steps(i, loop):
        run, acc = list(loop[0]), list(loop[1])
        for half in reversed(range(2)):
            start = pl.multiple_of((2 * (count - 1 - i) + half) * GROUP, GROUP)
            dt_rows = dt[0, pl.ds(start, GROUP), :]
            dy_rows = d_y[pl.ds(start, GROUP), :]
            for k in reversed(range(GROUP)):
                at = pl.ds(pl.multiple_of((start + k) * nstate, nstate), nstate)
                b_t = vectors[0, at, :LANES]
                c_t = vectors[0, at, LANES:]
                rows = pl.ds((half * GROUP + k) * GROUP, GROUP)
                before = start + k - 1
                if half == 0 and k == 0:
                    before = jnp.maximum(before, 0)
                before = pl.ds(pl.multiple_of(before * nstate, nstate), nstate)
                for g in range(groups):
                    old = low_state[0, before, lane[g]].astype(F32)
                    if half == 0 and k == 0:
                        old = jnp.where(start == 0, edge[0, 0, :, lane[g]], old)
                    dt_t = dt_rows[k : k + 1, lane[g]]
                    dy_t = dy_rows[k : k + 1, lane[g]]
                    d_state = run[g] + c_t * dy_t
                    low_grad[at, lane[g]] = d_state.astype(BF16)
                    decayed = jnp.exp(dt_t * rate[:, lane[g]]) * d_state
                    run[g] = decayed
                    d_exp = decayed * old
                    acc[g] = acc[g] + d_exp * dt_t
                    term_q = d_exp * rate[:, lane[g]]
                    term_r = d_state * b_t
                    pend_q[g, rows, :] = sum(term_q[s : s + GROUP] for s in range(0, nstate, GROUP))
                    pend_r[g, rows, :] = sum(term_r[s : s + GROUP] for s in range(0, nstate, GROUP))
            fold(pend_q, d_dta, start, half)
            fold(pend_r, d_dtu, start, half)
        return tuple(run), tuple(acc)

    run, acc = lax.fori_loop(
        0,
        count,
        steps,
        (tuple(carry[:, l] for l in lane), tuple(g_rate[:, l] for l in lane)),
    )
    d_b = gather(low_grad, dtu[...].astype(BF16), nstate)
    d_c = gather(low_state.at[0], d_rows.astype(BF16), nstate)
    for g in range(groups):
        carry[:, lane[g]] = run[g]
        g_rate[:, lane[g]] = acc[g]
    d_lin = (d_dtu[...] * u + d_dta[...]) * sigmoid_of_softplus(step)
    d_scan[0] = d_dtu[...] * step + d_rows * skip[...]
    d_low = d_lin.astype(BF16)
    full = jnp.concatenate([contract(dt_w[...], d_low, 1, 1), d_b, d_c], axis=0)
    d_proj[0] = full
    d_proj_low[0] = full.astype(BF16)
    small[:rank, :] += jnp.dot(dt_low, d_low, preferred_element_type=F32)
    row = rank + nstate
    small[row : row + 1, :] += jnp.sum(d_lin, axis=0, keepdims=True)
    small[row + 1 : row + 2, :] += jnp.sum(d_rows * u, axis=0, keepdims=True)

    @pl.when(last)
    def _():
        small[rank : rank + nstate, :] = g_rate[...] * rate
        small_theirs[...] = small[:, core_half(ids, chans, 1)]


def post_kernel(parts, ids, *refs):
    projs, refs = refs[:parts], refs[parts:]
    xs, refs = refs[:parts], refs[parts:]
    d_scan, d_gate, u_act, summed, inner, inv, w_full, gain, xw_t, conv_w = refs[:10]
    refs = refs[10:]
    d_inner_low, small, small_theirs, tiny, own = refs[:5]
    sends, refs = refs[5 : 4 + parts], refs[4 + parts :]
    padded, front, d_both = refs
    tokens, chans = d_scan.shape[1:]
    quarter = own.shape[2]
    taps = conv_w.shape[0]
    m = pl.program_id(0)

    @pl.when(m == 0)
    def _():
        padded[tokens:, :] = jnp.zeros((GROUP, chans), F32)
        front[:GROUP, :] = jnp.zeros((GROUP, chans), F32)
        small[...] = jnp.zeros(small.shape, F32)
        tiny[...] = jnp.zeros(tiny.shape, F32)

    proj = projs[0][0]
    for other in projs[1:]:
        proj = proj + other[0].astype(F32)
    d_proj = proj.astype(BF16)
    count = d_proj.shape[0]
    d_u = d_scan[0] + contract(d_proj, xw_t[...], 0, 0)
    small[:count, :] += jnp.dot(d_proj, u_act[0].astype(BF16), preferred_element_type=F32)
    conv = summed[0]
    sig = sigmoid(conv)
    d_conv = d_u * (sig * (1.0 + conv * (1.0 - sig)))
    padded[:tokens, :] = d_conv
    front[GROUP:, :] = inner[0]
    d_inner = 0.0
    for j in range(taps):
        d_inner = d_inner + conv_w[j : j + 1, :] * padded[pl.ds(taps - 1 - j, tokens), :]
        small[count + j : count + j + 1, :] += jnp.sum(
            d_conv * front[pl.ds(GROUP - taps + 1 + j, tokens), :], axis=0, keepdims=True
        )
    small[count + taps : count + taps + 1, :] += jnp.sum(d_conv, axis=0, keepdims=True)

    @pl.when(m == pl.num_programs(0) - 1)
    def _():
        small_theirs[...] = small[:, core_half(ids, chans, 1)]

    d_inner_low[0] = d_inner.astype(BF16)
    d_both[:, :chans] = d_inner.astype(BF16)
    d_both[:, chans:] = d_gate[0]
    scale = inv[0][:, :1]
    dots = 0.0
    for k in range(parts):
        cols = pl.ds(pl.multiple_of((ids[0] ^ k) * quarter, LANES), quarter)
        d_norm = contract(d_both[...], w_full[cols, :], 1, 1)
        if k == 0:
            own[0] = d_norm
        else:
            sends[k - 1][0] = d_norm.astype(BF16)
        along = d_norm * xs[k][0].astype(F32)
        tiny[0:1, cols] += jnp.sum(along * scale, axis=0, keepdims=True)
        weighted = along * gain[:, cols]
        for c in range(0, quarter, LANES):
            dots = dots + weighted[:, c : c + LANES]
    dots = jnp.sum(jnp.transpose(dots), axis=0, keepdims=True)
    tiny[1:2, pl.ds(pl.multiple_of(m * tokens, LANES), tokens)] = dots


def grad_kernel(chips, pairs, ids, *refs):
    lefts, rights, (mine, theirs) = refs[:pairs], refs[pairs : 2 * pairs], refs[2 * pairs :]
    wide = rights[0].shape[1]
    for p, (left, right) in enumerate(zip(lefts, rights)):
        at = slice(p * wide, (p + 1) * wide)
        if chips == 0:
            mine[:, at] = contract(left[...], right[...], 0, 0)
            continue
        rows = mine.shape[1]
        for side, out in enumerate((theirs, mine)):
            for j in range(chips):
                index = (ids[1] ^ (2 * j)) ^ (1 - side)
                cols = pl.ds(pl.multiple_of(index * rows, LANES), rows)
                out[j, :, at] = contract(left[:, cols], right[...], 0, 0).astype(out.dtype)


def merge_kernel(step, row, ids, mine, got, small, small_got, *refs):
    tinies, (own, part, *sends) = (refs[:2], refs[2:]) if row else ((), refs)
    rows = mine.shape[1]
    chans = small.shape[1]
    half = chans // 2
    part[...] = small[:, core_half(ids, chans)] + small_got[...]
    if row:
        for i in range(tinies[0].shape[1] // chans):
            cols = pl.ds(pl.multiple_of((ids[1] & 1) * half, LANES) + i * chans, half)
            part[row + i : row + i + 1, :] = tinies[0][0:1, cols] + tinies[1][0:1, cols]
    own[...] = mine[0].astype(F32) + got[0].astype(F32)
    pieces = part.shape[0] // step
    for j, send in enumerate(sends):
        send[:rows, :] = (mine[j + 1].astype(F32) + got[j + 1].astype(F32)).astype(BF16)
        for c in range(pieces):
            send[rows:, c * half : (c + 1) * half] = part[c * step : (c + 1) * step, :].astype(BF16)
        if pieces * half < send.shape[1]:
            send[rows:, pieces * half :] = jnp.zeros((step, send.shape[1] - pieces * half), BF16)


def add_received(step, own, part, gots, half):
    rows = own.shape[0]
    total = own[...]
    for got in gots:
        total = total + got[:rows, :].astype(F32)
    lanes = part.shape[1]
    for c in range(part.shape[0] // step):
        piece = part[c * step : (c + 1) * step, :]
        for got in gots:
            piece = piece + got[rows:, c * lanes : (c + 1) * lanes].astype(F32)
        half[c * step : (c + 1) * step, :] = piece
    return total


def final_early_kernel(step, own, part, *refs):
    gots, (grad_gate, grad_out, half) = refs[:-3], refs[-3:]
    total = add_received(step, own, part, gots, half)
    wide = grad_gate.shape[1]
    grad_gate[...] = total[:, :wide]
    grad_out[...] = jnp.transpose(total[:, wide:])


def final_late_kernel(step, own, part, grad_gate, *refs):
    gots, (grad_in, half) = refs[:-2], refs[-2:]
    grad_in[:, 0, :] = add_received(step, own, part, gots, half)
    grad_in[:, 1, :] = grad_gate[...]


def outputs_kernel(
    ids, scan_half, scan_got, post_half, post_got, gain, x_w, dt_w, dt_b, conv_w, conv_b, a_log, skip, scan, post
):
    chans = scan.shape[1]
    for full, half, got in ((scan, scan_half, scan_got), (post, post_half, post_got)):
        full[:, core_half(ids, chans)] = half[...]
        full[:, core_half(ids, chans, 1)] = got[...]
    rank = dt_w.shape[0]
    nstate = a_log.shape[0]
    count = x_w.shape[0]
    taps = conv_w.shape[0]
    dt_w[...] = scan[:rank, :]
    a_log[...] = scan[rank : rank + nstate, :]
    dt_b[...] = scan[rank + nstate : rank + nstate + 1, :]
    skip[...] = scan[rank + nstate + 1 : rank + nstate + 2, :]
    x_w[...] = post[:count, :]
    conv_w[...] = post[count : count + taps, :]
    conv_b[...] = post[count + taps : count + taps + 1, :]
    for i in range(gain.shape[1] // chans):
        row = count + taps + 1 + i
        gain[:, i * chans : (i + 1) * chans] = post[row : row + 1, :]


def whole(shape):
    return pl.BlockSpec(shape, lambda *_: (0,) * len(shape))


SMEM = pl.BlockSpec(memory_space=pltpu.SMEM)


def params(grid, mib=56):
    return pltpu.CompilerParams(
        dimension_semantics=("arbitrary",) * grid, vmem_limit_bytes=mib * 1024 * 1024
    )


def cost(micros):
    return pl.CostEstimate(flops=int(micros * 1.15e9), bytes_accessed=0, transcendentals=0)


def struct(shape, dtype):
    return jax.ShapeDtypeStruct(shape, dtype)


def run_pre(ids, xs, ws, gain, conv_w, conv_b, xw_t):
    micro, tokens, quarter = xs[0].shape
    width = gain.shape[1]
    chans = conv_w.shape[1]
    count = xw_t.shape[0]
    per = lambda *tail: pl.BlockSpec((1,) + tail, lambda m: (m,) + (0,) * len(tail))
    return pl.pallas_call(
        partial(pre_kernel, len(xs), len(ws)),
        grid=(micro,),
        in_specs=[SMEM]
        + [per(tokens, quarter)] * len(xs)
        + [whole(w.shape) for w in ws]
        + [whole(gain.shape), whole(conv_w.shape), whole(conv_b.shape), whole(xw_t.shape)],
        out_specs=[
            per(tokens, width),
            whole((width, ws[0].shape[1])),
            per(tokens, chans),
            per(tokens, chans),
            per(tokens, chans),
            per(tokens, chans),
            per(tokens, LANES),
            per(count, tokens),
            per(count, tokens),
        ],
        out_shape=[
            struct((micro, tokens, width), BF16),
            struct((width, ws[0].shape[1]), BF16),
            struct((micro, tokens, chans), F32),
            struct((micro, tokens, chans), F32),
            struct((micro, tokens, chans), F32),
            struct((micro, tokens, chans), F32),
            struct((micro, tokens, LANES), F32),
            struct((micro, count, tokens), F32),
            struct((micro, count, tokens), BF16),
        ],
        scratch_shapes=[pltpu.VMEM((tokens + GROUP, chans), F32)],
        compiler_params=params(1),
        cost_estimate=cost(7),
        name="pre",
    )(ids, *xs, *ws, gain, conv_w, conv_b, xw_t)


def run_fwd(ids, lens, projs, w_full, u_act, gate, dt_w, dt_b, a_log, skip):
    micro, tokens, chans = u_act.shape
    parts = len(projs)
    width = w_full.shape[0]
    quarter = width // parts
    count = projs[0].shape[1]
    nstate = a_log.shape[0]
    span = min(LANES, tokens)
    rows = lambda *tail: pl.BlockSpec((1, span) + tail, lambda m, b: (m, b) + (0,) * len(tail))
    return pl.pallas_call(
        partial(fwd_kernel, parts),
        grid=(micro, tokens // span),
        in_specs=[SMEM, SMEM]
        + [pl.BlockSpec((1, count, span), lambda m, b: (m, 0, b))] * parts
        + [pl.BlockSpec((width, chans), lambda m, b: (0, 2)), rows(chans), rows(chans)]
        + [whole(v.shape) for v in (dt_w, dt_b, a_log, skip)],
        out_specs=[
            rows(chans),
            rows(chans),
            rows(chans),
            pl.BlockSpec((1, 1, nstate, chans), lambda m, b: (m, b, 0, 0)),
            pl.BlockSpec((1, span * nstate, chans), lambda m, b: (m, b, 0)),
            pl.BlockSpec((1, span * nstate, 2 * LANES), lambda m, b: (m, b, 0)),
        ]
        + [rows(quarter)] * parts,
        out_shape=[
            struct((micro, tokens, chans), F32),
            struct((micro, tokens, chans), F32),
            struct((micro, tokens, chans), BF16),
            struct((micro, tokens // span, nstate, chans), F32),
            struct((micro, tokens * nstate, chans), BF16),
            struct((micro, tokens * nstate, 2 * LANES), F32),
            struct((micro, tokens, quarter), F32),
        ]
        + [struct((micro, tokens, quarter), BF16)] * (parts - 1),
        scratch_shapes=[pltpu.VMEM((span, chans), F32)] * 2
        + [pltpu.VMEM((chans // LANES, 2 * GROUP * GROUP, LANES), F32), pltpu.VMEM((nstate, chans), F32)],
        compiler_params=params(2),
        cost_estimate=cost(16),
        name="scan_forward",
    )(ids, lens, *projs, w_full, u_act, gate, dt_w, dt_b, a_log, skip)


def run_bwd(ids, lens, projs, cots, w_full, u_act, gate, dt, y_rows, edge, low_state, vectors, dt_w, a_log, skip):
    micro, tokens, chans = u_act.shape
    parts = len(projs)
    width = w_full.shape[0]
    quarter = cots[0].shape[2]
    count = projs[0].shape[1]
    nstate = a_log.shape[0]
    rank = dt_w.shape[0]
    span = min(LANES, tokens)
    blocks = tokens // span
    small = SCAN_STEP * -(-(rank + nstate + 2) // SCAN_STEP)
    rows = lambda *tail: pl.BlockSpec(
        (1, span) + tail, lambda m, b: (m, blocks - 1 - b) + (0,) * len(tail)
    )
    proj = pl.BlockSpec((1, count, span), lambda m, b: (m, 0, blocks - 1 - b))
    return pl.pallas_call(
        partial(bwd_kernel, parts),
        grid=(micro, blocks),
        in_specs=[SMEM, SMEM]
        + [proj] * parts
        + [rows(quarter)] * parts
        + [pl.BlockSpec((width, chans), lambda m, b: (0, 2)), rows(chans), rows(chans), rows(chans), rows(chans)]
        + [pl.BlockSpec((1, 1, nstate, chans), lambda m, b: (m, blocks - 1 - b, 0, 0))]
        + [pl.BlockSpec((1, span * nstate, chans), lambda m, b: (m, blocks - 1 - b, 0))]
        + [pl.BlockSpec((1, span * nstate, 2 * LANES), lambda m, b: (m, blocks - 1 - b, 0))]
        + [whole(v.shape) for v in (dt_w, a_log, skip)],
        out_specs=[rows(width), proj, proj, rows(chans), rows(chans), whole((small, chans)), whole((small, chans // 2))],
        out_shape=[
            struct((micro, tokens, width), BF16),
            struct((micro, count, tokens), F32),
            struct((micro, count, tokens), BF16),
            struct((micro, tokens, chans), F32),
            struct((micro, tokens, chans), BF16),
            struct((small, chans), F32),
            struct((small, chans // 2), F32),
        ],
        scratch_shapes=[pltpu.VMEM((span, chans), F32)] * 4
        + [pltpu.VMEM((chans // LANES, 2 * GROUP * GROUP, LANES), F32)] * 2
        + [pltpu.VMEM((nstate, chans), F32)] * 2
        + [pltpu.VMEM((span * nstate, chans), BF16)],
        compiler_params=params(2),
        cost_estimate=cost(21),
        name="scan_backward",
    )(ids, lens, *projs, *cots, w_full, u_act, gate, dt, y_rows, edge, low_state, vectors, dt_w, a_log, skip)


def run_post(ids, projs, xs, d_scan, d_gate, u_act, summed, inner, inv, w_full, gain, xw_t, conv_w):
    micro, tokens, chans = u_act.shape
    parts = len(projs)
    width = w_full.shape[0]
    quarter = width // parts
    count = projs[0].shape[1]
    taps = conv_w.shape[0]
    small = POST_STEP * -(-(count + taps + 1 + width // chans) // POST_STEP)
    lanes = max(width, LANES * -(-micro * tokens // LANES))
    per = lambda *tail: pl.BlockSpec((1,) + tail, lambda m: (m,) + (0,) * len(tail))
    return pl.pallas_call(
        partial(post_kernel, parts),
        grid=(micro,),
        in_specs=[SMEM]
        + [per(count, tokens)] * parts
        + [per(tokens, quarter)] * parts
        + [per(tokens, chans)] * 5
        + [per(tokens, LANES)]
        + [whole((width, 2 * chans))]
        + [whole(v.shape) for v in (gain, xw_t, conv_w)],
        out_specs=[
            per(tokens, chans),
            whole((small, chans)),
            whole((small, chans // 2)),
            whole((GROUP, lanes)),
        ]
        + [per(tokens, quarter)] * parts,
        out_shape=[
            struct((micro, tokens, chans), BF16),
            struct((small, chans), F32),
            struct((small, chans // 2), F32),
            struct((GROUP, lanes), F32),
            struct((micro, tokens, quarter), F32),
        ]
        + [struct((micro, tokens, quarter), BF16)] * (parts - 1),
        scratch_shapes=[pltpu.VMEM((tokens + GROUP, chans), F32)] * 2
        + [pltpu.VMEM((tokens, 2 * chans), BF16)],
        compiler_params=params(1),
        cost_estimate=cost(20),
        name="post",
    )(ids, *projs, *xs, d_scan, d_gate, u_act, summed, inner, inv, w_full, gain, xw_t, conv_w)


def run_grad(name, ids, lefts, rights, shape, chips):
    if chips == 0:
        outs = [struct(shape, F32), struct((GROUP, LANES), BF16)]
    else:
        outs = [struct((chips,) + shape, BF16)] * 2
    flat = lambda v: v.reshape(-1, v.shape[-1])
    return run_local(
        partial(grad_kernel, chips, len(lefts)), name, outs, ids, *map(flat, lefts), *map(flat, rights)
    )


VMEM = pl.BlockSpec(memory_space=pltpu.VMEM)


def run_local(kernel, name, outs, ids, *operands, scratch=()):
    return pl.pallas_call(
        kernel,
        grid=(1,),
        in_specs=([SMEM] if ids is not None else []) + [whole(v.shape) for v in operands],
        out_specs=[whole(v.shape) for v in outs],
        out_shape=outs,
        scratch_shapes=list(scratch),
        compiler_params=pltpu.CompilerParams(vmem_limit_bytes=56 * 1024 * 1024),
        cost_estimate=cost(0.3),
        name=name,
    )(*(() if ids is None else (ids,)), *operands)


def after(value, *earlier):
    return lax.optimization_barrier((value, earlier))[0]


def others(value, axis, step=1):
    count = lax.axis_size(axis)
    return [swap(value, axis, mask) for mask in range(step, count, step)]


def gather_line(value, axis, early=()):
    count = lax.axis_size(axis)
    got = {0: value}
    mask = count // 2
    while mask:
        for known in sorted(got):
            fresh = swap(got[known], axis, mask) if known or mask not in early else early[mask]
            got[known | mask] = fresh
        mask //= 2
    return [got[k] for k in range(count)]


def with_sibling(blocks):
    return blocks + [swap(block, "dp", 1) for block in blocks]


def sum_all(value):
    core = lax.rem(lax.axis_index("dp"), 2)
    half = value.shape[0] // 2
    halves = value.reshape((2, half) + value.shape[1:])
    mine = lax.dynamic_index_in_dim(halves, core, 0, keepdims=False)
    theirs = lax.dynamic_index_in_dim(halves, 1 - core, 0, keepdims=False)
    total = mine + swap(theirs, "dp", 1)
    for got in others(total, "dp", 2):
        total = total + got
    other = swap(total, "dp", 1)
    first = jnp.where(core == 0, total, other)
    second = jnp.where(core == 0, other, total)
    return jnp.concatenate([first, second], axis=0)


def body(
    tokens,
    lengths,
    norm_gain,
    in_weight,
    x_weight,
    dt_weight,
    dt_bias,
    conv_weight,
    conv_bias,
    a_log,
    skip,
    out_weight,
    cotangent,
):
    micro, seq, quarter = tokens.shape
    chans = in_weight.shape[2]
    width = norm_gain.shape[0]
    dps = lax.axis_size("dp")
    rank = dt_weight.shape[0]
    nstate = a_log.shape[0]
    taps = conv_weight.shape[0]
    count = x_weight.shape[1]
    ids = jnp.stack([lax.axis_index("tensor"), lax.axis_index("dp")]).astype(jnp.int32)
    lens = lengths[:, 0]
    gain = norm_gain[None]
    xw_t = x_weight.T
    in_rows = in_weight.reshape(in_weight.shape[0], 2 * chans)
    by_block = in_rows.shape[0] % LANES == 0
    chips = dps // 2 if by_block else 0
    parts = lax.axis_size("tensor")
    weight = jnp.concatenate([in_rows, out_weight.T], axis=1)

    xs = gather_line(tokens, "tensor")
    if by_block:
        mine = [weight] + [
            swap(weight, "dp", mask) for mask in range(2, dps, 2)
        ]
        blocks = with_sibling(after(mine, *xs))
    else:
        blocks = [lax.all_gather(weight, "dp", axis=0, tiled=True)]
    normed, w_full, inner, summed, u_act, gate, inv, proj, proj_low = run_pre(
        ids, xs, blocks, gain, conv_weight, conv_bias[None], xw_t
    )
    cot_early = after(cotangent, *xs)
    early = {mask: swap(cot_early, "tensor", mask) for mask in (parts // 2, 1)}
    projs = [proj] + others(proj_low, "tensor")
    far = after(early[parts // 2], *projs)
    early[parts // 2] = far
    cots = gather_line(cotangent, "tensor", early)
    dt, y_rows, gated, edge, low_state, vectors, own_out, *out_terms = run_fwd(
        ids, lens, projs, w_full, u_act, gate, dt_weight, dt_bias[None], a_log, skip[None]
    )
    out_got = [swap(term, "tensor", k + 1) for k, term in enumerate(out_terms)]
    cot_full, d_proj, d_proj_low, d_scan, d_gate, scan_small, scan_theirs = run_bwd(
        ids, lens, projs, cots, w_full, u_act, gate, dt, y_rows, edge, low_state, vectors, dt_weight, a_log, skip[None]
    )
    d_projs = [d_proj] + others(after(d_proj_low, *out_got), "tensor")
    branch = own_out
    for term in out_got:
        branch = branch + term.astype(F32)
    mixed = (tokens.astype(F32) + branch).astype(BF16)
    rows = weight.shape[0] if chips else width
    early_mine, early_theirs = run_grad(
        "grad_early",
        ids,
        [after(normed, d_projs[1]), cot_full],
        [d_gate, gated],
        (rows, 2 * chans),
        chips,
    )

    def merged(name, step, row, mine, theirs, small, small_theirs, tinies, wide):
        part = struct((small.shape[0], chans // 2), F32)
        own, part, *sends = run_local(
            partial(merge_kernel, step, row),
            name,
            [struct((rows, wide), F32), part] + [struct((rows + step, wide), BF16)] * (chips - 1),
            ids,
            mine,
            swap(theirs, "dp", 1),
            small,
            swap(small_theirs, "dp", 1),
            *tinies,
        )
        return own, part, sends

    if chips:
        early_own, early_part, sends = merged(
            "merge_early", SCAN_STEP, 0, early_mine, early_theirs, scan_small, scan_theirs, (), 2 * chans
        )
        early_gots = [swap(send, "dp", 2 * (j + 1)) for j, send in enumerate(sends)]
    d_inner, small, small_theirs, tiny, own_norm, *norm_terms = run_post(
        ids, d_projs, xs, d_scan, d_gate, u_act, summed, inner, inv, w_full, gain, xw_t, conv_weight
    )
    tiny_got = others(tiny, "tensor")
    near = parts // 2
    halves = [own_norm] + norm_terms
    passed = [swap(halves[k], "tensor", k) for k in range(1, near)]
    relayed = [swap(halves[near + k], "tensor", k) for k in range(1, near)]
    far = halves[near].astype(F32)
    for got in relayed:
        far = far + got.astype(F32)
    far = far.astype(BF16)
    norm_got = passed + [swap(far, "tensor", near)]
    late_mine, late_theirs = run_grad("grad_late", ids, [normed], [d_inner], (rows, chans), chips)
    for got in tiny_got:
        tiny = tiny + got
    row = count + taps + 1
    if chips:
        late_own, late_part, sends = merged(
            "merge_late",
            POST_STEP,
            row,
            after(late_mine, far),
            late_theirs,
            small,
            small_theirs,
            (tiny, swap(tiny, "dp", 1)),
            chans,
        )
        late_gots = [swap(send, "dp", 2 * (j + 1)) for j, send in enumerate(sends)]
        grad_gate, grad_out, scan_half = run_local(
            partial(final_early_kernel, SCAN_STEP),
            "final_early",
            [struct((rows, chans), F32), struct(out_weight.shape, F32), struct(early_part.shape, F32)],
            None,
            early_own,
            early_part,
            *early_gots,
        )
        grad_in, post_half = run_local(
            partial(final_late_kernel, POST_STEP),
            "final_late",
            [struct(in_weight.shape, F32), struct(late_part.shape, F32)],
            None,
            late_own,
            late_part,
            grad_gate,
            *late_gots,
        )
        g_gain, g_x, g_dt, g_dtb, g_conv, g_convb, g_alog, g_skip = run_local(
            outputs_kernel,
            "outputs",
            [
                struct((1, width), F32),
                struct((count, chans), F32),
                struct((rank, chans), F32),
                struct((1, chans), F32),
                struct((taps, chans), F32),
                struct((1, chans), F32),
                struct((nstate, chans), F32),
                struct((1, chans), F32),
            ],
            ids,
            scan_half,
            swap(scan_half, "dp", 1),
            post_half,
            swap(post_half, "dp", 1),
            scratch=[pltpu.VMEM((scan_small.shape[0], chans), F32), pltpu.VMEM((small.shape[0], chans), F32)],
        )
        smalls = (g_gain[0], g_x.T, g_dt, g_dtb[0], g_conv, g_convb[0], g_alog, g_skip[0])
    else:
        grad_inner = lax.psum_scatter(late_mine, "dp", scatter_dimension=0, tiled=True)
        early = lax.psum_scatter(early_mine, "dp", scatter_dimension=0, tiled=True)
        grad_in = jnp.stack([grad_inner, early[:, :chans]], axis=1)
        grad_out = early[:, chans:].T
        scan_small = sum_all(scan_small)
        small = sum_all(lax.dynamic_update_slice_in_dim(small, tiny[0, :width].reshape(-1, chans), row, 0))
        smalls = (
            small[row : row + width // chans].reshape(width),
            small[:count].T,
            scan_small[:rank],
            scan_small[rank + nstate],
            small[count : count + taps],
            small[count + taps],
            scan_small[rank : rank + nstate],
            scan_small[rank + nstate + 1],
        )
    d_norm = own_norm
    for term in norm_got:
        d_norm = d_norm + term.astype(F32)
    scale = inv[:, :, :1]
    dots = tiny[1, : micro * seq].reshape(micro, seq, 1)
    own_gain = lax.dynamic_slice_in_dim(norm_gain, ids[0] * quarter, quarter, 0)
    d_x = scale * (d_norm * own_gain) - tokens.astype(F32) * (scale * scale * scale * dots / width)
    input_grad = cotangent.astype(F32) + d_x
    return (mixed, input_grad, smalls[0], grad_in.reshape(in_weight.shape)) + smalls[1:] + (grad_out,)


def solution(mesh):
    rows = P(None, "dp", "tensor")
    chans = P(None, "tensor")
    return jax.shard_map(
        body,
        mesh=mesh,
        in_specs=(
            rows,
            P(None, "dp"),
            P(),
            P("dp", None, "tensor"),
            P("tensor", None),
            chans,
            P("tensor"),
            chans,
            P("tensor"),
            chans,
            P("tensor"),
            P("tensor", "dp"),
            rows,
        ),
        out_specs=(
            rows,
            rows,
            P(),
            P("dp", None, "tensor"),
            P("tensor", None),
            chans,
            P("tensor"),
            chans,
            P("tensor"),
            chans,
            P("tensor"),
            P("tensor", "dp"),
        ),
        check_vma=False,
    )
```

```python
from functools import partial

import jax
import jax.numpy as jnp
from jax import lax
from jax.experimental import pallas as pl
from jax.experimental.pallas import tpu as pltpu
from jax.sharding import PartitionSpec as P

EPS = 1e-05
F32 = jnp.float32
BF16 = jnp.bfloat16
GROUP = 8
LANES = 128
SCAN_STEP = 32
POST_STEP = 64


def contract(left, right, left_dim, right_dim):
    return lax.dot_general(
        left, right, (((left_dim,), (right_dim,)), ((), ())), preferred_element_type=F32
    )


def sigmoid(v):
    return 1.0 / (1.0 + jnp.exp(-v))


def softplus(v):
    return jnp.maximum(v, 0.0) + jnp.log1p(jnp.exp(-jnp.abs(v)))


def swap(value, axis, mask):
    count = lax.axis_size(axis)
    return lax.ppermute(value, axis, [(i, i ^ mask) for i in range(count)])


def pre_kernel(parts, blocks, ids, *refs):
    xs, refs = refs[:parts], refs[parts:]
    ws, refs = refs[:blocks], refs[blocks:]
    gain, conv_w, conv_b, xw_t = refs[:4]
    normed, w_full, inner, summed, u_act, gate, inv, proj, proj_low, padded = refs[4:]
    quarter = xs[0].shape[2]
    chans = inner.shape[2]

    @pl.when(pl.program_id(0) == 0)
    def _():
        gather_rows(ids, ws, w_full)
        padded[:GROUP, :] = jnp.zeros((GROUP, chans), F32)

    square = 0.0
    for x in xs:
        rows = x[0].astype(F32)
        square = square + jnp.sum(rows * rows, axis=1, keepdims=True)
    scale = lax.rsqrt(square / (parts * quarter) + EPS)
    inv[0] = jnp.broadcast_to(scale, inv.shape[1:])
    for k, x in enumerate(xs):
        cols = pl.ds(pl.multiple_of((ids[0] ^ k) * quarter, LANES), quarter)
        normed[0, :, cols] = (x[0].astype(F32) * scale * gain[:, cols]).astype(BF16)
    both = jnp.dot(normed[0], w_full[:, : 2 * chans], preferred_element_type=F32)
    gate[0] = both[:, chans:]
    inner_in = both[:, :chans]
    inner[0] = inner_in
    tokens = inner_in.shape[0]
    padded[GROUP:, :] = inner_in
    taps = conv_w.shape[0]
    total = jnp.broadcast_to(conv_b[...], inner_in.shape)
    for j in range(taps):
        total = total + conv_w[j : j + 1, :] * padded[pl.ds(GROUP - taps + 1 + j, tokens), :]
    summed[0] = total
    act = total * sigmoid(total)
    u_act[0] = act
    partial_sum = contract(xw_t[...], act.astype(BF16), 1, 1)
    proj[0] = partial_sum
    proj_low[0] = partial_sum.astype(BF16)


def core_half(ids, chans, flip=0):
    half = chans // 2
    return pl.ds(pl.multiple_of(((ids[1] & 1) ^ flip) * half, LANES), half)


def gather_rows(ids, blocks, full):
    if len(blocks) == 1:
        full[...] = blocks[0][...]
        return
    chips = len(blocks) // 2
    for side in range(2):
        for j in range(chips):
            block = blocks[side * chips + j]
            index = (ids[1] ^ (2 * j)) ^ side
            rows = block.shape[0]
            full[pl.ds(pl.multiple_of(index * rows, 16), rows), :] = block[...]


def split(v):
    high = v.astype(BF16)
    return high, (v - high.astype(F32)).astype(BF16)


def spread(left, right, out):
    count, span = left.shape
    lanes = lax.broadcasted_iota(jnp.int32, left.shape, 1)
    shape = (2 * span, 2 * LANES)
    from_left = lax.broadcasted_iota(jnp.int32, shape, 0) < span
    to_left = lax.broadcasted_iota(jnp.int32, shape, 1) < LANES
    ones = jnp.where(from_left == to_left, 1.0, 0.0).astype(BF16)
    rows = []
    for t in range(span):
        pair = [jnp.where(lanes == t, part, 0.0).astype(BF16) for part in (left, right)]
        rows.append(jnp.concatenate(pair, axis=1))
    out[...] = jnp.dot(jnp.concatenate(rows, axis=0), ones, preferred_element_type=F32)


def gather(left, right, count):
    span = right.shape[0]
    lanes = lax.broadcasted_iota(jnp.int32, (count, span), 1)
    wide = contract(left[...], right, 1, 1)
    totals = [jnp.zeros((count, span), F32)] * 4
    for t in range(span):
        totals[t % 4] = jnp.where(lanes == t, wide[t * count : (t + 1) * count, :], totals[t % 4])
    return (totals[0] + totals[1]) + (totals[2] + totals[3])


def sigmoid_of_softplus(step):
    series = step * (1.0 - step * (0.5 - step * (1.0 / 6.0 - step * (1.0 / 24.0))))
    return jnp.where(step < 0.05, series, 1.0 - jnp.exp(-step))


def fold(pend, out, start, half):
    for g in range(pend.shape[0]):
        total = pend[g, pl.ds(half * GROUP * GROUP, GROUP, stride=GROUP), :]
        for s in range(1, GROUP):
            total = total + pend[g, pl.ds(half * GROUP * GROUP + s, GROUP, stride=GROUP), :]
        out[pl.ds(start, GROUP), g * LANES : (g + 1) * LANES] = total


def fwd_kernel(parts, ids, lens, *refs):
    projs, refs = refs[:parts], refs[parts:]
    w_out, u_act, gate, dt_w, dt_b, a_log, skip = refs[:7]
    refs = refs[7:]
    dt, y_rows, gated, edge, low_state, vectors, own = refs[:7]
    sends, refs = refs[7 : 6 + parts], refs[6 + parts :]
    dtu, y, pend, carry = refs
    span, chans = dtu.shape
    nstate = a_log.shape[0]
    rank = dt_w.shape[0]
    block = pl.program_id(1)
    groups = chans // LANES

    @pl.when(block == 0)
    def _():
        carry[...] = jnp.zeros(carry.shape, F32)

    proj = projs[0][0]
    for other in projs[1:]:
        proj = proj + other[0].astype(F32)
    lin = contract(proj[:rank].astype(BF16), dt_w[...], 0, 0) + dt_b[...]
    step = softplus(lin)
    dt[0] = step
    dtu[...] = step * u_act[0]
    spread(proj[rank : rank + nstate], proj[rank + nstate :], vectors.at[0])
    rate = -jnp.exp(a_log[...])
    lane = [slice(g * LANES, (g + 1) * LANES) for g in range(groups)]

    edge[0, 0] = carry[...]

    def steps(i, state):
        state = list(state)
        for half in range(2):
            start = pl.multiple_of((2 * i + half) * GROUP, GROUP)
            dt_rows = dt[0, pl.ds(start, GROUP), :]
            dtu_rows = dtu[pl.ds(start, GROUP), :]
            for k in range(GROUP):
                at = pl.ds(pl.multiple_of((start + k) * nstate, nstate), nstate)
                b_t = vectors[0, at, :LANES]
                c_t = vectors[0, at, LANES:]
                rows = pl.ds((half * GROUP + k) * GROUP, GROUP)
                for g in range(groups):
                    dt_t = dt_rows[k : k + 1, lane[g]]
                    dtu_t = dtu_rows[k : k + 1, lane[g]]
                    new = jnp.exp(dt_t * rate[:, lane[g]]) * state[g] + dtu_t * b_t
                    state[g] = new
                    low_state[0, at, lane[g]] = new.astype(BF16)
                    term = c_t * new
                    pend[g, rows, :] = sum(term[s : s + GROUP] for s in range(0, nstate, GROUP))
            fold(pend, y, start, half)
        return tuple(state)

    last = lax.fori_loop(0, span // (2 * GROUP), steps, tuple(carry[:, l] for l in lane))
    for g in range(groups):
        carry[:, lane[g]] = last[g]
    rows = y[...] + skip[...] * u_act[0]
    y_rows[0] = rows
    gate_in = gate[0]
    position = block * span + lax.broadcasted_iota(jnp.int32, (span, 1), 0)
    live = (position < lens[pl.program_id(0)]).astype(F32)
    low = (rows * (gate_in * sigmoid(gate_in)) * live).astype(BF16)
    gated[0] = low
    quarter = own.shape[2]
    for k in range(parts):
        rows = pl.ds(pl.multiple_of((ids[0] ^ k) * quarter, LANES), quarter)
        term = contract(low, w_out[rows, :], 1, 1)
        if k == 0:
            own[0] = term
        else:
            sends[k - 1][0] = term.astype(BF16)


def bwd_kernel(parts, ids, lens, *refs):
    projs, refs = refs[:parts], refs[parts:]
    cots, refs = refs[:parts], refs[parts:]
    w_full, u_act, gate, dt, y_rows, edge, low_state, vectors, dt_w, a_log, skip = refs[:11]
    refs = refs[11:]
    cot_full, d_proj, d_proj_low, d_scan, d_gate, small, small_theirs = refs[:7]
    dtu, d_y, d_dtu, d_dta, pend_q, pend_r, carry, g_rate, low_grad = refs[7:]
    span, chans = dtu.shape
    nstate = a_log.shape[0]
    rank = dt_w.shape[0]
    first = (pl.program_id(0) == 0) & (pl.program_id(1) == 0)
    last = (pl.program_id(0) == pl.num_programs(0) - 1) & (pl.program_id(1) == pl.num_programs(1) - 1)
    block = pl.num_programs(1) - 1 - pl.program_id(1)
    groups = chans // LANES
    quarter = cots[0].shape[2]
    lane = [slice(g * LANES, (g + 1) * LANES) for g in range(groups)]

    @pl.when(first)
    def _():
        small[...] = jnp.zeros(small.shape, F32)
        g_rate[...] = jnp.zeros(g_rate.shape, F32)

    @pl.when(pl.program_id(1) == 0)
    def _():
        carry[...] = jnp.zeros(carry.shape, F32)

    for k, cot in enumerate(cots):
        cols = pl.ds(pl.multiple_of((ids[0] ^ k) * quarter, LANES), quarter)
        cot_full[0, :, cols] = cot[0]
    d_gated = jnp.dot(cot_full[0], w_full[...], preferred_element_type=F32)

    proj = projs[0][0]
    for other in projs[1:]:
        proj = proj + other[0].astype(F32)
    dt_low = proj[:rank].astype(BF16)
    u = u_act[0]
    step = dt[0]
    dtu[...] = step * u
    gate_in = gate[0]
    gate_sig = sigmoid(gate_in)
    position = block * span + lax.broadcasted_iota(jnp.int32, (span, 1), 0)
    live = (position < lens[pl.program_id(0)]).astype(F32)
    d_live = d_gated * live
    d_rows = d_live * (gate_in * gate_sig)
    d_y[...] = d_rows
    d_gate[0] = (d_live * y_rows[0] * (gate_sig * (1.0 + gate_in * (1.0 - gate_sig)))).astype(BF16)
    rate = -jnp.exp(a_log[...])
    count = span // (2 * GROUP)

    def steps(i, loop):
        run, acc = list(loop[0]), list(loop[1])
        for half in reversed(range(2)):
            start = pl.multiple_of((2 * (count - 1 - i) + half) * GROUP, GROUP)
            dt_rows = dt[0, pl.ds(start, GROUP), :]
            dy_rows = d_y[pl.ds(start, GROUP), :]
            for k in reversed(range(GROUP)):
                at = pl.ds(pl.multiple_of((start + k) * nstate, nstate), nstate)
                b_t = vectors[0, at, :LANES]
                c_t = vectors[0, at, LANES:]
                rows = pl.ds((half * GROUP + k) * GROUP, GROUP)
                before = start + k - 1
                if half == 0 and k == 0:
                    before = jnp.maximum(before, 0)
                before = pl.ds(pl.multiple_of(before * nstate, nstate), nstate)
                for g in range(groups):
                    old = low_state[0, before, lane[g]].astype(F32)
                    if half == 0 and k == 0:
                        old = jnp.where(start == 0, edge[0, 0, :, lane[g]], old)
                    dt_t = dt_rows[k : k + 1, lane[g]]
                    dy_t = dy_rows[k : k + 1, lane[g]]
                    d_state = run[g] + c_t * dy_t
                    low_grad[at, lane[g]] = d_state.astype(BF16)
                    decayed = jnp.exp(dt_t * rate[:, lane[g]]) * d_state
                    run[g] = decayed
                    d_exp = decayed * old
                    acc[g] = acc[g] + d_exp * dt_t
                    term_q = d_exp * rate[:, lane[g]]
                    term_r = d_state * b_t
                    pend_q[g, rows, :] = sum(term_q[s : s + GROUP] for s in range(0, nstate, GROUP))
                    pend_r[g, rows, :] = sum(term_r[s : s + GROUP] for s in range(0, nstate, GROUP))
            fold(pend_q, d_dta, start, half)
            fold(pend_r, d_dtu, start, half)
        return tuple(run), tuple(acc)

    run, acc = lax.fori_loop(
        0,
        count,
        steps,
        (tuple(carry[:, l] for l in lane), tuple(g_rate[:, l] for l in lane)),
    )
    d_b = gather(low_grad, dtu[...].astype(BF16), nstate)
    d_c = gather(low_state.at[0], d_rows.astype(BF16), nstate)
    for g in range(groups):
        carry[:, lane[g]] = run[g]
        g_rate[:, lane[g]] = acc[g]
    d_lin = (d_dtu[...] * u + d_dta[...]) * sigmoid_of_softplus(step)
    d_scan[0] = d_dtu[...] * step + d_rows * skip[...]
    d_low = d_lin.astype(BF16)
    full = jnp.concatenate([contract(dt_w[...], d_low, 1, 1), d_b, d_c], axis=0)
    d_proj[0] = full
    d_proj_low[0] = full.astype(BF16)
    small[:rank, :] += jnp.dot(dt_low, d_low, preferred_element_type=F32)
    row = rank + nstate
    small[row : row + 1, :] += jnp.sum(d_lin, axis=0, keepdims=True)
    small[row + 1 : row + 2, :] += jnp.sum(d_rows * u, axis=0, keepdims=True)

    @pl.when(last)
    def _():
        small[rank : rank + nstate, :] = g_rate[...] * rate
        small_theirs[...] = small[:, core_half(ids, chans, 1)]


def post_kernel(parts, ids, *refs):
    projs, refs = refs[:parts], refs[parts:]
    xs, refs = refs[:parts], refs[parts:]
    d_scan, d_gate, u_act, summed, inner, inv, w_full, gain, xw_t, conv_w = refs[:10]
    refs = refs[10:]
    d_inner_low, small, small_theirs, tiny, own = refs[:5]
    sends, refs = refs[5 : 4 + parts], refs[4 + parts :]
    padded, front, d_both = refs
    tokens, chans = d_scan.shape[1:]
    quarter = own.shape[2]
    taps = conv_w.shape[0]
    m = pl.program_id(0)

    @pl.when(m == 0)
    def _():
        padded[tokens:, :] = jnp.zeros((GROUP, chans), F32)
        front[:GROUP, :] = jnp.zeros((GROUP, chans), F32)
        small[...] = jnp.zeros(small.shape, F32)
        tiny[...] = jnp.zeros(tiny.shape, F32)

    proj = projs[0][0]
    for other in projs[1:]:
        proj = proj + other[0].astype(F32)
    d_proj = proj.astype(BF16)
    count = d_proj.shape[0]
    d_u = d_scan[0] + contract(d_proj, xw_t[...], 0, 0)
    small[:count, :] += jnp.dot(d_proj, u_act[0].astype(BF16), preferred_element_type=F32)
    conv = summed[0]
    sig = sigmoid(conv)
    d_conv = d_u * (sig * (1.0 + conv * (1.0 - sig)))
    padded[:tokens, :] = d_conv
    front[GROUP:, :] = inner[0]
    d_inner = 0.0
    for j in range(taps):
        d_inner = d_inner + conv_w[j : j + 1, :] * padded[pl.ds(taps - 1 - j, tokens), :]
        small[count + j : count + j + 1, :] += jnp.sum(
            d_conv * front[pl.ds(GROUP - taps + 1 + j, tokens), :], axis=0, keepdims=True
        )
    small[count + taps : count + taps + 1, :] += jnp.sum(d_conv, axis=0, keepdims=True)

    @pl.when(m == pl.num_programs(0) - 1)
    def _():
        small_theirs[...] = small[:, core_half(ids, chans, 1)]

    d_inner_low[0] = d_inner.astype(BF16)
    d_both[:, :chans] = d_inner.astype(BF16)
    d_both[:, chans:] = d_gate[0]
    scale = inv[0][:, :1]
    dots = 0.0
    for k in range(parts):
        cols = pl.ds(pl.multiple_of((ids[0] ^ k) * quarter, LANES), quarter)
        d_norm = contract(d_both[...], w_full[cols, :], 1, 1)
        if k == 0:
            own[0] = d_norm
        else:
            sends[k - 1][0] = d_norm.astype(BF16)
        along = d_norm * xs[k][0].astype(F32)
        tiny[0:1, cols] += jnp.sum(along * scale, axis=0, keepdims=True)
        weighted = along * gain[:, cols]
        for c in range(0, quarter, LANES):
            dots = dots + weighted[:, c : c + LANES]
    dots = jnp.sum(jnp.transpose(dots), axis=0, keepdims=True)
    tiny[1:2, pl.ds(pl.multiple_of(m * tokens, LANES), tokens)] = dots


def grad_kernel(chips, pairs, ids, *refs):
    lefts, rights, (mine, theirs) = refs[:pairs], refs[pairs : 2 * pairs], refs[2 * pairs :]
    wide = rights[0].shape[1]
    for p, (left, right) in enumerate(zip(lefts, rights)):
        at = slice(p * wide, (p + 1) * wide)
        if chips == 0:
            mine[:, at] = contract(left[...], right[...], 0, 0)
            continue
        rows = mine.shape[1]
        for side, out in enumerate((theirs, mine)):
            for j in range(chips):
                index = (ids[1] ^ (2 * j)) ^ (1 - side)
                cols = pl.ds(pl.multiple_of(index * rows, LANES), rows)
                out[j, :, at] = contract(left[:, cols], right[...], 0, 0).astype(out.dtype)


def merge_kernel(step, row, ids, mine, got, small, small_got, *refs):
    tinies, (own, part, *sends) = (refs[:2], refs[2:]) if row else ((), refs)
    rows = mine.shape[1]
    chans = small.shape[1]
    half = chans // 2
    part[...] = small[:, core_half(ids, chans)] + small_got[...]
    if row:
        for i in range(tinies[0].shape[1] // chans):
            cols = pl.ds(pl.multiple_of((ids[1] & 1) * half, LANES) + i * chans, half)
            part[row + i : row + i + 1, :] = tinies[0][0:1, cols] + tinies[1][0:1, cols]
    own[...] = mine[0].astype(F32) + got[0].astype(F32)
    pieces = part.shape[0] // step
    for j, send in enumerate(sends):
        send[:rows, :] = (mine[j + 1].astype(F32) + got[j + 1].astype(F32)).astype(BF16)
        for c in range(pieces):
            send[rows:, c * half : (c + 1) * half] = part[c * step : (c + 1) * step, :].astype(BF16)
        if pieces * half < send.shape[1]:
            send[rows:, pieces * half :] = jnp.zeros((step, send.shape[1] - pieces * half), BF16)


def add_received(step, own, part, gots, half):
    rows = own.shape[0]
    total = own[...]
    for got in gots:
        total = total + got[:rows, :].astype(F32)
    lanes = part.shape[1]
    for c in range(part.shape[0] // step):
        piece = part[c * step : (c + 1) * step, :]
        for got in gots:
            piece = piece + got[rows:, c * lanes : (c + 1) * lanes].astype(F32)
        half[c * step : (c + 1) * step, :] = piece
    return total


def final_early_kernel(step, own, part, *refs):
    gots, (grad_gate, grad_out, half) = refs[:-3], refs[-3:]
    total = add_received(step, own, part, gots, half)
    wide = grad_gate.shape[1]
    grad_gate[...] = total[:, :wide]
    grad_out[...] = jnp.transpose(total[:, wide:])


def final_late_kernel(step, own, part, grad_gate, *refs):
    gots, (grad_in, half) = refs[:-2], refs[-2:]
    grad_in[:, 0, :] = add_received(step, own, part, gots, half)
    grad_in[:, 1, :] = grad_gate[...]


def outputs_kernel(
    ids, scan_half, scan_got, post_half, post_got, gain, x_w, dt_w, dt_b, conv_w, conv_b, a_log, skip, scan, post
):
    chans = scan.shape[1]
    for full, half, got in ((scan, scan_half, scan_got), (post, post_half, post_got)):
        full[:, core_half(ids, chans)] = half[...]
        full[:, core_half(ids, chans, 1)] = got[...]
    rank = dt_w.shape[0]
    nstate = a_log.shape[0]
    count = x_w.shape[0]
    taps = conv_w.shape[0]
    dt_w[...] = scan[:rank, :]
    a_log[...] = scan[rank : rank + nstate, :]
    dt_b[...] = scan[rank + nstate : rank + nstate + 1, :]
    skip[...] = scan[rank + nstate + 1 : rank + nstate + 2, :]
    x_w[...] = post[:count, :]
    conv_w[...] = post[count : count + taps, :]
    conv_b[...] = post[count + taps : count + taps + 1, :]
    for i in range(gain.shape[1] // chans):
        row = count + taps + 1 + i
        gain[:, i * chans : (i + 1) * chans] = post[row : row + 1, :]


def whole(shape):
    return pl.BlockSpec(shape, lambda *_: (0,) * len(shape))


SMEM = pl.BlockSpec(memory_space=pltpu.SMEM)


def params(grid, mib=64):
    return pltpu.CompilerParams(
        dimension_semantics=("arbitrary",) * grid, vmem_limit_bytes=mib * 1024 * 1024
    )


def cost(micros):
    return pl.CostEstimate(flops=int(micros * 1.15e9), bytes_accessed=0, transcendentals=0)


def struct(shape, dtype):
    return jax.ShapeDtypeStruct(shape, dtype)


def run_pre(ids, xs, ws, gain, conv_w, conv_b, xw_t):
    micro, tokens, quarter = xs[0].shape
    width = gain.shape[1]
    chans = conv_w.shape[1]
    count = xw_t.shape[0]
    per = lambda *tail: pl.BlockSpec((1,) + tail, lambda m: (m,) + (0,) * len(tail))
    return pl.pallas_call(
        partial(pre_kernel, len(xs), len(ws)),
        grid=(micro,),
        in_specs=[SMEM]
        + [per(tokens, quarter)] * len(xs)
        + [whole(w.shape) for w in ws]
        + [whole(gain.shape), whole(conv_w.shape), whole(conv_b.shape), whole(xw_t.shape)],
        out_specs=[
            per(tokens, width),
            whole((width, ws[0].shape[1])),
            per(tokens, chans),
            per(tokens, chans),
            per(tokens, chans),
            per(tokens, chans),
            per(tokens, LANES),
            per(count, tokens),
            per(count, tokens),
        ],
        out_shape=[
            struct((micro, tokens, width), BF16),
            struct((width, ws[0].shape[1]), BF16),
            struct((micro, tokens, chans), F32),
            struct((micro, tokens, chans), F32),
            struct((micro, tokens, chans), F32),
            struct((micro, tokens, chans), F32),
            struct((micro, tokens, LANES), F32),
            struct((micro, count, tokens), F32),
            struct((micro, count, tokens), BF16),
        ],
        scratch_shapes=[pltpu.VMEM((tokens + GROUP, chans), F32)],
        compiler_params=params(1),
        cost_estimate=cost(7),
        name="pre",
    )(ids, *xs, *ws, gain, conv_w, conv_b, xw_t)


def run_fwd(ids, lens, projs, w_full, u_act, gate, dt_w, dt_b, a_log, skip):
    micro, tokens, chans = u_act.shape
    parts = len(projs)
    width = w_full.shape[0]
    quarter = width // parts
    count = projs[0].shape[1]
    nstate = a_log.shape[0]
    span = min(LANES, tokens)
    rows = lambda *tail: pl.BlockSpec((1, span) + tail, lambda m, b: (m, b) + (0,) * len(tail))
    return pl.pallas_call(
        partial(fwd_kernel, parts),
        grid=(micro, tokens // span),
        in_specs=[SMEM, SMEM]
        + [pl.BlockSpec((1, count, span), lambda m, b: (m, 0, b))] * parts
        + [pl.BlockSpec((width, chans), lambda m, b: (0, 2)), rows(chans), rows(chans)]
        + [whole(v.shape) for v in (dt_w, dt_b, a_log, skip)],
        out_specs=[
            rows(chans),
            rows(chans),
            rows(chans),
            pl.BlockSpec((1, 1, nstate, chans), lambda m, b: (m, b, 0, 0)),
            pl.BlockSpec((1, span * nstate, chans), lambda m, b: (m, b, 0)),
            pl.BlockSpec((1, span * nstate, 2 * LANES), lambda m, b: (m, b, 0)),
        ]
        + [rows(quarter)] * parts,
        out_shape=[
            struct((micro, tokens, chans), F32),
            struct((micro, tokens, chans), F32),
            struct((micro, tokens, chans), BF16),
            struct((micro, tokens // span, nstate, chans), F32),
            struct((micro, tokens * nstate, chans), BF16),
            struct((micro, tokens * nstate, 2 * LANES), F32),
            struct((micro, tokens, quarter), F32),
        ]
        + [struct((micro, tokens, quarter), BF16)] * (parts - 1),
        scratch_shapes=[pltpu.VMEM((span, chans), F32)] * 2
        + [pltpu.VMEM((chans // LANES, 2 * GROUP * GROUP, LANES), F32), pltpu.VMEM((nstate, chans), F32)],
        compiler_params=params(2),
        cost_estimate=cost(16),
        name="scan_forward",
    )(ids, lens, *projs, w_full, u_act, gate, dt_w, dt_b, a_log, skip)


def run_bwd(ids, lens, projs, cots, w_full, u_act, gate, dt, y_rows, edge, low_state, vectors, dt_w, a_log, skip):
    micro, tokens, chans = u_act.shape
    parts = len(projs)
    width = w_full.shape[0]
    quarter = cots[0].shape[2]
    count = projs[0].shape[1]
    nstate = a_log.shape[0]
    rank = dt_w.shape[0]
    span = min(LANES, tokens)
    blocks = tokens // span
    small = SCAN_STEP * -(-(rank + nstate + 2) // SCAN_STEP)
    rows = lambda *tail: pl.BlockSpec(
        (1, span) + tail, lambda m, b: (m, blocks - 1 - b) + (0,) * len(tail)
    )
    proj = pl.BlockSpec((1, count, span), lambda m, b: (m, 0, blocks - 1 - b))
    return pl.pallas_call(
        partial(bwd_kernel, parts),
        grid=(micro, blocks),
        in_specs=[SMEM, SMEM]
        + [proj] * parts
        + [rows(quarter)] * parts
        + [pl.BlockSpec((width, chans), lambda m, b: (0, 2)), rows(chans), rows(chans), rows(chans), rows(chans)]
        + [pl.BlockSpec((1, 1, nstate, chans), lambda m, b: (m, blocks - 1 - b, 0, 0))]
        + [pl.BlockSpec((1, span * nstate, chans), lambda m, b: (m, blocks - 1 - b, 0))]
        + [pl.BlockSpec((1, span * nstate, 2 * LANES), lambda m, b: (m, blocks - 1 - b, 0))]
        + [whole(v.shape) for v in (dt_w, a_log, skip)],
        out_specs=[rows(width), proj, proj, rows(chans), rows(chans), whole((small, chans)), whole((small, chans // 2))],
        out_shape=[
            struct((micro, tokens, width), BF16),
            struct((micro, count, tokens), F32),
            struct((micro, count, tokens), BF16),
            struct((micro, tokens, chans), F32),
            struct((micro, tokens, chans), BF16),
            struct((small, chans), F32),
            struct((small, chans // 2), F32),
        ],
        scratch_shapes=[pltpu.VMEM((span, chans), F32)] * 4
        + [pltpu.VMEM((chans // LANES, 2 * GROUP * GROUP, LANES), F32)] * 2
        + [pltpu.VMEM((nstate, chans), F32)] * 2
        + [pltpu.VMEM((span * nstate, chans), BF16)],
        compiler_params=params(2),
        cost_estimate=cost(21),
        name="scan_backward",
    )(ids, lens, *projs, *cots, w_full, u_act, gate, dt, y_rows, edge, low_state, vectors, dt_w, a_log, skip)


def run_post(ids, projs, xs, d_scan, d_gate, u_act, summed, inner, inv, w_full, gain, xw_t, conv_w):
    micro, tokens, chans = u_act.shape
    parts = len(projs)
    width = w_full.shape[0]
    quarter = width // parts
    count = projs[0].shape[1]
    taps = conv_w.shape[0]
    small = POST_STEP * -(-(count + taps + 1 + width // chans) // POST_STEP)
    lanes = max(width, LANES * -(-micro * tokens // LANES))
    per = lambda *tail: pl.BlockSpec((1,) + tail, lambda m: (m,) + (0,) * len(tail))
    return pl.pallas_call(
        partial(post_kernel, parts),
        grid=(micro,),
        in_specs=[SMEM]
        + [per(count, tokens)] * parts
        + [per(tokens, quarter)] * parts
        + [per(tokens, chans)] * 5
        + [per(tokens, LANES)]
        + [whole((width, 2 * chans))]
        + [whole(v.shape) for v in (gain, xw_t, conv_w)],
        out_specs=[
            per(tokens, chans),
            whole((small, chans)),
            whole((small, chans // 2)),
            whole((GROUP, lanes)),
        ]
        + [per(tokens, quarter)] * parts,
        out_shape=[
            struct((micro, tokens, chans), BF16),
            struct((small, chans), F32),
            struct((small, chans // 2), F32),
            struct((GROUP, lanes), F32),
            struct((micro, tokens, quarter), F32),
        ]
        + [struct((micro, tokens, quarter), BF16)] * (parts - 1),
        scratch_shapes=[pltpu.VMEM((tokens + GROUP, chans), F32)] * 2
        + [pltpu.VMEM((tokens, 2 * chans), BF16)],
        compiler_params=params(1),
        cost_estimate=cost(20),
        name="post",
    )(ids, *projs, *xs, d_scan, d_gate, u_act, summed, inner, inv, w_full, gain, xw_t, conv_w)


def run_grad(name, ids, lefts, rights, shape, chips):
    if chips == 0:
        outs = [struct(shape, F32), struct((GROUP, LANES), BF16)]
    else:
        outs = [struct((chips,) + shape, BF16)] * 2
    flat = lambda v: v.reshape(-1, v.shape[-1])
    return run_local(
        partial(grad_kernel, chips, len(lefts)), name, outs, ids, *map(flat, lefts), *map(flat, rights)
    )


VMEM = pl.BlockSpec(memory_space=pltpu.VMEM)


def run_local(kernel, name, outs, ids, *operands, scratch=()):
    return pl.pallas_call(
        kernel,
        grid=(1,),
        in_specs=([SMEM] if ids is not None else []) + [whole(v.shape) for v in operands],
        out_specs=[whole(v.shape) for v in outs],
        out_shape=outs,
        scratch_shapes=list(scratch),
        compiler_params=pltpu.CompilerParams(vmem_limit_bytes=64 * 1024 * 1024),
        cost_estimate=cost(0.3),
        name=name,
    )(*(() if ids is None else (ids,)), *operands)


def after(value, *earlier):
    return lax.optimization_barrier((value, earlier))[0]


def others(value, axis, step=1):
    count = lax.axis_size(axis)
    return [swap(value, axis, mask) for mask in range(step, count, step)]


def gather_line(value, axis, early=()):
    count = lax.axis_size(axis)
    got = {0: value}
    mask = count // 2
    while mask:
        for known in sorted(got):
            fresh = swap(got[known], axis, mask) if known or mask not in early else early[mask]
            got[known | mask] = fresh
        mask //= 2
    return [got[k] for k in range(count)]


def with_sibling(blocks):
    return blocks + [swap(block, "dp", 1) for block in blocks]


def sum_all(value):
    core = lax.rem(lax.axis_index("dp"), 2)
    half = value.shape[0] // 2
    halves = value.reshape((2, half) + value.shape[1:])
    mine = lax.dynamic_index_in_dim(halves, core, 0, keepdims=False)
    theirs = lax.dynamic_index_in_dim(halves, 1 - core, 0, keepdims=False)
    total = mine + swap(theirs, "dp", 1)
    for got in others(total, "dp", 2):
        total = total + got
    other = swap(total, "dp", 1)
    first = jnp.where(core == 0, total, other)
    second = jnp.where(core == 0, other, total)
    return jnp.concatenate([first, second], axis=0)


def body(
    tokens,
    lengths,
    norm_gain,
    in_weight,
    x_weight,
    dt_weight,
    dt_bias,
    conv_weight,
    conv_bias,
    a_log,
    skip,
    out_weight,
    cotangent,
):
    micro, seq, quarter = tokens.shape
    chans = in_weight.shape[2]
    width = norm_gain.shape[0]
    dps = lax.axis_size("dp")
    rank = dt_weight.shape[0]
    nstate = a_log.shape[0]
    taps = conv_weight.shape[0]
    count = x_weight.shape[1]
    ids = jnp.stack([lax.axis_index("tensor"), lax.axis_index("dp")]).astype(jnp.int32)
    lens = lengths[:, 0]
    gain = norm_gain[None]
    xw_t = x_weight.T
    in_rows = in_weight.reshape(in_weight.shape[0], 2 * chans)
    by_block = in_rows.shape[0] % LANES == 0
    chips = dps // 2 if by_block else 0
    parts = lax.axis_size("tensor")
    weight = jnp.concatenate([in_rows, out_weight.T], axis=1)

    xs = gather_line(tokens, "tensor")
    if by_block:
        mine = [weight] + [
            swap(weight, "dp", mask) for mask in range(2, dps, 2)
        ]
        blocks = with_sibling(after(mine, *xs))
    else:
        blocks = [lax.all_gather(weight, "dp", axis=0, tiled=True)]
    normed, w_full, inner, summed, u_act, gate, inv, proj, proj_low = run_pre(
        ids, xs, blocks, gain, conv_weight, conv_bias[None], xw_t
    )
    cot_early = after(cotangent, *xs)
    early = {mask: swap(cot_early, "tensor", mask) for mask in (parts // 2, 1)}
    projs = [proj] + others(proj_low, "tensor")
    far = after(early[parts // 2], *projs)
    early[parts // 2] = far
    cots = gather_line(cotangent, "tensor", early)
    dt, y_rows, gated, edge, low_state, vectors, own_out, *out_terms = run_fwd(
        ids, lens, projs, w_full, u_act, gate, dt_weight, dt_bias[None], a_log, skip[None]
    )
    out_got = [swap(term, "tensor", k + 1) for k, term in enumerate(out_terms)]
    cot_full, d_proj, d_proj_low, d_scan, d_gate, scan_small, scan_theirs = run_bwd(
        ids, lens, projs, cots, w_full, u_act, gate, dt, y_rows, edge, low_state, vectors, dt_weight, a_log, skip[None]
    )
    d_projs = [d_proj] + others(after(d_proj_low, *out_got), "tensor")
    branch = own_out
    for term in out_got:
        branch = branch + term.astype(F32)
    mixed = (tokens.astype(F32) + branch).astype(BF16)
    rows = weight.shape[0] if chips else width
    early_mine, early_theirs = run_grad(
        "grad_early",
        ids,
        [after(normed, d_projs[1]), cot_full],
        [d_gate, gated],
        (rows, 2 * chans),
        chips,
    )

    def merged(name, step, row, mine, theirs, small, small_theirs, tinies, wide):
        part = struct((small.shape[0], chans // 2), F32)
        own, part, *sends = run_local(
            partial(merge_kernel, step, row),
            name,
            [struct((rows, wide), F32), part] + [struct((rows + step, wide), BF16)] * (chips - 1),
            ids,
            mine,
            swap(theirs, "dp", 1),
            small,
            swap(small_theirs, "dp", 1),
            *tinies,
        )
        return own, part, sends

    if chips:
        early_own, early_part, sends = merged(
            "merge_early", SCAN_STEP, 0, early_mine, early_theirs, scan_small, scan_theirs, (), 2 * chans
        )
        early_gots = [swap(send, "dp", 2 * (j + 1)) for j, send in enumerate(sends)]
    d_inner, small, small_theirs, tiny, own_norm, *norm_terms = run_post(
        ids, d_projs, xs, d_scan, d_gate, u_act, summed, inner, inv, w_full, gain, xw_t, conv_weight
    )
    tiny_got = others(tiny, "tensor")
    near = parts // 2
    halves = [own_norm] + norm_terms
    passed = [swap(halves[k], "tensor", k) for k in range(1, near)]
    relayed = [swap(halves[near + k], "tensor", k) for k in range(1, near)]
    far = halves[near].astype(F32)
    for got in relayed:
        far = far + got.astype(F32)
    far = far.astype(BF16)
    norm_got = passed + [swap(far, "tensor", near)]
    late_mine, late_theirs = run_grad("grad_late", ids, [normed], [d_inner], (rows, chans), chips)
    for got in tiny_got:
        tiny = tiny + got
    row = count + taps + 1
    if chips:
        late_own, late_part, sends = merged(
            "merge_late",
            POST_STEP,
            row,
            after(late_mine, far),
            late_theirs,
            small,
            small_theirs,
            (tiny, swap(tiny, "dp", 1)),
            chans,
        )
        late_gots = [swap(send, "dp", 2 * (j + 1)) for j, send in enumerate(sends)]
        grad_gate, grad_out, scan_half = run_local(
            partial(final_early_kernel, SCAN_STEP),
            "final_early",
            [struct((rows, chans), F32), struct(out_weight.shape, F32), struct(early_part.shape, F32)],
            None,
            early_own,
            early_part,
            *early_gots,
        )
        grad_in, post_half = run_local(
            partial(final_late_kernel, POST_STEP),
            "final_late",
            [struct(in_weight.shape, F32), struct(late_part.shape, F32)],
            None,
            late_own,
            late_part,
            grad_gate,
            *late_gots,
        )
        g_gain, g_x, g_dt, g_dtb, g_conv, g_convb, g_alog, g_skip = run_local(
            outputs_kernel,
            "outputs",
            [
                struct((1, width), F32),
                struct((count, chans), F32),
                struct((rank, chans), F32),
                struct((1, chans), F32),
                struct((taps, chans), F32),
                struct((1, chans), F32),
                struct((nstate, chans), F32),
                struct((1, chans), F32),
            ],
            ids,
            scan_half,
            swap(scan_half, "dp", 1),
            post_half,
            swap(post_half, "dp", 1),
            scratch=[pltpu.VMEM((scan_small.shape[0], chans), F32), pltpu.VMEM((small.shape[0], chans), F32)],
        )
        smalls = (g_gain[0], g_x.T, g_dt, g_dtb[0], g_conv, g_convb[0], g_alog, g_skip[0])
    else:
        grad_inner = lax.psum_scatter(late_mine, "dp", scatter_dimension=0, tiled=True)
        early = lax.psum_scatter(early_mine, "dp", scatter_dimension=0, tiled=True)
        grad_in = jnp.stack([grad_inner, early[:, :chans]], axis=1)
        grad_out = early[:, chans:].T
        scan_small = sum_all(scan_small)
        small = sum_all(lax.dynamic_update_slice_in_dim(small, tiny[0, :width].reshape(-1, chans), row, 0))
        smalls = (
            small[row : row + width // chans].reshape(width),
            small[:count].T,
            scan_small[:rank],
            scan_small[rank + nstate],
            small[count : count + taps],
            small[count + taps],
            scan_small[rank : rank + nstate],
            scan_small[rank + nstate + 1],
        )
    d_norm = own_norm
    for term in norm_got:
        d_norm = d_norm + term.astype(F32)
    scale = inv[:, :, :1]
    dots = tiny[1, : micro * seq].reshape(micro, seq, 1)
    own_gain = lax.dynamic_slice_in_dim(norm_gain, ids[0] * quarter, quarter, 0)
    d_x = scale * (d_norm * own_gain) - tokens.astype(F32) * (scale * scale * scale * dots / width)
    input_grad = cotangent.astype(F32) + d_x
    return (mixed, input_grad, smalls[0], grad_in.reshape(in_weight.shape)) + smalls[1:] + (grad_out,)


def solution(mesh):
    rows = P(None, "dp", "tensor")
    chans = P(None, "tensor")
    return jax.shard_map(
        body,
        mesh=mesh,
        in_specs=(
            rows,
            P(None, "dp"),
            P(),
            P("dp", None, "tensor"),
            P("tensor", None),
            chans,
            P("tensor"),
            chans,
            P("tensor"),
            chans,
            P("tensor"),
            P("tensor", "dp"),
            rows,
        ),
        out_specs=(
            rows,
            rows,
            P(),
            P("dp", None, "tensor"),
            P("tensor", None),
            chans,
            P("tensor"),
            chans,
            P("tensor"),
            chans,
            P("tensor"),
            P("tensor", "dp"),
        ),
        check_vma=False,
    )
```

```python
from functools import partial

import jax
import jax.numpy as jnp
from jax import lax
from jax.experimental import pallas as pl
from jax.experimental.pallas import tpu as pltpu
from jax.sharding import PartitionSpec as P

EPS = 1e-05
F32 = jnp.float32
BF16 = jnp.bfloat16
GROUP = 8
LANES = 128
SCAN_STEP = 32
POST_STEP = 64


def contract(left, right, left_dim, right_dim):
    return lax.dot_general(
        left, right, (((left_dim,), (right_dim,)), ((), ())), preferred_element_type=F32
    )


def sigmoid(v):
    return 1.0 / (1.0 + jnp.exp(-v))


def softplus(v):
    return jnp.maximum(v, 0.0) + jnp.log1p(jnp.exp(-jnp.abs(v)))


def swap(value, axis, mask):
    count = lax.axis_size(axis)
    return lax.ppermute(value, axis, [(i, i ^ mask) for i in range(count)])


def pre_kernel(parts, blocks, ids, *refs):
    xs, refs = refs[:parts], refs[parts:]
    ws, refs = refs[:blocks], refs[blocks:]
    gain, conv_w, conv_b, xw_t = refs[:4]
    normed, w_full, inner, summed, u_act, gate, inv, proj, proj_low, padded = refs[4:]
    quarter = xs[0].shape[2]
    chans = inner.shape[2]

    @pl.when(pl.program_id(0) == 0)
    def _():
        gather_rows(ids, ws, w_full)
        padded[:GROUP, :] = jnp.zeros((GROUP, chans), F32)

    square = 0.0
    for x in xs:
        rows = x[0].astype(F32)
        square = square + jnp.sum(rows * rows, axis=1, keepdims=True)
    scale = lax.rsqrt(square / (parts * quarter) + EPS)
    inv[0] = jnp.broadcast_to(scale, inv.shape[1:])
    for k, x in enumerate(xs):
        cols = pl.ds(pl.multiple_of((ids[0] ^ k) * quarter, LANES), quarter)
        normed[0, :, cols] = (x[0].astype(F32) * scale * gain[:, cols]).astype(BF16)
    both = jnp.dot(normed[0], w_full[:, : 2 * chans], preferred_element_type=F32)
    gate[0] = both[:, chans:]
    inner_in = both[:, :chans]
    inner[0] = inner_in
    tokens = inner_in.shape[0]
    padded[GROUP:, :] = inner_in
    taps = conv_w.shape[0]
    total = jnp.broadcast_to(conv_b[...], inner_in.shape)
    for j in range(taps):
        total = total + conv_w[j : j + 1, :] * padded[pl.ds(GROUP - taps + 1 + j, tokens), :]
    summed[0] = total
    act = total * sigmoid(total)
    u_act[0] = act
    partial_sum = contract(xw_t[...], act.astype(BF16), 1, 1)
    proj[0] = partial_sum
    proj_low[0] = partial_sum.astype(BF16)


def core_half(ids, chans, flip=0):
    half = chans // 2
    return pl.ds(pl.multiple_of(((ids[1] & 1) ^ flip) * half, LANES), half)


def gather_rows(ids, blocks, full):
    if len(blocks) == 1:
        full[...] = blocks[0][...]
        return
    chips = len(blocks) // 2
    for side in range(2):
        for j in range(chips):
            block = blocks[side * chips + j]
            index = (ids[1] ^ (2 * j)) ^ side
            rows = block.shape[0]
            full[pl.ds(pl.multiple_of(index * rows, 16), rows), :] = block[...]


def split(v):
    high = v.astype(BF16)
    return high, (v - high.astype(F32)).astype(BF16)


def spread(left, right, out):
    count, span = left.shape
    lanes = lax.broadcasted_iota(jnp.int32, left.shape, 1)
    shape = (2 * span, 2 * LANES)
    from_left = lax.broadcasted_iota(jnp.int32, shape, 0) < span
    to_left = lax.broadcasted_iota(jnp.int32, shape, 1) < LANES
    ones = jnp.where(from_left == to_left, 1.0, 0.0).astype(BF16)
    rows = []
    for t in range(span):
        pair = [jnp.where(lanes == t, part, 0.0).astype(BF16) for part in (left, right)]
        rows.append(jnp.concatenate(pair, axis=1))
    out[...] = jnp.dot(jnp.concatenate(rows, axis=0), ones, preferred_element_type=F32)


def gather(left, right, count):
    span = right.shape[0]
    lanes = lax.broadcasted_iota(jnp.int32, (count, span), 1)
    wide = contract(left[...], right, 1, 1)
    totals = [jnp.zeros((count, span), F32)] * 4
    for t in range(span):
        totals[t % 4] = jnp.where(lanes == t, wide[t * count : (t + 1) * count, :], totals[t % 4])
    return (totals[0] + totals[1]) + (totals[2] + totals[3])


def sigmoid_of_softplus(step):
    series = step * (1.0 - step * (0.5 - step * (1.0 / 6.0 - step * (1.0 / 24.0))))
    return jnp.where(step < 0.05, series, 1.0 - jnp.exp(-step))


def fold(pend, out, start, half):
    for g in range(pend.shape[0]):
        total = pend[g, pl.ds(half * GROUP * GROUP, GROUP, stride=GROUP), :]
        for s in range(1, GROUP):
            total = total + pend[g, pl.ds(half * GROUP * GROUP + s, GROUP, stride=GROUP), :]
        out[pl.ds(start, GROUP), g * LANES : (g + 1) * LANES] = total


def fwd_kernel(parts, ids, lens, *refs):
    projs, refs = refs[:parts], refs[parts:]
    w_out, u_act, gate, dt_w, dt_b, a_log, skip = refs[:7]
    refs = refs[7:]
    dt, y_rows, gated, edge, low_state, vectors, own = refs[:7]
    sends, refs = refs[7 : 6 + parts], refs[6 + parts :]
    dtu, y, pend, carry = refs
    span, chans = dtu.shape
    nstate = a_log.shape[0]
    rank = dt_w.shape[0]
    block = pl.program_id(1)
    groups = chans // LANES

    @pl.when(block == 0)
    def _():
        carry[...] = jnp.zeros(carry.shape, F32)

    proj = projs[0][0]
    for other in projs[1:]:
        proj = proj + other[0].astype(F32)
    lin = contract(proj[:rank].astype(BF16), dt_w[...], 0, 0) + dt_b[...]
    step = softplus(lin)
    dt[0] = step
    dtu[...] = step * u_act[0]
    spread(proj[rank : rank + nstate], proj[rank + nstate :], vectors.at[0])
    rate = -jnp.exp(a_log[...])
    lane = [slice(g * LANES, (g + 1) * LANES) for g in range(groups)]

    edge[0, 0] = carry[...]

    def steps(i, state):
        state = list(state)
        for half in range(2):
            start = pl.multiple_of((2 * i + half) * GROUP, GROUP)
            dt_rows = dt[0, pl.ds(start, GROUP), :]
            dtu_rows = dtu[pl.ds(start, GROUP), :]
            for k in range(GROUP):
                at = pl.ds(pl.multiple_of((start + k) * nstate, nstate), nstate)
                b_t = vectors[0, at, :LANES]
                c_t = vectors[0, at, LANES:]
                rows = pl.ds((half * GROUP + k) * GROUP, GROUP)
                for g in range(groups):
                    dt_t = dt_rows[k : k + 1, lane[g]]
                    dtu_t = dtu_rows[k : k + 1, lane[g]]
                    new = jnp.exp(dt_t * rate[:, lane[g]]) * state[g] + dtu_t * b_t
                    state[g] = new
                    low_state[0, at, lane[g]] = new.astype(BF16)
                    term = c_t * new
                    pend[g, rows, :] = sum(term[s : s + GROUP] for s in range(0, nstate, GROUP))
            fold(pend, y, start, half)
        return tuple(state)

    last = lax.fori_loop(0, span // (2 * GROUP), steps, tuple(carry[:, l] for l in lane))
    for g in range(groups):
        carry[:, lane[g]] = last[g]
    rows = y[...] + skip[...] * u_act[0]
    y_rows[0] = rows
    gate_in = gate[0]
    position = block * span + lax.broadcasted_iota(jnp.int32, (span, 1), 0)
    live = (position < lens[pl.program_id(0)]).astype(F32)
    low = (rows * (gate_in * sigmoid(gate_in)) * live).astype(BF16)
    gated[0] = low
    quarter = own.shape[2]
    for k in range(parts):
        rows = pl.ds(pl.multiple_of((ids[0] ^ k) * quarter, LANES), quarter)
        term = contract(low, w_out[rows, :], 1, 1)
        if k == 0:
            own[0] = term
        else:
            sends[k - 1][0] = term.astype(BF16)


def bwd_kernel(parts, ids, lens, *refs):
    projs, refs = refs[:parts], refs[parts:]
    cots, refs = refs[:parts], refs[parts:]
    w_full, u_act, gate, dt, y_rows, edge, low_state, vectors, dt_w, a_log, skip = refs[:11]
    refs = refs[11:]
    cot_full, d_proj, d_proj_low, d_scan, d_gate, small, small_theirs = refs[:7]
    dtu, d_y, d_dtu, d_dta, pend_q, pend_r, carry, g_rate, low_grad = refs[7:]
    span, chans = dtu.shape
    nstate = a_log.shape[0]
    rank = dt_w.shape[0]
    first = (pl.program_id(0) == 0) & (pl.program_id(1) == 0)
    last = (pl.program_id(0) == pl.num_programs(0) - 1) & (pl.program_id(1) == pl.num_programs(1) - 1)
    block = pl.num_programs(1) - 1 - pl.program_id(1)
    groups = chans // LANES
    quarter = cots[0].shape[2]
    lane = [slice(g * LANES, (g + 1) * LANES) for g in range(groups)]

    @pl.when(first)
    def _():
        small[...] = jnp.zeros(small.shape, F32)
        g_rate[...] = jnp.zeros(g_rate.shape, F32)

    @pl.when(pl.program_id(1) == 0)
    def _():
        carry[...] = jnp.zeros(carry.shape, F32)

    for k, cot in enumerate(cots):
        cols = pl.ds(pl.multiple_of((ids[0] ^ k) * quarter, LANES), quarter)
        cot_full[0, :, cols] = cot[0]
    d_gated = jnp.dot(cot_full[0], w_full[...], preferred_element_type=F32)

    proj = projs[0][0]
    for other in projs[1:]:
        proj = proj + other[0].astype(F32)
    dt_low = proj[:rank].astype(BF16)
    u = u_act[0]
    step = dt[0]
    dtu[...] = step * u
    gate_in = gate[0]
    gate_sig = sigmoid(gate_in)
    position = block * span + lax.broadcasted_iota(jnp.int32, (span, 1), 0)
    live = (position < lens[pl.program_id(0)]).astype(F32)
    d_live = d_gated * live
    d_rows = d_live * (gate_in * gate_sig)
    d_y[...] = d_rows
    d_gate[0] = (d_live * y_rows[0] * (gate_sig * (1.0 + gate_in * (1.0 - gate_sig)))).astype(BF16)
    rate = -jnp.exp(a_log[...])
    count = span // (2 * GROUP)

    def steps(i, loop):
        run, acc = list(loop[0]), list(loop[1])
        for half in reversed(range(2)):
            start = pl.multiple_of((2 * (count - 1 - i) + half) * GROUP, GROUP)
            dt_rows = dt[0, pl.ds(start, GROUP), :]
            dy_rows = d_y[pl.ds(start, GROUP), :]
            for k in reversed(range(GROUP)):
                at = pl.ds(pl.multiple_of((start + k) * nstate, nstate), nstate)
                b_t = vectors[0, at, :LANES]
                c_t = vectors[0, at, LANES:]
                rows = pl.ds((half * GROUP + k) * GROUP, GROUP)
                before = start + k - 1
                if half == 0 and k == 0:
                    before = jnp.maximum(before, 0)
                before = pl.ds(pl.multiple_of(before * nstate, nstate), nstate)
                for g in range(groups):
                    old = low_state[0, before, lane[g]].astype(F32)
                    if half == 0 and k == 0:
                        old = jnp.where(start == 0, edge[0, 0, :, lane[g]], old)
                    dt_t = dt_rows[k : k + 1, lane[g]]
                    dy_t = dy_rows[k : k + 1, lane[g]]
                    d_state = run[g] + c_t * dy_t
                    low_grad[at, lane[g]] = d_state.astype(BF16)
                    decayed = jnp.exp(dt_t * rate[:, lane[g]]) * d_state
                    run[g] = decayed
                    d_exp = decayed * old
                    acc[g] = acc[g] + d_exp * dt_t
                    term_q = d_exp * rate[:, lane[g]]
                    term_r = d_state * b_t
                    pend_q[g, rows, :] = sum(term_q[s : s + GROUP] for s in range(0, nstate, GROUP))
                    pend_r[g, rows, :] = sum(term_r[s : s + GROUP] for s in range(0, nstate, GROUP))
            fold(pend_q, d_dta, start, half)
            fold(pend_r, d_dtu, start, half)
        return tuple(run), tuple(acc)

    run, acc = lax.fori_loop(
        0,
        count,
        steps,
        (tuple(carry[:, l] for l in lane), tuple(g_rate[:, l] for l in lane)),
    )
    d_b = gather(low_grad, dtu[...].astype(BF16), nstate)
    d_c = gather(low_state.at[0], d_rows.astype(BF16), nstate)
    for g in range(groups):
        carry[:, lane[g]] = run[g]
        g_rate[:, lane[g]] = acc[g]
    d_lin = (d_dtu[...] * u + d_dta[...]) * sigmoid_of_softplus(step)
    d_scan[0] = d_dtu[...] * step + d_rows * skip[...]
    d_low = d_lin.astype(BF16)
    full = jnp.concatenate([contract(dt_w[...], d_low, 1, 1), d_b, d_c], axis=0)
    d_proj[0] = full
    d_proj_low[0] = full.astype(BF16)
    small[:rank, :] += jnp.dot(dt_low, d_low, preferred_element_type=F32)
    row = rank + nstate
    small[row : row + 1, :] += jnp.sum(d_lin, axis=0, keepdims=True)
    small[row + 1 : row + 2, :] += jnp.sum(d_rows * u, axis=0, keepdims=True)

    @pl.when(last)
    def _():
        small[rank : rank + nstate, :] = g_rate[...] * rate
        small_theirs[...] = small[:, core_half(ids, chans, 1)]


def post_kernel(parts, ids, *refs):
    projs, refs = refs[:parts], refs[parts:]
    xs, refs = refs[:parts], refs[parts:]
    d_scan, d_gate, u_act, summed, inner, inv, w_full, gain, xw_t, conv_w = refs[:10]
    refs = refs[10:]
    d_inner_low, small, small_theirs, tiny, own = refs[:5]
    sends, refs = refs[5 : 4 + parts], refs[4 + parts :]
    padded, front, d_both = refs
    tokens, chans = d_scan.shape[1:]
    quarter = own.shape[2]
    taps = conv_w.shape[0]
    m = pl.program_id(0)

    @pl.when(m == 0)
    def _():
        padded[tokens:, :] = jnp.zeros((GROUP, chans), F32)
        front[:GROUP, :] = jnp.zeros((GROUP, chans), F32)
        small[...] = jnp.zeros(small.shape, F32)
        tiny[...] = jnp.zeros(tiny.shape, F32)

    proj = projs[0][0]
    for other in projs[1:]:
        proj = proj + other[0].astype(F32)
    d_proj = proj.astype(BF16)
    count = d_proj.shape[0]
    d_u = d_scan[0] + contract(d_proj, xw_t[...], 0, 0)
    small[:count, :] += jnp.dot(d_proj, u_act[0].astype(BF16), preferred_element_type=F32)
    conv = summed[0]
    sig = sigmoid(conv)
    d_conv = d_u * (sig * (1.0 + conv * (1.0 - sig)))
    padded[:tokens, :] = d_conv
    front[GROUP:, :] = inner[0]
    d_inner = 0.0
    for j in range(taps):
        d_inner = d_inner + conv_w[j : j + 1, :] * padded[pl.ds(taps - 1 - j, tokens), :]
        small[count + j : count + j + 1, :] += jnp.sum(
            d_conv * front[pl.ds(GROUP - taps + 1 + j, tokens), :], axis=0, keepdims=True
        )
    small[count + taps : count + taps + 1, :] += jnp.sum(d_conv, axis=0, keepdims=True)

    @pl.when(m == pl.num_programs(0) - 1)
    def _():
        small_theirs[...] = small[:, core_half(ids, chans, 1)]

    d_inner_low[0] = d_inner.astype(BF16)
    d_both[:, :chans] = d_inner.astype(BF16)
    d_both[:, chans:] = d_gate[0]
    scale = inv[0][:, :1]
    dots = 0.0
    for k in range(parts):
        cols = pl.ds(pl.multiple_of((ids[0] ^ k) * quarter, LANES), quarter)
        d_norm = contract(d_both[...], w_full[cols, :], 1, 1)
        if k == 0:
            own[0] = d_norm
        else:
            sends[k - 1][0] = d_norm.astype(BF16)
        along = d_norm * xs[k][0].astype(F32)
        tiny[0:1, cols] += jnp.sum(along * scale, axis=0, keepdims=True)
        weighted = along * gain[:, cols]
        for c in range(0, quarter, LANES):
            dots = dots + weighted[:, c : c + LANES]
    dots = jnp.sum(jnp.transpose(dots), axis=0, keepdims=True)
    tiny[1:2, pl.ds(pl.multiple_of(m * tokens, LANES), tokens)] = dots


def grad_kernel(chips, pairs, ids, *refs):
    lefts, rights, (mine, theirs) = refs[:pairs], refs[pairs : 2 * pairs], refs[2 * pairs :]
    wide = rights[0].shape[1]
    for p, (left, right) in enumerate(zip(lefts, rights)):
        at = slice(p * wide, (p + 1) * wide)
        if chips == 0:
            mine[:, at] = contract(left[...], right[...], 0, 0)
            continue
        rows = mine.shape[1]
        for side, out in enumerate((theirs, mine)):
            for j in range(chips):
                index = (ids[1] ^ (2 * j)) ^ (1 - side)
                cols = pl.ds(pl.multiple_of(index * rows, LANES), rows)
                out[j, :, at] = contract(left[:, cols], right[...], 0, 0).astype(out.dtype)


def merge_kernel(step, row, ids, mine, got, small, small_got, *refs):
    tinies, (own, part, *sends) = (refs[:2], refs[2:]) if row else ((), refs)
    rows = mine.shape[1]
    chans = small.shape[1]
    half = chans // 2
    part[...] = small[:, core_half(ids, chans)] + small_got[...]
    if row:
        for i in range(tinies[0].shape[1] // chans):
            cols = pl.ds(pl.multiple_of((ids[1] & 1) * half, LANES) + i * chans, half)
            part[row + i : row + i + 1, :] = tinies[0][0:1, cols] + tinies[1][0:1, cols]
    own[...] = mine[0].astype(F32) + got[0].astype(F32)
    pieces = part.shape[0] // step
    for j, send in enumerate(sends):
        send[:rows, :] = (mine[j + 1].astype(F32) + got[j + 1].astype(F32)).astype(BF16)
        for c in range(pieces):
            send[rows:, c * half : (c + 1) * half] = part[c * step : (c + 1) * step, :].astype(BF16)
        if pieces * half < send.shape[1]:
            send[rows:, pieces * half :] = jnp.zeros((step, send.shape[1] - pieces * half), BF16)


def add_received(step, own, part, gots, half):
    rows = own.shape[0]
    total = own[...]
    for got in gots:
        total = total + got[:rows, :].astype(F32)
    lanes = part.shape[1]
    for c in range(part.shape[0] // step):
        piece = part[c * step : (c + 1) * step, :]
        for got in gots:
            piece = piece + got[rows:, c * lanes : (c + 1) * lanes].astype(F32)
        half[c * step : (c + 1) * step, :] = piece
    return total


def final_early_kernel(step, own, part, *refs):
    gots, (grad_gate, grad_out, half) = refs[:-3], refs[-3:]
    total = add_received(step, own, part, gots, half)
    wide = grad_gate.shape[1]
    grad_gate[...] = total[:, :wide]
    grad_out[...] = jnp.transpose(total[:, wide:])


def final_late_kernel(step, own, part, grad_gate, *refs):
    gots, (grad_in, half) = refs[:-2], refs[-2:]
    grad_in[:, 0, :] = add_received(step, own, part, gots, half)
    grad_in[:, 1, :] = grad_gate[...]


def outputs_kernel(
    ids, scan_half, scan_got, post_half, post_got, gain, x_w, dt_w, dt_b, conv_w, conv_b, a_log, skip, scan, post
):
    chans = scan.shape[1]
    for full, half, got in ((scan, scan_half, scan_got), (post, post_half, post_got)):
        full[:, core_half(ids, chans)] = half[...]
        full[:, core_half(ids, chans, 1)] = got[...]
    rank = dt_w.shape[0]
    nstate = a_log.shape[0]
    count = x_w.shape[0]
    taps = conv_w.shape[0]
    dt_w[...] = scan[:rank, :]
    a_log[...] = scan[rank : rank + nstate, :]
    dt_b[...] = scan[rank + nstate : rank + nstate + 1, :]
    skip[...] = scan[rank + nstate + 1 : rank + nstate + 2, :]
    x_w[...] = post[:count, :]
    conv_w[...] = post[count : count + taps, :]
    conv_b[...] = post[count + taps : count + taps + 1, :]
    for i in range(gain.shape[1] // chans):
        row = count + taps + 1 + i
        gain[:, i * chans : (i + 1) * chans] = post[row : row + 1, :]


def whole(shape):
    return pl.BlockSpec(shape, lambda *_: (0,) * len(shape))


SMEM = pl.BlockSpec(memory_space=pltpu.SMEM)


def params(grid, mib=64):
    return pltpu.CompilerParams(
        dimension_semantics=("arbitrary",) * grid, vmem_limit_bytes=mib * 1024 * 1024
    )


def cost(micros):
    return pl.CostEstimate(flops=int(micros * 1.15e9), bytes_accessed=0, transcendentals=0)


def struct(shape, dtype):
    return jax.ShapeDtypeStruct(shape, dtype)


def run_pre(ids, xs, ws, gain, conv_w, conv_b, xw_t):
    micro, tokens, quarter = xs[0].shape
    width = gain.shape[1]
    chans = conv_w.shape[1]
    count = xw_t.shape[0]
    per = lambda *tail: pl.BlockSpec((1,) + tail, lambda m: (m,) + (0,) * len(tail))
    return pl.pallas_call(
        partial(pre_kernel, len(xs), len(ws)),
        grid=(micro,),
        in_specs=[SMEM]
        + [per(tokens, quarter)] * len(xs)
        + [whole(w.shape) for w in ws]
        + [whole(gain.shape), whole(conv_w.shape), whole(conv_b.shape), whole(xw_t.shape)],
        out_specs=[
            per(tokens, width),
            whole((width, ws[0].shape[1])),
            per(tokens, chans),
            per(tokens, chans),
            per(tokens, chans),
            per(tokens, chans),
            per(tokens, LANES),
            per(count, tokens),
            per(count, tokens),
        ],
        out_shape=[
            struct((micro, tokens, width), BF16),
            struct((width, ws[0].shape[1]), BF16),
            struct((micro, tokens, chans), F32),
            struct((micro, tokens, chans), F32),
            struct((micro, tokens, chans), F32),
            struct((micro, tokens, chans), F32),
            struct((micro, tokens, LANES), F32),
            struct((micro, count, tokens), F32),
            struct((micro, count, tokens), BF16),
        ],
        scratch_shapes=[pltpu.VMEM((tokens + GROUP, chans), F32)],
        compiler_params=params(1),
        cost_estimate=cost(7),
        name="pre",
    )(ids, *xs, *ws, gain, conv_w, conv_b, xw_t)


def run_fwd(ids, lens, projs, w_full, u_act, gate, dt_w, dt_b, a_log, skip):
    micro, tokens, chans = u_act.shape
    parts = len(projs)
    width = w_full.shape[0]
    quarter = width // parts
    count = projs[0].shape[1]
    nstate = a_log.shape[0]
    span = min(LANES, tokens)
    rows = lambda *tail: pl.BlockSpec((1, span) + tail, lambda m, b: (m, b) + (0,) * len(tail))
    return pl.pallas_call(
        partial(fwd_kernel, parts),
        grid=(micro, tokens // span),
        in_specs=[SMEM, SMEM]
        + [pl.BlockSpec((1, count, span), lambda m, b: (m, 0, b))] * parts
        + [pl.BlockSpec((width, chans), lambda m, b: (0, 2)), rows(chans), rows(chans)]
        + [whole(v.shape) for v in (dt_w, dt_b, a_log, skip)],
        out_specs=[
            rows(chans),
            rows(chans),
            rows(chans),
            pl.BlockSpec((1, 1, nstate, chans), lambda m, b: (m, b, 0, 0)),
            pl.BlockSpec((1, span * nstate, chans), lambda m, b: (m, b, 0)),
            pl.BlockSpec((1, span * nstate, 2 * LANES), lambda m, b: (m, b, 0)),
        ]
        + [rows(quarter)] * parts,
        out_shape=[
            struct((micro, tokens, chans), F32),
            struct((micro, tokens, chans), F32),
            struct((micro, tokens, chans), BF16),
            struct((micro, tokens // span, nstate, chans), F32),
            struct((micro, tokens * nstate, chans), BF16),
            struct((micro, tokens * nstate, 2 * LANES), F32),
            struct((micro, tokens, quarter), F32),
        ]
        + [struct((micro, tokens, quarter), BF16)] * (parts - 1),
        scratch_shapes=[pltpu.VMEM((span, chans), F32)] * 2
        + [pltpu.VMEM((chans // LANES, 2 * GROUP * GROUP, LANES), F32), pltpu.VMEM((nstate, chans), F32)],
        compiler_params=params(2),
        cost_estimate=cost(16),
        name="scan_forward",
    )(ids, lens, *projs, w_full, u_act, gate, dt_w, dt_b, a_log, skip)


def run_bwd(ids, lens, projs, cots, w_full, u_act, gate, dt, y_rows, edge, low_state, vectors, dt_w, a_log, skip):
    micro, tokens, chans = u_act.shape
    parts = len(projs)
    width = w_full.shape[0]
    quarter = cots[0].shape[2]
    count = projs[0].shape[1]
    nstate = a_log.shape[0]
    rank = dt_w.shape[0]
    span = min(LANES, tokens)
    blocks = tokens // span
    small = SCAN_STEP * -(-(rank + nstate + 2) // SCAN_STEP)
    rows = lambda *tail: pl.BlockSpec(
        (1, span) + tail, lambda m, b: (m, blocks - 1 - b) + (0,) * len(tail)
    )
    proj = pl.BlockSpec((1, count, span), lambda m, b: (m, 0, blocks - 1 - b))
    return pl.pallas_call(
        partial(bwd_kernel, parts),
        grid=(micro, blocks),
        in_specs=[SMEM, SMEM]
        + [proj] * parts
        + [rows(quarter)] * parts
        + [pl.BlockSpec((width, chans), lambda m, b: (0, 2)), rows(chans), rows(chans), rows(chans), rows(chans)]
        + [pl.BlockSpec((1, 1, nstate, chans), lambda m, b: (m, blocks - 1 - b, 0, 0))]
        + [pl.BlockSpec((1, span * nstate, chans), lambda m, b: (m, blocks - 1 - b, 0))]
        + [pl.BlockSpec((1, span * nstate, 2 * LANES), lambda m, b: (m, blocks - 1 - b, 0))]
        + [whole(v.shape) for v in (dt_w, a_log, skip)],
        out_specs=[rows(width), proj, proj, rows(chans), rows(chans), whole((small, chans)), whole((small, chans // 2))],
        out_shape=[
            struct((micro, tokens, width), BF16),
            struct((micro, count, tokens), F32),
            struct((micro, count, tokens), BF16),
            struct((micro, tokens, chans), F32),
            struct((micro, tokens, chans), BF16),
            struct((small, chans), F32),
            struct((small, chans // 2), F32),
        ],
        scratch_shapes=[pltpu.VMEM((span, chans), F32)] * 4
        + [pltpu.VMEM((chans // LANES, 2 * GROUP * GROUP, LANES), F32)] * 2
        + [pltpu.VMEM((nstate, chans), F32)] * 2
        + [pltpu.VMEM((span * nstate, chans), BF16)],
        compiler_params=params(2),
        cost_estimate=cost(21),
        name="scan_backward",
    )(ids, lens, *projs, *cots, w_full, u_act, gate, dt, y_rows, edge, low_state, vectors, dt_w, a_log, skip)


def run_post(ids, projs, xs, d_scan, d_gate, u_act, summed, inner, inv, w_full, gain, xw_t, conv_w):
    micro, tokens, chans = u_act.shape
    parts = len(projs)
    width = w_full.shape[0]
    quarter = width // parts
    count = projs[0].shape[1]
    taps = conv_w.shape[0]
    small = POST_STEP * -(-(count + taps + 1 + width // chans) // POST_STEP)
    lanes = max(width, LANES * -(-micro * tokens // LANES))
    per = lambda *tail: pl.BlockSpec((1,) + tail, lambda m: (m,) + (0,) * len(tail))
    return pl.pallas_call(
        partial(post_kernel, parts),
        grid=(micro,),
        in_specs=[SMEM]
        + [per(count, tokens)] * parts
        + [per(tokens, quarter)] * parts
        + [per(tokens, chans)] * 5
        + [per(tokens, LANES)]
        + [whole((width, 2 * chans))]
        + [whole(v.shape) for v in (gain, xw_t, conv_w)],
        out_specs=[
            per(tokens, chans),
            whole((small, chans)),
            whole((small, chans // 2)),
            whole((GROUP, lanes)),
        ]
        + [per(tokens, quarter)] * parts,
        out_shape=[
            struct((micro, tokens, chans), BF16),
            struct((small, chans), F32),
            struct((small, chans // 2), F32),
            struct((GROUP, lanes), F32),
            struct((micro, tokens, quarter), F32),
        ]
        + [struct((micro, tokens, quarter), BF16)] * (parts - 1),
        scratch_shapes=[pltpu.VMEM((tokens + GROUP, chans), F32)] * 2
        + [pltpu.VMEM((tokens, 2 * chans), BF16)],
        compiler_params=params(1),
        cost_estimate=cost(20),
        name="post",
    )(ids, *projs, *xs, d_scan, d_gate, u_act, summed, inner, inv, w_full, gain, xw_t, conv_w)


def run_grad(name, ids, lefts, rights, shape, chips):
    if chips == 0:
        outs = [struct(shape, F32), struct((GROUP, LANES), BF16)]
    else:
        outs = [struct((chips,) + shape, BF16)] * 2
    flat = lambda v: v.reshape(-1, v.shape[-1])
    return run_local(
        partial(grad_kernel, chips, len(lefts)), name, outs, ids, *map(flat, lefts), *map(flat, rights)
    )


VMEM = pl.BlockSpec(memory_space=pltpu.VMEM)


def run_local(kernel, name, outs, ids, *operands, scratch=()):
    return pl.pallas_call(
        kernel,
        grid=(1,),
        in_specs=([SMEM] if ids is not None else []) + [whole(v.shape) for v in operands],
        out_specs=[whole(v.shape) for v in outs],
        out_shape=outs,
        scratch_shapes=list(scratch),
        compiler_params=pltpu.CompilerParams(vmem_limit_bytes=64 * 1024 * 1024),
        cost_estimate=cost(0.3),
        name=name,
    )(*(() if ids is None else (ids,)), *operands)


def after(value, *earlier):
    return lax.optimization_barrier((value, earlier))[0]


def others(value, axis, step=1):
    count = lax.axis_size(axis)
    return [swap(value, axis, mask) for mask in range(step, count, step)]


def gather_line(value, axis, early=()):
    count = lax.axis_size(axis)
    got = {0: value}
    mask = count // 2
    while mask:
        for known in sorted(got):
            fresh = swap(got[known], axis, mask) if known or mask not in early else early[mask]
            got[known | mask] = fresh
        mask //= 2
    return [got[k] for k in range(count)]


def with_sibling(blocks):
    return blocks + [swap(block, "dp", 1) for block in blocks]


def sum_all(value):
    core = lax.rem(lax.axis_index("dp"), 2)
    half = value.shape[0] // 2
    halves = value.reshape((2, half) + value.shape[1:])
    mine = lax.dynamic_index_in_dim(halves, core, 0, keepdims=False)
    theirs = lax.dynamic_index_in_dim(halves, 1 - core, 0, keepdims=False)
    total = mine + swap(theirs, "dp", 1)
    for got in others(total, "dp", 2):
        total = total + got
    other = swap(total, "dp", 1)
    first = jnp.where(core == 0, total, other)
    second = jnp.where(core == 0, other, total)
    return jnp.concatenate([first, second], axis=0)


def body(
    tokens,
    lengths,
    norm_gain,
    in_weight,
    x_weight,
    dt_weight,
    dt_bias,
    conv_weight,
    conv_bias,
    a_log,
    skip,
    out_weight,
    cotangent,
):
    micro, seq, quarter = tokens.shape
    chans = in_weight.shape[2]
    width = norm_gain.shape[0]
    dps = lax.axis_size("dp")
    rank = dt_weight.shape[0]
    nstate = a_log.shape[0]
    taps = conv_weight.shape[0]
    count = x_weight.shape[1]
    ids = jnp.stack([lax.axis_index("tensor"), lax.axis_index("dp")]).astype(jnp.int32)
    lens = lengths[:, 0]
    gain = norm_gain[None]
    xw_t = x_weight.T
    in_rows = in_weight.reshape(in_weight.shape[0], 2 * chans)
    by_block = in_rows.shape[0] % LANES == 0
    chips = dps // 2 if by_block else 0
    parts = lax.axis_size("tensor")
    weight = jnp.concatenate([in_rows, out_weight.T], axis=1)

    xs = gather_line(tokens, "tensor")
    if by_block:
        mine = [weight] + [
            swap(weight, "dp", mask) for mask in range(2, dps, 2)
        ]
        blocks = with_sibling(after(mine, *xs))
    else:
        blocks = [lax.all_gather(weight, "dp", axis=0, tiled=True)]
    normed, w_full, inner, summed, u_act, gate, inv, proj, proj_low = run_pre(
        ids, xs, blocks, gain, conv_weight, conv_bias[None], xw_t
    )
    cot_early = after(cotangent, *xs)
    early = {mask: swap(cot_early, "tensor", mask) for mask in (parts // 2, 1)}
    projs = [proj] + others(proj_low, "tensor")
    far = after(early[parts // 2], *projs)
    early[parts // 2] = far
    cots = gather_line(cotangent, "tensor", early)
    dt, y_rows, gated, edge, low_state, vectors, own_out, *out_terms = run_fwd(
        ids, lens, projs, w_full, u_act, gate, dt_weight, dt_bias[None], a_log, skip[None]
    )
    out_got = [swap(term, "tensor", k + 1) for k, term in enumerate(out_terms)]
    cot_full, d_proj, d_proj_low, d_scan, d_gate, scan_small, scan_theirs = run_bwd(
        ids, lens, projs, cots, w_full, u_act, gate, dt, y_rows, edge, low_state, vectors, dt_weight, a_log, skip[None]
    )
    d_projs = [d_proj] + others(after(d_proj_low, *out_got), "tensor")
    branch = own_out
    for term in out_got:
        branch = branch + term.astype(F32)
    mixed = (tokens.astype(F32) + branch).astype(BF16)
    rows = weight.shape[0] if chips else width
    early_mine, early_theirs = run_grad(
        "grad_early",
        ids,
        [after(normed, d_projs[1]), cot_full],
        [d_gate, gated],
        (rows, 2 * chans),
        chips,
    )

    def merged(name, step, row, mine, theirs, small, small_theirs, tinies, wide):
        part = struct((small.shape[0], chans // 2), F32)
        own, part, *sends = run_local(
            partial(merge_kernel, step, row),
            name,
            [struct((rows, wide), F32), part] + [struct((rows + step, wide), BF16)] * (chips - 1),
            ids,
            mine,
            swap(theirs, "dp", 1),
            small,
            swap(small_theirs, "dp", 1),
            *tinies,
        )
        return own, part, sends

    if chips:
        early_own, early_part, sends = merged(
            "merge_early", SCAN_STEP, 0, early_mine, early_theirs, scan_small, scan_theirs, (), 2 * chans
        )
        early_gots = [swap(send, "dp", 2 * (j + 1)) for j, send in enumerate(sends)]
    d_inner, small, small_theirs, tiny, own_norm, *norm_terms = run_post(
        ids, d_projs, xs, d_scan, d_gate, u_act, summed, inner, inv, w_full, gain, xw_t, conv_weight
    )
    tiny_got = others(after(tiny, sends) if chips else tiny, "tensor")
    near = parts // 2
    halves = [own_norm] + norm_terms
    passed = [swap(halves[k], "tensor", k) for k in range(1, near)]
    relayed = [swap(halves[near + k], "tensor", k) for k in range(1, near)]
    far = halves[near].astype(F32)
    for got in relayed:
        far = far + got.astype(F32)
    far = far.astype(BF16)
    norm_got = passed + [swap(far, "tensor", near)]
    late_mine, late_theirs = run_grad("grad_late", ids, [normed], [d_inner], (rows, chans), chips)
    for got in tiny_got:
        tiny = tiny + got
    row = count + taps + 1
    if chips:
        late_own, late_part, sends = merged(
            "merge_late",
            POST_STEP,
            row,
            after(late_mine, far),
            late_theirs,
            small,
            small_theirs,
            (tiny, swap(tiny, "dp", 1)),
            chans,
        )
        late_gots = [swap(send, "dp", 2 * (j + 1)) for j, send in enumerate(sends)]
        grad_gate, grad_out, scan_half = run_local(
            partial(final_early_kernel, SCAN_STEP),
            "final_early",
            [struct((rows, chans), F32), struct(out_weight.shape, F32), struct(early_part.shape, F32)],
            None,
            early_own,
            early_part,
            *early_gots,
        )
        grad_in, post_half = run_local(
            partial(final_late_kernel, POST_STEP),
            "final_late",
            [struct(in_weight.shape, F32), struct(late_part.shape, F32)],
            None,
            late_own,
            late_part,
            grad_gate,
            *late_gots,
        )
        g_gain, g_x, g_dt, g_dtb, g_conv, g_convb, g_alog, g_skip = run_local(
            outputs_kernel,
            "outputs",
            [
                struct((1, width), F32),
                struct((count, chans), F32),
                struct((rank, chans), F32),
                struct((1, chans), F32),
                struct((taps, chans), F32),
                struct((1, chans), F32),
                struct((nstate, chans), F32),
                struct((1, chans), F32),
            ],
            ids,
            scan_half,
            swap(scan_half, "dp", 1),
            post_half,
            swap(post_half, "dp", 1),
            scratch=[pltpu.VMEM((scan_small.shape[0], chans), F32), pltpu.VMEM((small.shape[0], chans), F32)],
        )
        smalls = (g_gain[0], g_x.T, g_dt, g_dtb[0], g_conv, g_convb[0], g_alog, g_skip[0])
    else:
        grad_inner = lax.psum_scatter(late_mine, "dp", scatter_dimension=0, tiled=True)
        early = lax.psum_scatter(early_mine, "dp", scatter_dimension=0, tiled=True)
        grad_in = jnp.stack([grad_inner, early[:, :chans]], axis=1)
        grad_out = early[:, chans:].T
        scan_small = sum_all(scan_small)
        small = sum_all(lax.dynamic_update_slice_in_dim(small, tiny[0, :width].reshape(-1, chans), row, 0))
        smalls = (
            small[row : row + width // chans].reshape(width),
            small[:count].T,
            scan_small[:rank],
            scan_small[rank + nstate],
            small[count : count + taps],
            small[count + taps],
            scan_small[rank : rank + nstate],
            scan_small[rank + nstate + 1],
        )
    d_norm = own_norm
    for term in norm_got:
        d_norm = d_norm + term.astype(F32)
    scale = inv[:, :, :1]
    dots = tiny[1, : micro * seq].reshape(micro, seq, 1)
    own_gain = lax.dynamic_slice_in_dim(norm_gain, ids[0] * quarter, quarter, 0)
    d_x = scale * (d_norm * own_gain) - tokens.astype(F32) * (scale * scale * scale * dots / width)
    input_grad = cotangent.astype(F32) + d_x
    return (mixed, input_grad, smalls[0], grad_in.reshape(in_weight.shape)) + smalls[1:] + (grad_out,)


def solution(mesh):
    rows = P(None, "dp", "tensor")
    chans = P(None, "tensor")
    return jax.shard_map(
        body,
        mesh=mesh,
        in_specs=(
            rows,
            P(None, "dp"),
            P(),
            P("dp", None, "tensor"),
            P("tensor", None),
            chans,
            P("tensor"),
            chans,
            P("tensor"),
            chans,
            P("tensor"),
            P("tensor", "dp"),
            rows,
        ),
        out_specs=(
            rows,
            rows,
            P(),
            P("dp", None, "tensor"),
            P("tensor", None),
            chans,
            P("tensor"),
            chans,
            P("tensor"),
            chans,
            P("tensor"),
            P("tensor", "dp"),
        ),
        check_vma=False,
    )
```
